32 devices in a mesh: batch: 4 (over y, x), ctx: 8 (over z, core).
Axes of the slice: x: 2, y: 2, z: 4, core: 2. Of those that a mesh axis runs over, the one named last changes fastest.
Arguments:
- tokens: bfloat16 [4, 1536, 960], P('batch', 'ctx'), may hold values from -6 to 6
- attention_weights: bfloat16 [2457600], P(('batch', 'ctx')), may hold values from -2 to 2
- feedforward_weights: bfloat16 [7372800], P(('batch', 'ctx')), may hold values from -1 to 1
- norm_gains: float32 [2, 960], P(None, 'ctx'), may hold values from 0.5 to 1.5
- span_order: int32 [4, 16], P('batch', 'ctx'), may hold values from 0 to 15, as said below
- cotangent: bfloat16 [4, 1536, 960], P('batch', 'ctx'), may hold values from -6 to 6
Outputs:
- out_tokens: bfloat16 [4, 1536, 960], P('batch', 'ctx')
- grad_tokens: float32 [4, 1536, 960], P('batch', 'ctx')
- grad_attention: float32 [2457600], P(('batch', 'ctx'))
- grad_feedforward: float32 [7372800], P(('batch', 'ctx'))
- grad_norm_gains: float32 [2, 960], P(None, 'ctx')
The draws below stay inside these ranges and needn't reach their ends.
Inputs may be any that keep to these rules, and one draw needn't show every extreme that they name: `span_order`: each row is a permutation of 0 to 15 in which entries 2c and 2c + 1 sum to 15.
All inputs are finite; a program needn't handle non-finite values.
Results may differ from the reference program's by a relative error of at most 0.025.
Values may be sent and summed in bfloat16 or wider, within the bound.
No kernel may reach another device: no remote copies, remote signals or barrier semaphores. Data moves between devices by JAX's collectives and lax.ppermute only.
A program may use at most 192 MiB of HBM per device.

```python
import math
import jax
import jax.numpy as jnp
from jax import lax

D = 960
HEADS = 15
KV_HEADS = 5
HEAD_DIM = 64
FF = 2560
TOK_DEV = 192
SEQS = 4
LEN = 1536
SPANS = 16
QW = 960
KVW = 320
GROUP = 3
ATT = 2457600
MLP = 7372800


def draw_attention_weights(key, part):
    key = jax.random.fold_in(key, 11)
    index = jnp.arange(ATT)
    second = D * QW + D * KVW
    third = second + D * KVW
    scales = jnp.where(index < second, 1.5 / D ** 0.5, jnp.where(index < third, 1.0 / D ** 0.5, 3.0 / QW ** 0.5))
    unit_draw = jax.random.truncated_normal(key, -3.0, 3.0, (ATT,), jnp.float32)
    return (unit_draw * scales).astype(jnp.bfloat16)


def draw_feedforward_weights(key, part):
    key = jax.random.fold_in(key, 23)
    index = jnp.arange(MLP)
    scales = jnp.where(index < 2 * D * FF, 1.0 / D ** 0.5, 2.0 / FF ** 0.5)
    unit_draw = jax.random.truncated_normal(key, -3.0, 3.0, (MLP,), jnp.float32)
    return (unit_draw * scales).astype(jnp.bfloat16)


def draw_span_order(key, part):
    key = jax.random.fold_in(key, 37)
    row_keys = jax.random.split(key, SEQS)
    lower = jax.vmap(lambda row_key: jax.random.permutation(row_key, SPANS // 2))(row_keys)
    paired = jnp.stack([lower, SPANS - 1 - lower], axis=-1)
    return paired.reshape(SEQS, SPANS).astype(jnp.int32)


def block_scale(own_key, dims, cuts, smallest, top_value):
    level, own = 1.0, jax.random.fold_in(own_key, 6)
    for position, blocks in cuts:
        draws = jnp.exp(jax.random.uniform(jax.random.fold_in(own, position), (blocks,), jnp.float32, smallest / len(cuts), top_value / len(cuts)))
        level = level * jnp.repeat(draws, dims[position] // blocks).reshape([-1 if axis == position else 1 for axis in range(len(dims))])
    return level


def bell_draw(stream_key, shape, width, most, shards=(), kind=jnp.bfloat16):
    loudness = block_scale(stream_key, shape, shards, -0.22, 0.18) if shards else 1.0
    values = jax.random.normal(stream_key, shape, jnp.float32) * width * loudness
    return jnp.minimum(jnp.maximum(values, -most), most).astype(kind)


def setup_inputs(seed: int = 0) -> dict:
    key_list = jax.random.split(jax.random.key(seed), 7)
    tokens = bell_draw(key_list[0], (SEQS, LEN, D), 1.0, 6.0, ((0, 4), (1, 8)))
    attention_weights = draw_attention_weights(jax.random.fold_in(key_list[6], 71), 0)
    feedforward_weights = draw_feedforward_weights(jax.random.fold_in(key_list[6], 71), 0)
    norm_gains = jnp.clip(1.0 + 0.1 * jax.random.normal(key_list[3], (2, D), jnp.float32), 0.5, 1.5)
    span_order = draw_span_order(jax.random.fold_in(key_list[6], 71), 0)
    cotangent = bell_draw(key_list[5], (SEQS, LEN, D), 1.0, 6.0, ((0, 4), (1, 8)))
    return dict(tokens=tokens, attention_weights=attention_weights, feedforward_weights=feedforward_weights, norm_gains=norm_gains, span_order=span_order, cotangent=cotangent)


@jax.custom_vjp
def low(v):
    return lax.optimization_barrier(v.astype(jnp.bfloat16)).astype(jnp.float32)

@jax.custom_vjp
def low_back(v):
    return v

def low_keep(v):
    return (low(v), None)

def low_pass(kept, grad):
    return (grad,)

def back_keep(v):
    return (v, None)

def back_low(kept, grad):
    return (low(grad),)
low.defvjp(low_keep, low_pass)
low_back.defvjp(back_keep, back_low)
ROPE_BASE = 100000.0
EPS = 1e-05
NEG = -1e+30

def matmul(left, right):
    return jnp.dot(left, right, precision=lax.Precision.HIGHEST)

def normalize(values, gain):
    return values * lax.rsqrt(lax.optimization_barrier(jnp.mean(values * values, -1, keepdims=True)) + EPS) * gain

def rope_tables(positions):
    halves = HEAD_DIM // 2
    inverse_freq = ROPE_BASE ** (-jnp.arange(halves, dtype=jnp.float32) / halves)
    angles = positions.astype(jnp.float32)[:, None] * inverse_freq[None, :]
    return (jnp.cos(angles), jnp.sin(angles))

def rotate(values, cos_table, sin_table):
    halves = HEAD_DIM // 2
    first = values[..., :halves]
    second = values[..., halves:]
    cos_table = cos_table[:, None, :]
    sin_table = sin_table[:, None, :]
    return jnp.concatenate([first * cos_table - second * sin_table, second * cos_table + first * sin_table], -1)

def split_flat(flat, shapes):
    pieces = []
    offset = 0
    for rows_in, cols_in in shapes:
        pieces.append(flat[offset:offset + rows_in * cols_in].reshape(rows_in, cols_in))
        offset += rows_in * cols_in
    return pieces

def layer(inputs, attention, feedforward, gains, positions):
    w_query, w_key, w_value, w_out = split_flat(attention, [(D, QW), (D, KVW), (D, KVW), (QW, D)])
    w_gate, w_up, w_down = split_flat(feedforward, [(D, FF), (D, FF), (FF, D)])
    hidden = low(normalize(inputs, gains[0]))
    cos_table, sin_table = rope_tables(positions)
    query_raw = low_back(matmul(hidden, w_query)).reshape(LEN, HEADS, HEAD_DIM)
    key_raw = low_back(matmul(hidden, w_key)).reshape(LEN, KV_HEADS, HEAD_DIM)
    values = low(low_back(matmul(hidden, w_value))).reshape(LEN, KV_HEADS, HEAD_DIM)
    queries = low(rotate(query_raw, cos_table, sin_table)).reshape(LEN, KV_HEADS, GROUP, HEAD_DIM)
    keys = low(rotate(key_raw, cos_table, sin_table))
    block = math.gcd(LEN, 512)
    query_blocks = queries.reshape(LEN // block, block, KV_HEADS, GROUP, HEAD_DIM)
    pos_blocks = positions.reshape(LEN // block, block)

    def attend(item):
        query_block, query_pos = item
        scores = jnp.einsum('qhgd,khd->hgqk', query_block, keys, precision=lax.Precision.HIGHEST) * HEAD_DIM ** (-0.5)
        scores = low_back(scores)
        visible = positions[None, None, None, :] <= query_pos[None, None, :, None]
        scores = jnp.where(visible, scores, NEG)
        probs = low(jax.nn.softmax(scores, axis=-1))
        return jnp.einsum('hgqk,khd->qhgd', probs, values, precision=lax.Precision.HIGHEST)
    attended = lax.map(jax.checkpoint(attend), (query_blocks, pos_blocks)).reshape(LEN, QW)
    attended = low(low_back(attended))
    middle = inputs + low_back(matmul(attended, w_out))
    hidden_two = low(normalize(middle, gains[1]))
    gate = low_back(matmul(hidden_two, w_gate))
    upward = low_back(matmul(hidden_two, w_up))
    activ = low(jax.nn.silu(gate) * upward)
    return middle + low_back(matmul(activ, w_down))

def reference(tokens, attention_weights, feedforward_weights, norm_gains, span_order, cotangent):
    attention = attention_weights.astype(jnp.float32)
    feedforward = feedforward_weights.astype(jnp.float32)
    gains = norm_gains.astype(jnp.float32)
    halves = TOK_DEV // 2
    offsets = jnp.arange(halves, dtype=jnp.int32)

    def one_sequence(carry, item):
        inputs, grad_out, order = item
        positions = (order.astype(jnp.int32)[:, None] * halves + offsets[None, :]).reshape(LEN)
        result, pull = jax.vjp(lambda a, b, c, d: layer(a, b, c, d, positions), inputs.astype(jnp.float32), attention, feedforward, gains)
        grad_in, grad_att, grad_ff, grad_gain = pull(grad_out.astype(jnp.float32))
        carry = (carry[0] + grad_att, carry[1] + grad_ff, carry[2] + grad_gain)
        return (carry, (result.astype(jnp.bfloat16), grad_in))
    start = (jnp.zeros((ATT,), jnp.float32), jnp.zeros((MLP,), jnp.float32), jnp.zeros((2, D), jnp.float32))
    totals, outputs = lax.scan(one_sequence, start, (tokens, cotangent, span_order))
    return (outputs[0], outputs[1], totals[0], totals[1], totals[2])
```

```python
import math

import jax
import jax.numpy as jnp
from jax import lax
from jax.experimental import pallas as pl
from jax.experimental.pallas import tpu as pltpu
from jax.sharding import PartitionSpec as P

D = 960
HEADS = 15
KV_HEADS = 5
HEAD_DIM = 64
FF = 2560


ROPE_BASE = 100000.0
EPS = 1e-05
NEG = -1e30


def normalize(values, gain):
    return values * lax.rsqrt(jnp.mean(values * values, -1, keepdims=True) + EPS) * gain


def swiglu(gate, upward):
    return jax.nn.silu(gate) * upward


def rope_tables(positions):
    halves = HEAD_DIM // 2
    inverse_freq = ROPE_BASE ** (-jnp.arange(halves, dtype=jnp.float32) / halves)
    angles = positions.astype(jnp.float32)[:, None] * inverse_freq[None, :]
    return (jnp.cos(angles), jnp.sin(angles))


def rotate(values, cos_table, sin_table):
    halves = HEAD_DIM // 2
    first = values[..., :halves]
    second = values[..., halves:]
    cos_table = cos_table[:, None, :]
    sin_table = sin_table[:, None, :]
    return jnp.concatenate(
        [first * cos_table - second * sin_table, second * cos_table + first * sin_table], -1
    )


def split_flat(flat, shapes):
    pieces = []
    offset = 0
    for rows_in, cols_in in shapes:
        pieces.append(flat[offset : offset + rows_in * cols_in].reshape(rows_in, cols_in))
        offset += rows_in * cols_in
    return pieces


def unpack(att_flat, ff_flat):
    width_q = HEADS * HEAD_DIM
    width_kv = KV_HEADS * HEAD_DIM
    att_parts = split_flat(att_flat, [(D, width_q), (D, width_kv), (D, width_kv), (width_q, D)])
    ff_parts = split_flat(ff_flat, [(D, FF), (D, FF), (FF, D)])
    return (att_parts, ff_parts)


def score_block(queries, key_block, query_pos, key_pos):
    keys_three = key_block.reshape(key_block.shape[0], KV_HEADS, HEAD_DIM)
    scores = jnp.einsum(
        "qhgd,khd->hgqk", queries, keys_three, preferred_element_type=jnp.float32
    ) * HEAD_DIM ** (-0.5)
    visible = key_pos[None, None, None, :] <= query_pos[None, None, :, None]
    return (scores, visible)


def attention_forward(queries, key_all, value_all, query_pos, key_pos, block):
    rows_here = queries.shape[0]
    group = HEADS // KV_HEADS
    count = key_all.shape[0] // block
    key_blocks = key_all.reshape(count, block, key_all.shape[1])
    value_blocks = value_all.reshape(count, block, value_all.shape[1])
    pos_blocks = key_pos.reshape(count, block)

    def online_step(carry, item):
        top, total, accum = carry
        key_block, value_block, pos_block = item
        scores, visible = score_block(queries, key_block, query_pos, pos_block)
        scores = jnp.where(visible, scores, NEG)
        new_top = jnp.maximum(top, jnp.max(scores, -1))
        weights = jnp.where(visible, jnp.exp(scores - new_top[..., None]), 0.0)
        factor = jnp.exp(top - new_top)
        total = total * factor + jnp.sum(weights, -1)
        values_three = value_block.reshape(block, KV_HEADS, HEAD_DIM)
        accum = accum * jnp.transpose(factor, (2, 0, 1))[..., None]
        accum = accum + jnp.einsum(
            "hgqk,khd->qhgd",
            weights.astype(jnp.bfloat16),
            values_three,
            preferred_element_type=jnp.float32,
        )
        return ((new_top, total, accum), None)

    start_top = jnp.full((KV_HEADS, group, rows_here), NEG, jnp.float32)
    start_total = jnp.zeros((KV_HEADS, group, rows_here), jnp.float32)
    start_out = jnp.zeros((rows_here, KV_HEADS, group, HEAD_DIM), jnp.float32)
    (top, total, accum), unused = lax.scan(
        online_step, (start_top, start_total, start_out), (key_blocks, value_blocks, pos_blocks)
    )
    log_total = top + jnp.log(total)
    attended = accum / jnp.transpose(total, (2, 0, 1))[..., None]
    return (attended, log_total)


def attention_backward(
    queries, key_all, value_all, query_pos, key_pos, block, log_total, grad_out, attended
):
    rows_here = queries.shape[0]
    group = HEADS // KV_HEADS
    width_kv = key_all.shape[1]
    count = key_all.shape[0] // block
    items = (
        key_all.reshape(count, block, width_kv),
        value_all.reshape(count, block, width_kv),
        key_pos.reshape(count, block),
    )
    delta = jnp.transpose(jnp.sum(grad_out.astype(jnp.float32) * attended, -1), (1, 2, 0))

    def grad_step(grad_query, item):
        key_block, value_block, pos_block = item
        scores, visible = score_block(queries, key_block, query_pos, pos_block)
        probs = jnp.where(visible, jnp.exp(scores - log_total[..., None]), 0.0)
        values_three = value_block.reshape(block, KV_HEADS, HEAD_DIM)
        grad_probs = jnp.einsum(
            "qhgd,khd->hgqk", grad_out, values_three, preferred_element_type=jnp.float32
        )
        grad_scores = (probs * (grad_probs - delta[..., None])).astype(jnp.bfloat16)
        keys_three = key_block.reshape(block, KV_HEADS, HEAD_DIM)
        grad_query = grad_query + jnp.einsum(
            "hgqk,khd->qhgd", grad_scores, keys_three, preferred_element_type=jnp.float32
        )
        grad_key = jnp.einsum(
            "hgqk,qhgd->khd", grad_scores, queries, preferred_element_type=jnp.float32
        )
        grad_value = jnp.einsum(
            "hgqk,qhgd->khd",
            probs.astype(jnp.bfloat16),
            grad_out,
            preferred_element_type=jnp.float32,
        )
        return (
            grad_query,
            (grad_key.reshape(block, width_kv), grad_value.reshape(block, width_kv)),
        )

    start_query = jnp.zeros((rows_here, KV_HEADS, group, HEAD_DIM), jnp.float32)
    grad_query, (grad_keys, grad_values) = lax.scan(grad_step, start_query, items)
    return (
        grad_query,
        grad_keys.reshape(count * block, width_kv),
        grad_values.reshape(count * block, width_kv),
    )


def local_any(tokens, attention_weights, feedforward_weights, norm_gains, span_order, cotangent):
    ctx_count = lax.axis_size("ctx")
    batch_count = lax.axis_size("batch")
    rows_here = tokens.shape[1]
    halves = rows_here // 2
    length = rows_here * ctx_count
    group = HEADS // KV_HEADS
    width_q = HEADS * HEAD_DIM
    width_kv = KV_HEADS * HEAD_DIM
    block = math.gcd(length, 512)
    scaling = HEAD_DIM ** (-0.5)
    att_full, ff_full = (
        lax.all_gather(attention_weights, ("batch", "ctx"), axis=0, tiled=True),
        lax.all_gather(feedforward_weights, ("batch", "ctx"), axis=0, tiled=True),
    )
    gain_full = lax.all_gather(norm_gains, "ctx", axis=1, tiled=True)
    order_full = lax.all_gather(span_order, "ctx", axis=1, tiled=True)
    offsets = jnp.arange(halves, dtype=jnp.int32)
    key_pos = (order_full[0][:, None] * halves + offsets[None, :]).reshape(length)
    query_pos = (span_order[0][:, None] * halves + offsets[None, :]).reshape(rows_here)
    cos_table, sin_table = rope_tables(query_pos)
    (w_query, w_key, w_value, w_out), (w_gate, w_up, w_down) = unpack(att_full, ff_full)
    inputs = tokens[0].astype(jnp.float32)
    hidden_f, norm_one_pull = jax.vjp(normalize, inputs, gain_full[0])
    hidden = hidden_f.astype(jnp.bfloat16)
    query_raw = jnp.dot(hidden, w_query, preferred_element_type=jnp.float32).reshape(
        rows_here, HEADS, HEAD_DIM
    )
    key_raw = jnp.dot(hidden, w_key, preferred_element_type=jnp.float32).reshape(
        rows_here, KV_HEADS, HEAD_DIM
    )
    values = jnp.dot(hidden, w_value, preferred_element_type=jnp.float32).astype(jnp.bfloat16)
    query_rot, query_pull = jax.vjp(lambda a: rotate(a, cos_table, sin_table), query_raw)
    key_rot, key_pull = jax.vjp(lambda a: rotate(a, cos_table, sin_table), key_raw)
    queries = query_rot.astype(jnp.bfloat16).reshape(rows_here, KV_HEADS, group, HEAD_DIM)
    keys = key_rot.astype(jnp.bfloat16).reshape(rows_here, width_kv)
    key_all, value_all = (
        lax.all_gather(keys, "ctx", axis=0, tiled=True),
        lax.all_gather(values, "ctx", axis=0, tiled=True),
    )
    attended, log_total = attention_forward(queries, key_all, value_all, query_pos, key_pos, block)
    attended_low = attended.reshape(rows_here, width_q).astype(jnp.bfloat16)
    middle = inputs + jnp.dot(attended_low, w_out, preferred_element_type=jnp.float32)
    hidden_two_f, norm_two_pull = jax.vjp(normalize, middle, gain_full[1])
    hidden_two = hidden_two_f.astype(jnp.bfloat16)
    gate = jnp.dot(hidden_two, w_gate, preferred_element_type=jnp.float32)
    upward = jnp.dot(hidden_two, w_up, preferred_element_type=jnp.float32)
    activ_f, swiglu_pull = jax.vjp(swiglu, gate, upward)
    activ = activ_f.astype(jnp.bfloat16)
    result = middle + jnp.dot(activ, w_down, preferred_element_type=jnp.float32)
    grad_result = cotangent[0]
    grad_down = jnp.einsum("tf,td->fd", activ, grad_result, preferred_element_type=jnp.float32)
    grad_activ = jnp.einsum("td,fd->tf", grad_result, w_down, preferred_element_type=jnp.float32)
    grad_gate_f, grad_up_f = swiglu_pull(grad_activ)
    grad_gate = grad_gate_f.astype(jnp.bfloat16)
    grad_upward = grad_up_f.astype(jnp.bfloat16)
    grad_w_gate = jnp.einsum("td,tf->df", hidden_two, grad_gate, preferred_element_type=jnp.float32)
    grad_w_up = jnp.einsum("td,tf->df", hidden_two, grad_upward, preferred_element_type=jnp.float32)
    grad_hidden_two = jnp.einsum("tf,df->td", grad_gate, w_gate, preferred_element_type=jnp.float32)
    grad_hidden_two = grad_hidden_two + jnp.einsum(
        "tf,df->td", grad_upward, w_up, preferred_element_type=jnp.float32
    )
    grad_middle_norm, grad_gain_two = norm_two_pull(grad_hidden_two)
    grad_middle = grad_result.astype(jnp.float32) + grad_middle_norm
    grad_branch = grad_middle.astype(jnp.bfloat16)
    grad_w_out = jnp.einsum(
        "tq,td->qd", attended_low, grad_branch, preferred_element_type=jnp.float32
    )
    grad_attended = jnp.einsum(
        "td,qd->tq", grad_branch, w_out, preferred_element_type=jnp.float32
    ).astype(jnp.bfloat16)
    grad_attended = grad_attended.reshape(rows_here, KV_HEADS, group, HEAD_DIM)
    grad_query_rot, grad_key_all, grad_value_all = attention_backward(
        queries, key_all, value_all, query_pos, key_pos, block, log_total, grad_attended, attended
    )
    grad_key_rot, grad_value_f = (
        lax.psum_scatter(
            grad_key_all.astype(jnp.bfloat16), "ctx", scatter_dimension=0, tiled=True
        ).astype(jnp.float32),
        lax.psum_scatter(
            grad_value_all.astype(jnp.bfloat16), "ctx", scatter_dimension=0, tiled=True
        ).astype(jnp.float32),
    )
    grad_query_raw = query_pull(grad_query_rot.reshape(rows_here, HEADS, HEAD_DIM) * scaling)[0]
    grad_key_raw = key_pull(grad_key_rot.reshape(rows_here, KV_HEADS, HEAD_DIM) * scaling)[0]
    grad_query = grad_query_raw.reshape(rows_here, width_q).astype(jnp.bfloat16)
    grad_key = grad_key_raw.reshape(rows_here, width_kv).astype(jnp.bfloat16)
    grad_value = grad_value_f.astype(jnp.bfloat16)
    grad_w_query = jnp.einsum("td,tq->dq", hidden, grad_query, preferred_element_type=jnp.float32)
    grad_w_key = jnp.einsum("td,tq->dq", hidden, grad_key, preferred_element_type=jnp.float32)
    grad_w_value = jnp.einsum("td,tq->dq", hidden, grad_value, preferred_element_type=jnp.float32)
    grad_hidden = jnp.einsum("tq,dq->td", grad_query, w_query, preferred_element_type=jnp.float32)
    grad_hidden = grad_hidden + jnp.einsum(
        "tq,dq->td", grad_key, w_key, preferred_element_type=jnp.float32
    )
    grad_hidden = grad_hidden + jnp.einsum(
        "tq,dq->td", grad_value, w_value, preferred_element_type=jnp.float32
    )
    grad_inputs_norm, grad_gain_one = norm_one_pull(grad_hidden)
    grad_inputs = grad_middle + grad_inputs_norm
    grad_att_flat = jnp.concatenate(
        [
            grad_w_query.reshape(-1),
            grad_w_key.reshape(-1),
            grad_w_value.reshape(-1),
            grad_w_out.reshape(-1),
        ]
    )
    grad_ff_flat = jnp.concatenate(
        [grad_w_gate.reshape(-1), grad_w_up.reshape(-1), grad_down.reshape(-1)]
    )
    width_own = D // ctx_count
    gain_terms = jnp.stack([grad_gain_one, grad_gain_two]).reshape(2, ctx_count, width_own)
    gain_terms = jnp.transpose(gain_terms, (1, 0, 2)).reshape(ctx_count, 2 * width_own)
    gain_terms = jnp.broadcast_to(
        gain_terms[None], (batch_count, ctx_count, 2 * width_own)
    ).reshape(batch_count * ctx_count, 2 * width_own)
    att_part, ff_part, gain_part = (
        lax.psum_scatter(
            grad_att_flat.astype(jnp.bfloat16), "batch", scatter_dimension=0, tiled=True
        ).astype(jnp.float32),
        lax.psum_scatter(
            grad_ff_flat.astype(jnp.bfloat16), "batch", scatter_dimension=0, tiled=True
        ).astype(jnp.float32),
        lax.psum_scatter(
            gain_terms.astype(jnp.bfloat16), "batch", scatter_dimension=0, tiled=True
        ).astype(jnp.float32),
    )
    grad_att_own, grad_ff_own, gain_own = (
        lax.psum_scatter(
            att_part.astype(jnp.bfloat16), "ctx", scatter_dimension=0, tiled=True
        ).astype(jnp.float32),
        lax.psum_scatter(
            ff_part.astype(jnp.bfloat16), "ctx", scatter_dimension=0, tiled=True
        ).astype(jnp.float32),
        lax.psum_scatter(
            gain_part.astype(jnp.bfloat16), "ctx", scatter_dimension=0, tiled=True
        ).astype(jnp.float32),
    )
    grad_gain_own = gain_own.reshape(2, width_own)
    return (
        result.astype(jnp.bfloat16)[None],
        grad_inputs[None],
        grad_att_own,
        grad_ff_own,
        grad_gain_own,
    )


CHUNK = 4


def sort_rows(spans_ref, own_ref, other_ref, sorted_ref, span):
    for m, ref in enumerate((own_ref, other_ref)):
        for z in range(4):
            for j in range(2):
                start = pl.multiple_of(spans_ref[m, z, j] * span, span)
                sorted_ref[pl.ds(start, span), :] = ref[z, j * span : (j + 1) * span, :]


def group_rows(ref, part, span, head):
    group = HEADS // KV_HEADS
    rows = ref[part * span : (part + 1) * span, :]
    columns = [
        rows[:, (head * group + j) * HEAD_DIM : (head * group + j + 1) * HEAD_DIM]
        for j in range(group)
    ]
    return jnp.concatenate(columns, 0)


def seen(position, step, span, rows, cols):
    row = lax.broadcasted_iota(jnp.int32, (rows, cols), 0) % span
    col = lax.broadcasted_iota(jnp.int32, (rows, cols), 1)
    return col + step * cols <= row + position * span


def attend_kernel(
    spans_ref, q_ref, own_ref, other_ref, out_ref, lse_ref, sorted_ref, q_scr, top_ref, sum_ref, acc_ref
):
    group = HEADS // KV_HEADS
    span = q_ref.shape[0] // 2
    width_kv = KV_HEADS * HEAD_DIM
    rows, cols = group * span, CHUNK * span
    sort_rows(spans_ref, own_ref, other_ref, sorted_ref, span)
    for part in range(2):
        position = spans_ref[0, 4, part]
        for g in range(KV_HEADS):
            q_scr[g] = group_rows(q_ref, part, span, g) * jnp.bfloat16(HEAD_DIM**-0.5)
        top_ref[...] = jnp.full(top_ref.shape, NEG, jnp.float32)
        sum_ref[...] = jnp.zeros(sum_ref.shape, jnp.float32)
        acc_ref[...] = jnp.zeros(acc_ref.shape, jnp.float32)

        def step(i, unused):
            visible = seen(position, i, span, rows, cols)
            base = pl.multiple_of(i * cols, cols)
            for g in range(KV_HEADS):
                k = sorted_ref[pl.ds(base, cols), g * HEAD_DIM : (g + 1) * HEAD_DIM]
                v = sorted_ref[
                    pl.ds(base, cols), width_kv + g * HEAD_DIM : width_kv + (g + 1) * HEAD_DIM
                ]
                s = lax.dot_general(
                    q_scr[g], k, (((1,), (1,)), ((), ())), preferred_element_type=jnp.float32
                )
                s = jnp.where(visible, s, NEG)
                old = top_ref[g]
                top = jnp.maximum(old, jnp.max(s, 1, keepdims=True))
                weights = jnp.where(visible, jnp.exp(s - top), 0.0)
                factor = jnp.exp(old - top)
                top_ref[g] = top
                sum_ref[g] = sum_ref[g] * factor + jnp.sum(weights, 1, keepdims=True)
                acc_ref[g] = acc_ref[g] * factor + jnp.dot(
                    weights.astype(jnp.bfloat16), v, preferred_element_type=jnp.float32
                )
            return 0

        lax.fori_loop(0, (position + CHUNK) // CHUNK, step, 0)
        for g in range(KV_HEADS):
            out = acc_ref[g] / sum_ref[g]
            lse_ref[part * KV_HEADS + g] = top_ref[g] + jnp.log(sum_ref[g])
            for j in range(group):
                h = g * group + j
                out_ref[part * span : (part + 1) * span, h * HEAD_DIM : (h + 1) * HEAD_DIM] = out[
                    j * span : (j + 1) * span
                ]


def attend(spans, queries, own, other):
    rows, width = queries.shape
    group = HEADS // KV_HEADS
    stacked = group * rows // 2
    vmem = pl.BlockSpec(memory_space=pltpu.VMEM)
    return pl.pallas_call(
        attend_kernel,
        out_shape=(
            jax.ShapeDtypeStruct((rows, width), jnp.float32),
            jax.ShapeDtypeStruct((2 * KV_HEADS, stacked, 1), jnp.float32),
        ),
        in_specs=[pl.BlockSpec(memory_space=pltpu.SMEM), vmem, vmem, vmem],
        out_specs=(vmem, vmem),
        scratch_shapes=[
            pltpu.VMEM((8 * rows, own.shape[2]), jnp.bfloat16),
            pltpu.VMEM((KV_HEADS, stacked, HEAD_DIM), jnp.bfloat16),
            pltpu.VMEM((KV_HEADS, stacked, 1), jnp.float32),
            pltpu.VMEM((KV_HEADS, stacked, 1), jnp.float32),
            pltpu.VMEM((KV_HEADS, stacked, HEAD_DIM), jnp.float32),
        ],
        compiler_params=pltpu.CompilerParams(vmem_limit_bytes=24 * 2**20),
        name="attend",
    )(spans, queries, own, other)


def attend_back_kernel(
    spans_ref, q_ref, own_ref, other_ref, out_ref, lse_ref, grad_ref,
    dq_ref, own_grad_ref, other_grad_ref,
    sorted_ref, q_scr, grad_scr, delta_ref, dq_scr, dk_scr, dv_scr,
):
    group = HEADS // KV_HEADS
    span = q_ref.shape[0] // 2
    width_kv = KV_HEADS * HEAD_DIM
    rows, cols = group * span, CHUNK * span
    sort_rows(spans_ref, own_ref, other_ref, sorted_ref, span)
    dk_scr[...] = jnp.zeros(dk_scr.shape, jnp.float32)
    dv_scr[...] = jnp.zeros(dv_scr.shape, jnp.float32)
    for part in range(2):
        position = spans_ref[0, 4, part]
        for g in range(KV_HEADS):
            q_scr[g] = group_rows(q_ref, part, span, g) * jnp.bfloat16(HEAD_DIM**-0.5)
            grad = group_rows(grad_ref, part, span, g)
            grad_scr[g] = grad
            delta_ref[g] = jnp.sum(
                grad.astype(jnp.float32) * group_rows(out_ref, part, span, g), 1, keepdims=True
            )
        dq_scr[...] = jnp.zeros(dq_scr.shape, jnp.float32)

        def step(i, unused):
            visible = seen(position, i, span, rows, cols)
            base = pl.multiple_of(i * cols, cols)
            for g in range(KV_HEADS):
                k = sorted_ref[pl.ds(base, cols), g * HEAD_DIM : (g + 1) * HEAD_DIM]
                v = sorted_ref[
                    pl.ds(base, cols), width_kv + g * HEAD_DIM : width_kv + (g + 1) * HEAD_DIM
                ]
                q, grad = q_scr[g], grad_scr[g]
                s = lax.dot_general(
                    q, k, (((1,), (1,)), ((), ())), preferred_element_type=jnp.float32
                )
                probs = jnp.where(visible, jnp.exp(s - lse_ref[part * KV_HEADS + g]), 0.0)
                grad_probs = lax.dot_general(
                    grad, v, (((1,), (1,)), ((), ())), preferred_element_type=jnp.float32
                )
                grad_s = (probs * (grad_probs - delta_ref[g])).astype(jnp.bfloat16)
                dq_scr[g] += jnp.dot(grad_s, k, preferred_element_type=jnp.float32)
                dk_scr[g, pl.ds(base, cols), :] += lax.dot_general(
                    grad_s, q, (((0,), (0,)), ((), ())), preferred_element_type=jnp.float32
                )
                dv_scr[g, pl.ds(base, cols), :] += lax.dot_general(
                    probs.astype(jnp.bfloat16), grad, (((0,), (0,)), ((), ())),
                    preferred_element_type=jnp.float32,
                )
            return 0

        lax.fori_loop(0, (position + CHUNK) // CHUNK, step, 0)
        for g in range(KV_HEADS):
            dq = dq_scr[g] * HEAD_DIM**-0.5
            for j in range(group):
                h = g * group + j
                dq_ref[part * span : (part + 1) * span, h * HEAD_DIM : (h + 1) * HEAD_DIM] = dq[
                    j * span : (j + 1) * span
                ]
    for m, ref in enumerate((own_grad_ref, other_grad_ref)):
        for z in range(4):
            for j in range(2):
                start = pl.multiple_of(spans_ref[m, z, j] * span, span)
                parts = [scr[g, pl.ds(start, span), :] for scr in (dk_scr, dv_scr) for g in range(KV_HEADS)]
                ref[z, j * span : (j + 1) * span, :] = jnp.concatenate(parts, 1).astype(jnp.bfloat16)


def attend_back(spans, queries, own, other, out, lse, grad):
    rows, width = queries.shape
    group = HEADS // KV_HEADS
    stacked = group * rows // 2
    wide = own.shape[2]
    vmem = pl.BlockSpec(memory_space=pltpu.VMEM)
    return pl.pallas_call(
        attend_back_kernel,
        out_shape=(
            jax.ShapeDtypeStruct((rows, width), jnp.float32),
            jax.ShapeDtypeStruct((4, rows, wide), jnp.bfloat16),
            jax.ShapeDtypeStruct((4, rows, wide), jnp.bfloat16),
        ),
        in_specs=[pl.BlockSpec(memory_space=pltpu.SMEM)] + [vmem] * 6,
        out_specs=(vmem, vmem, vmem),
        scratch_shapes=[
            pltpu.VMEM((8 * rows, wide), jnp.bfloat16),
            pltpu.VMEM((KV_HEADS, stacked, HEAD_DIM), jnp.bfloat16),
            pltpu.VMEM((KV_HEADS, stacked, HEAD_DIM), jnp.bfloat16),
            pltpu.VMEM((KV_HEADS, stacked, 1), jnp.float32),
            pltpu.VMEM((KV_HEADS, stacked, HEAD_DIM), jnp.float32),
            pltpu.VMEM((KV_HEADS, 8 * rows, HEAD_DIM), jnp.float32),
            pltpu.VMEM((KV_HEADS, 8 * rows, HEAD_DIM), jnp.float32),
        ],
        compiler_params=pltpu.CompilerParams(vmem_limit_bytes=32 * 2**20),
        name="attend_back",
    )(spans, queries, own, other, out, lse, grad)


BF = jnp.bfloat16
F32 = jnp.float32
LANES = 128
GU_PAD = 96
X_PAIRS = [(j, j ^ 1) for j in range(4)]
Y_PAIRS = [(j, j ^ 2) for j in range(4)]
CORE_PAIRS = [(j, j ^ 1) for j in range(8)]
EXTRA = 2


def up_pairs(first, last):
    return [(2 * z + c, 2 * z + 2 + c) for z in range(first, last) for c in range(2)]


def down_pairs(first, last):
    return [(2 * z + 2 + c, 2 * z + c) for z in range(first, last) for c in range(2)]


def swap_x(a):
    return lax.ppermute(a, "batch", X_PAIRS)


def swap_y(a):
    return lax.ppermute(a, "batch", Y_PAIRS)


def swap_core(a):
    return lax.ppermute(a, "ctx", CORE_PAIRS)


def tiles(a):
    rows, cols = a.shape
    a = a.reshape(rows // 8, 8, cols // LANES, LANES)
    return a.transpose(0, 2, 1, 3).reshape(rows * cols // (8 * LANES), 8, LANES)


def untile(a, cols):
    rows = a.shape[0] * 8 * LANES // cols
    a = a.reshape(rows // 8, cols // LANES, 8, LANES)
    return a.transpose(0, 2, 1, 3).reshape(rows, cols)


def pad_to(a, rows, cols):
    return jnp.pad(a, ((0, rows - a.shape[0]), (0, cols - a.shape[1])))


def halves_of(a):
    half = a.shape[1] // 2
    return jnp.stack([tiles(a[:, :half]), tiles(a[:, half:])])


def whole_of(pair, cols):
    return jnp.concatenate([untile(pair[0], cols // 2), untile(pair[1], cols // 2)], 1)


def gather_line(a, z):
    u1 = lax.ppermute(a, "ctx", up_pairs(0, 3))
    d1 = lax.ppermute(a, "ctx", down_pairs(0, 3))
    u2 = lax.ppermute(u1, "ctx", up_pairs(1, 3))
    d2 = lax.ppermute(d1, "ctx", down_pairs(0, 2))
    u3 = lax.ppermute(u2, "ctx", up_pairs(2, 3))
    d3 = lax.ppermute(d2, "ctx", down_pairs(0, 1))
    seven = jnp.stack([u3, u2, u1, a, d1, d2, d3])
    return lax.dynamic_slice_in_dim(seven, 3 - z, 4, 0)


def gather_plane(a):
    first, second = a[:2], a[2:]
    x_first = swap_x(first)
    y_second = swap_y(second)
    x_second = swap_x(second)
    y_first = swap_y(first)
    diag_first = swap_y(x_first)
    diag_second = swap_x(y_second)
    return ((first, second), (x_first, x_second), (y_first, y_second), (diag_first, diag_second))


def place(pieces, b, start, stop):
    shape = pieces[0][0].shape
    whole = jnp.zeros((4, 4, shape[1], stop - start, 8, LANES), BF)
    for step, pair in enumerate(pieces):
        for part, piece in enumerate(pair):
            whole = lax.dynamic_update_slice(
                whole, piece[None, :, :, start:stop], (b ^ step, 2 * part, 0, 0, 0, 0)
            )
    return whole


def add(*terms):
    total = terms[0].astype(F32)
    for term in terms[1:]:
        total = total + term.astype(F32)
    return total.astype(BF)


def scatter_plane(g, b):
    own, xs, ys, ds = [lax.dynamic_index_in_dim(g, b ^ k, 0, keepdims=False) for k in range(4)]
    diag_first = swap_x(ds[:2])
    diag_second = swap_y(ds[2:])
    x_first = swap_x(xs[:2])
    y_second = swap_y(ys[2:])
    x_second = swap_x(add(xs[2:], diag_second))
    y_first = swap_y(add(ys[:2], diag_first))
    return jnp.concatenate(
        [add(own[:2], x_first, y_first), add(own[2:], x_second, y_second)], 0
    )


def scatter_line(t, z):
    def block(k):
        return lax.dynamic_index_in_dim(t, jnp.clip(z + k, 0, 3), 0, keepdims=False)

    def pass_on(a, first, last, way):
        if way > 0:
            got = lax.ppermute(a, "ctx", up_pairs(first, last))
            return jnp.where((z > first) & (z <= last), got, 0)
        got = lax.ppermute(a, "ctx", down_pairs(first, last))
        return jnp.where((z >= first) & (z < last), got, 0)

    up = pass_on(block(3), 0, 1, 1)
    down = pass_on(block(-3), 2, 3, -1)
    up = pass_on(add(block(2), up), 0, 2, 1)
    down = pass_on(add(block(-2), down), 1, 3, -1)
    up = pass_on(add(block(1), up), 0, 3, 1)
    down = pass_on(add(block(-1), down), 0, 3, -1)
    return block(0).astype(F32) + up.astype(F32) + down.astype(F32)


def split_high(a, parts):
    out = []
    for unused in range(parts):
        high = lax.reduce_precision(a, 8, 7)
        out.append(high.astype(BF))
        a = a - high
    return out


def local_block(tokens, attention_weights, feedforward_weights, norm_gains, span_order, cotangent):
    rows_here = tokens.shape[1]
    halves = rows_here // 2
    width_q = HEADS * HEAD_DIM
    width_kv = KV_HEADS * HEAD_DIM
    wide = 2 * 512
    b = lax.axis_index("batch")
    place_ctx = lax.axis_index("ctx")
    z = place_ctx // 2
    c = place_ctx % 2
    device = b * 8 + place_ctx
    own_gain = D // 8

    def pick(first, second):
        return jnp.where(c == 0, first, second)

    def merge(mine, other):
        return pick(
            jnp.concatenate([mine, other], -1), jnp.concatenate([other, mine], -1)
        )

    def half_of(a, k):
        half = a.shape[-1] // 2
        return jnp.where((c ^ k) == 0, a[..., :half], a[..., half:])

    def pair_up(shard):
        mine = pick(shard[0], shard[1])
        other = swap_core(pick(shard[1], shard[0]))
        return pick(jnp.stack([mine, other]), jnp.stack([other, mine]))

    att_rows = attention_weights.shape[0] // D
    att_shard = halves_of(pad_to(attention_weights.reshape(att_rows, D), att_rows, wide))
    gain_parts = jnp.stack(split_high(norm_gains, 3), 1)
    gain_rows = jnp.pad(gain_parts, ((0, 0), (0, 8 * EXTRA - 3), (0, LANES - own_gain)))
    gain_rows = gain_rows.reshape(2, EXTRA, 8, LANES)
    att_chip = pair_up(jnp.concatenate([att_shard, gain_rows], 1))
    att_pieces = gather_plane(gather_line(att_chip, z))
    att_body = att_rows * wide // (2 * 8 * LANES)
    att_mine = place(att_pieces, b, 0, att_body).reshape(-1, 8, LANES)
    gain_mine = place(att_pieces, b, att_body, att_body + EXTRA)
    att_other = swap_core(att_mine)
    gain_other = swap_core(gain_mine)

    def gain_from(a):
        parts = a[0, :, :, 0, :3, :own_gain].astype(F32)
        return (parts[:, :, 0] + parts[:, :, 1] + parts[:, :, 2]).reshape(D)

    gain_m, gain_o = gain_from(gain_mine), gain_from(gain_other)
    gain_full = jnp.stack([pick(gain_m, gain_o), pick(gain_o, gain_m)])

    gu_rows = feedforward_weights.shape[0] // FF
    down_rows = feedforward_weights.shape[0] // D
    mixed = 2 * D // gu_rows
    rest = 2 * D - mixed * gu_rows
    rest_pad = -(-rest // 8) * 8
    gu_shard = halves_of(pad_to(feedforward_weights.reshape(gu_rows, FF), GU_PAD, FF))
    down_shard = halves_of(pad_to(feedforward_weights.reshape(down_rows, D), down_rows, wide))
    mixed_shard = jnp.concatenate(
        [
            halves_of(pad_to(feedforward_weights[: rest * FF].reshape(rest, FF), rest_pad, FF)),
            halves_of(
                pad_to(feedforward_weights[rest * FF :].reshape(-1, D), down_rows - rest * FF // D, wide)
            ),
        ],
        1,
    )
    ff_shard = jnp.where(device < mixed, gu_shard, jnp.where(device == mixed, mixed_shard, down_shard))
    ff_pieces = gather_plane(gather_line(pair_up(ff_shard), z))
    ff_body = ff_shard.shape[1]
    ff_mine = place(ff_pieces, b, 0, ff_body).reshape(-1, 8, LANES)
    ff_other = swap_core(ff_mine)
    gu_total = mixed * GU_PAD + rest_pad
    gu_cut = gu_total * FF // (2 * 8 * LANES)

    def matrices(a):
        return untile(a[:gu_cut], FF // 2), untile(a[gu_cut:], wide // 2)

    gu_m, down_m = matrices(ff_mine)
    gu_o, down_o = matrices(ff_other)

    pad_row = jnp.arange(gu_total, dtype=jnp.int32)
    true_row = pad_row // GU_PAD * gu_rows + pad_row % GU_PAD
    real = pad_row % GU_PAD < gu_rows
    is_gate = real & (true_row < D)
    is_up = real & (true_row >= D)
    spread = ((true_row % D)[None, :] == jnp.arange(D, dtype=jnp.int32)[:, None]) & real[None, :]
    spread = spread.astype(BF)
    third = D // 3
    order3 = jnp.arange(D, dtype=jnp.int32)
    perm3 = (order3[:, None] == (order3 % third * 3 + order3 // third)[None, :]).astype(BF)

    offsets = jnp.arange(halves, dtype=jnp.int32)
    query_pos = (span_order[0][:, None] * halves + offsets[None, :]).reshape(rows_here)
    cos_table, sin_table = rope_tables(query_pos)

    inputs = tokens[0].astype(F32)
    hidden_f, norm_one_pull = jax.vjp(normalize, inputs, gain_full[0])
    hidden = hidden_f.astype(BF)
    hidden3 = jnp.dot(hidden, perm3, preferred_element_type=F32).astype(BF)
    hidden3 = hidden3.reshape(rows_here, 3, third)
    att_m, att_o = untile(att_mine, wide // 2), untile(att_other, wide // 2)
    cut_k, cut_v, cut_o = D, D + third, D + 2 * third

    def project(a, start, stop):
        return merge(
            jnp.dot(a, att_m[start:stop], preferred_element_type=F32),
            jnp.dot(a, att_o[start:stop], preferred_element_type=F32),
        )

    def thirds(start, stop):
        out = project(hidden3.transpose(1, 0, 2).reshape(3 * rows_here, third), start, stop)
        out = out.reshape(3, rows_here, wide)
        return out[0, :, :third] + out[1, :, third : 2 * third] + out[2, :, 2 * third : 3 * third]

    query_raw = project(hidden, 0, D)[:, :width_q].reshape(rows_here, HEADS, HEAD_DIM)
    key_raw = thirds(cut_k, cut_v).reshape(rows_here, KV_HEADS, HEAD_DIM)
    values = thirds(cut_v, cut_o).astype(BF)
    query_rot, query_pull = jax.vjp(lambda a: rotate(a, cos_table, sin_table), query_raw)
    key_rot, key_pull = jax.vjp(lambda a: rotate(a, cos_table, sin_table), key_raw)
    queries = query_rot.astype(BF).reshape(rows_here, width_q)
    keys = key_rot.astype(BF).reshape(rows_here, width_kv)

    span_rows = jnp.pad(span_order.astype(BF), ((0, 15), (0, 2 * width_kv - 2)))
    key_value = jnp.concatenate([jnp.concatenate([keys, values], 1), span_rows], 0)
    line_mine = gather_line(key_value, z)
    line_other = swap_core(line_mine)
    spans = jnp.stack([line_mine[:, rows_here, :2], line_other[:, rows_here, :2]]).astype(jnp.int32)
    spans = jnp.concatenate([spans, jnp.broadcast_to(span_order[None], (2, 1, 2))], 1)
    attended, log_total = attend(spans, queries, line_mine, line_other)
    attended_low = attended.astype(BF)
    middle = inputs + project(attended_low, cut_o, cut_o + D)[:, :D]
    hidden_two_f, norm_two_pull = jax.vjp(normalize, middle, gain_full[1])
    hidden_two = hidden_two_f.astype(BF)
    spread_two = jnp.dot(hidden_two, spread, preferred_element_type=F32).astype(BF)
    for_gate = jnp.where(is_gate[None, :], spread_two, 0)
    for_up = jnp.where(is_up[None, :], spread_two, 0)
    gate_end = -(-D // gu_rows) * GU_PAD
    up_start = D // gu_rows * GU_PAD

    def widen(a, start, stop):
        return merge(
            jnp.dot(a[:, start:stop], gu_m[start:stop], preferred_element_type=F32),
            jnp.dot(a[:, start:stop], gu_o[start:stop], preferred_element_type=F32),
        )

    gate = widen(for_gate, 0, gate_end)
    upward = widen(for_up, up_start, gu_total)
    activ_f, swiglu_pull = jax.vjp(swiglu, gate, upward)
    activ = activ_f.astype(BF)
    result = middle + merge(
        jnp.dot(activ, down_m, preferred_element_type=F32),
        jnp.dot(activ, down_o, preferred_element_type=F32),
    )[:, :D]

    grad_result = cotangent[0]
    grad_wide = jnp.pad(grad_result, ((0, 0), (0, wide - D)))

    def times_transposed(a, w):
        return lax.dot_general(a, w, (((1,), (1,)), ((), ())), preferred_element_type=F32)

    def transposed_times(a, w):
        return lax.dot_general(a, w, (((0,), (0,)), ((), ())), preferred_element_type=F32)

    grad_activ = times_transposed(half_of(grad_wide, 0), down_m)
    grad_activ = grad_activ + times_transposed(half_of(grad_wide, 1), down_o)
    grad_gate_f, grad_up_f = swiglu_pull(grad_activ)
    grad_gate = grad_gate_f.astype(BF)
    grad_upward = grad_up_f.astype(BF)
    stacked_in = jnp.concatenate([for_gate, for_up], 0)
    stacked_out = jnp.concatenate([grad_gate, grad_upward], 0)

    def ff_terms(k):
        gu = transposed_times(stacked_in, half_of(stacked_out, k)).astype(BF)
        down = transposed_times(activ, half_of(grad_wide, k)).astype(BF)
        return jnp.concatenate([tiles(gu), tiles(down)], 0)

    ff_from = swap_core(ff_terms(1))
    ff_sum = add(ff_terms(0), ff_from).reshape(4, 4, 2, ff_body, 8, LANES)
    ff_own = scatter_line(scatter_plane(ff_sum, b), z)

    def narrow(a, start, stop):
        return times_transposed(half_of(a, 0), gu_m[start:stop]) + times_transposed(
            half_of(a, 1), gu_o[start:stop]
        )

    back_gate = jnp.where(is_gate[None, :gate_end], narrow(grad_gate, 0, gate_end), 0.0)
    back_up = jnp.where(is_up[None, up_start:], narrow(grad_upward, up_start, gu_total), 0.0)

    def collapse(a, start, stop):
        parts = jnp.concatenate(split_high(a, 2), 1)
        table = jnp.concatenate([spread[:, start:stop]] * 2, 1)
        return times_transposed(parts, table)

    grad_hidden_two = collapse(back_gate, 0, gate_end) + collapse(back_up, up_start, gu_total)
    grad_middle_norm, grad_gain_two = norm_two_pull(grad_hidden_two)
    grad_middle = grad_result.astype(F32) + grad_middle_norm
    grad_branch = grad_middle.astype(BF)
    branch_wide = jnp.pad(grad_branch, ((0, 0), (0, wide - D)))

    def project_back(a, start, stop):
        return times_transposed(half_of(a, 0), att_m[start:stop]) + times_transposed(
            half_of(a, 1), att_o[start:stop]
        )

    grad_attended = project_back(branch_wide, cut_o, cut_o + D).astype(BF)
    grad_query_rot, both_mine, both_other = attend_back(
        spans, queries, line_mine, line_other, attended, log_total, grad_attended
    )
    both_from = swap_core(both_other.astype(BF))
    both_own = scatter_line(add(both_mine, both_from), z)
    grad_key_rot, grad_value_f = both_own[:, :width_kv], both_own[:, width_kv:]
    grad_query_raw = query_pull(grad_query_rot.reshape(rows_here, HEADS, HEAD_DIM))[0]
    grad_key_raw = key_pull(grad_key_rot.reshape(rows_here, KV_HEADS, HEAD_DIM))[0]
    grad_query = grad_query_raw.reshape(rows_here, width_q).astype(BF)
    grad_key = grad_key_raw.reshape(rows_here, width_kv).astype(BF)
    grad_value = grad_value_f.astype(BF)

    def spots(a):
        return jnp.concatenate(
            [jnp.pad(a, ((0, 0), (q * third, wide - (q + 1) * third))) for q in range(3)], 0
        )

    query_wide = jnp.pad(grad_query, ((0, 0), (0, wide - D)))
    key_spots, value_spots = spots(grad_key), spots(grad_value)
    hidden_rows = hidden3.transpose(1, 0, 2).reshape(3 * rows_here, third)
    back_three = project_back(key_spots, cut_k, cut_v) + project_back(value_spots, cut_v, cut_o)
    back_three = back_three.reshape(3, rows_here, third).transpose(1, 0, 2).reshape(rows_here, D)
    grad_hidden = project_back(query_wide, 0, D) + times_transposed(
        jnp.concatenate(split_high(back_three, 2), 1), jnp.concatenate([perm3, perm3], 1)
    )
    grad_inputs_norm, grad_gain_one = norm_one_pull(grad_hidden)
    grad_inputs = grad_middle + grad_inputs_norm

    gain_terms = jnp.stack([grad_gain_one, grad_gain_two]).reshape(2, 8, own_gain)
    gain_terms = jnp.pad(
        jnp.stack(split_high(gain_terms, 2), 2),
        ((0, 0), (0, 0), (0, 8 * EXTRA - 2), (0, LANES - own_gain)),
    ).reshape(2, 4, 2, EXTRA, 8, LANES)

    def att_terms(k):
        terms = jnp.concatenate(
            [
                transposed_times(hidden, half_of(query_wide, k)).astype(BF),
                transposed_times(hidden_rows, half_of(key_spots, k)).astype(BF),
                transposed_times(hidden_rows, half_of(value_spots, k)).astype(BF),
                transposed_times(attended_low, half_of(branch_wide, k)).astype(BF),
            ],
            0,
        )
        gain = jnp.where((c ^ k) == 0, gain_terms[0], gain_terms[1])
        gain = jnp.broadcast_to(gain[None], (4, 4, 2, EXTRA, 8, LANES))
        return jnp.concatenate([tiles(terms).reshape(4, 4, 2, att_body, 8, LANES), gain], 3)

    att_from = swap_core(att_terms(1))
    att_own = scatter_line(scatter_plane(add(att_terms(0), att_from), b), z)

    def settle(own):
        mine = pick(own[0], own[1])
        other = swap_core(pick(own[1], own[0]))
        return pick(jnp.stack([mine, other]), jnp.stack([other, mine]))

    ff_done = settle(ff_own)
    att_done = settle(att_own)
    gain_own = att_done[:, att_body, 0, :own_gain] + att_done[:, att_body, 1, :own_gain]
    att_flat = whole_of(att_done[:, :att_body], wide)[:, :D].reshape(-1)
    gu_flat = whole_of(ff_done, FF)[:gu_rows].reshape(-1)
    down_flat = whole_of(ff_done, wide)[:, :D].reshape(-1)
    cut = rest_pad * FF // (2 * 8 * LANES)
    mixed_flat = jnp.concatenate(
        [
            whole_of(ff_done[:, :cut], FF)[:rest].reshape(-1),
            whole_of(ff_done[:, cut:], wide)[:, :D].reshape(-1),
        ]
    )
    ff_flat = jnp.where(device < mixed, gu_flat, jnp.where(device == mixed, mixed_flat, down_flat))
    return (
        result.astype(BF)[None],
        grad_inputs[None],
        att_flat,
        ff_flat,
        gain_own,
    )


def solution(mesh):
    fits = mesh.shape["batch"] == 4 and mesh.shape["ctx"] == 8
    local = local_block if fits else local_any
    placed = (
        P("batch", "ctx", None),
        P(("batch", "ctx")),
        P(("batch", "ctx")),
        P(None, "ctx"),
        P("batch", "ctx"),
        P("batch", "ctx", None),
    )
    return jax.shard_map(
        local,
        mesh=mesh,
        in_specs=placed,
        out_specs=(
            P("batch", "ctx", None),
            P("batch", "ctx", None),
            P(("batch", "ctx")),
            P(("batch", "ctx")),
            P(None, "ctx"),
        ),
        check_vma=False,
    )
```

```python
import functools
import math

import jax
import jax.numpy as jnp
from jax import lax
from jax.experimental import pallas as pl
from jax.experimental.pallas import tpu as pltpu
from jax.sharding import PartitionSpec as P

D = 960
HEADS = 15
KV_HEADS = 5
HEAD_DIM = 64
FF = 2560


ROPE_BASE = 100000.0
EPS = 1e-05
NEG = -1e30


def normalize(values, gain):
    return values * lax.rsqrt(jnp.mean(values * values, -1, keepdims=True) + EPS) * gain


def swiglu(gate, upward):
    return jax.nn.silu(gate) * upward


def rope_tables(positions):
    halves = HEAD_DIM // 2
    inverse_freq = ROPE_BASE ** (-jnp.arange(halves, dtype=jnp.float32) / halves)
    angles = positions.astype(jnp.float32)[:, None] * inverse_freq[None, :]
    return (jnp.cos(angles), jnp.sin(angles))


def rotate(values, cos_table, sin_table):
    halves = HEAD_DIM // 2
    first = values[..., :halves]
    second = values[..., halves:]
    cos_table = cos_table[:, None, :]
    sin_table = sin_table[:, None, :]
    return jnp.concatenate(
        [first * cos_table - second * sin_table, second * cos_table + first * sin_table], -1
    )


def split_flat(flat, shapes):
    pieces = []
    offset = 0
    for rows_in, cols_in in shapes:
        pieces.append(flat[offset : offset + rows_in * cols_in].reshape(rows_in, cols_in))
        offset += rows_in * cols_in
    return pieces


def unpack(att_flat, ff_flat):
    width_q = HEADS * HEAD_DIM
    width_kv = KV_HEADS * HEAD_DIM
    att_parts = split_flat(att_flat, [(D, width_q), (D, width_kv), (D, width_kv), (width_q, D)])
    ff_parts = split_flat(ff_flat, [(D, FF), (D, FF), (FF, D)])
    return (att_parts, ff_parts)


def score_block(queries, key_block, query_pos, key_pos):
    keys_three = key_block.reshape(key_block.shape[0], KV_HEADS, HEAD_DIM)
    scores = jnp.einsum(
        "qhgd,khd->hgqk", queries, keys_three, preferred_element_type=jnp.float32
    ) * HEAD_DIM ** (-0.5)
    visible = key_pos[None, None, None, :] <= query_pos[None, None, :, None]
    return (scores, visible)


def attention_forward(queries, key_all, value_all, query_pos, key_pos, block):
    rows_here = queries.shape[0]
    group = HEADS // KV_HEADS
    count = key_all.shape[0] // block
    key_blocks = key_all.reshape(count, block, key_all.shape[1])
    value_blocks = value_all.reshape(count, block, value_all.shape[1])
    pos_blocks = key_pos.reshape(count, block)

    def online_step(carry, item):
        top, total, accum = carry
        key_block, value_block, pos_block = item
        scores, visible = score_block(queries, key_block, query_pos, pos_block)
        scores = jnp.where(visible, scores, NEG)
        new_top = jnp.maximum(top, jnp.max(scores, -1))
        weights = jnp.where(visible, jnp.exp(scores - new_top[..., None]), 0.0)
        factor = jnp.exp(top - new_top)
        total = total * factor + jnp.sum(weights, -1)
        values_three = value_block.reshape(block, KV_HEADS, HEAD_DIM)
        accum = accum * jnp.transpose(factor, (2, 0, 1))[..., None]
        accum = accum + jnp.einsum(
            "hgqk,khd->qhgd",
            weights.astype(jnp.bfloat16),
            values_three,
            preferred_element_type=jnp.float32,
        )
        return ((new_top, total, accum), None)

    start_top = jnp.full((KV_HEADS, group, rows_here), NEG, jnp.float32)
    start_total = jnp.zeros((KV_HEADS, group, rows_here), jnp.float32)
    start_out = jnp.zeros((rows_here, KV_HEADS, group, HEAD_DIM), jnp.float32)
    (top, total, accum), unused = lax.scan(
        online_step, (start_top, start_total, start_out), (key_blocks, value_blocks, pos_blocks)
    )
    log_total = top + jnp.log(total)
    attended = accum / jnp.transpose(total, (2, 0, 1))[..., None]
    return (attended, log_total)


def attention_backward(
    queries, key_all, value_all, query_pos, key_pos, block, log_total, grad_out, attended
):
    rows_here = queries.shape[0]
    group = HEADS // KV_HEADS
    width_kv = key_all.shape[1]
    count = key_all.shape[0] // block
    items = (
        key_all.reshape(count, block, width_kv),
        value_all.reshape(count, block, width_kv),
        key_pos.reshape(count, block),
    )
    delta = jnp.transpose(jnp.sum(grad_out.astype(jnp.float32) * attended, -1), (1, 2, 0))

    def grad_step(grad_query, item):
        key_block, value_block, pos_block = item
        scores, visible = score_block(queries, key_block, query_pos, pos_block)
        probs = jnp.where(visible, jnp.exp(scores - log_total[..., None]), 0.0)
        values_three = value_block.reshape(block, KV_HEADS, HEAD_DIM)
        grad_probs = jnp.einsum(
            "qhgd,khd->hgqk", grad_out, values_three, preferred_element_type=jnp.float32
        )
        grad_scores = (probs * (grad_probs - delta[..., None])).astype(jnp.bfloat16)
        keys_three = key_block.reshape(block, KV_HEADS, HEAD_DIM)
        grad_query = grad_query + jnp.einsum(
            "hgqk,khd->qhgd", grad_scores, keys_three, preferred_element_type=jnp.float32
        )
        grad_key = jnp.einsum(
            "hgqk,qhgd->khd", grad_scores, queries, preferred_element_type=jnp.float32
        )
        grad_value = jnp.einsum(
            "hgqk,qhgd->khd",
            probs.astype(jnp.bfloat16),
            grad_out,
            preferred_element_type=jnp.float32,
        )
        return (
            grad_query,
            (grad_key.reshape(block, width_kv), grad_value.reshape(block, width_kv)),
        )

    start_query = jnp.zeros((rows_here, KV_HEADS, group, HEAD_DIM), jnp.float32)
    grad_query, (grad_keys, grad_values) = lax.scan(grad_step, start_query, items)
    return (
        grad_query,
        grad_keys.reshape(count * block, width_kv),
        grad_values.reshape(count * block, width_kv),
    )


def local_any(tokens, attention_weights, feedforward_weights, norm_gains, span_order, cotangent):
    ctx_count = lax.axis_size("ctx")
    batch_count = lax.axis_size("batch")
    rows_here = tokens.shape[1]
    halves = rows_here // 2
    length = rows_here * ctx_count
    group = HEADS // KV_HEADS
    width_q = HEADS * HEAD_DIM
    width_kv = KV_HEADS * HEAD_DIM
    block = math.gcd(length, 512)
    scaling = HEAD_DIM ** (-0.5)
    att_full, ff_full = (
        lax.all_gather(attention_weights, ("batch", "ctx"), axis=0, tiled=True),
        lax.all_gather(feedforward_weights, ("batch", "ctx"), axis=0, tiled=True),
    )
    gain_full = lax.all_gather(norm_gains, "ctx", axis=1, tiled=True)
    order_full = lax.all_gather(span_order, "ctx", axis=1, tiled=True)
    offsets = jnp.arange(halves, dtype=jnp.int32)
    key_pos = (order_full[0][:, None] * halves + offsets[None, :]).reshape(length)
    query_pos = (span_order[0][:, None] * halves + offsets[None, :]).reshape(rows_here)
    cos_table, sin_table = rope_tables(query_pos)
    (w_query, w_key, w_value, w_out), (w_gate, w_up, w_down) = unpack(att_full, ff_full)
    inputs = tokens[0].astype(jnp.float32)
    hidden_f, norm_one_pull = jax.vjp(normalize, inputs, gain_full[0])
    hidden = hidden_f.astype(jnp.bfloat16)
    query_raw = jnp.dot(hidden, w_query, preferred_element_type=jnp.float32).reshape(
        rows_here, HEADS, HEAD_DIM
    )
    key_raw = jnp.dot(hidden, w_key, preferred_element_type=jnp.float32).reshape(
        rows_here, KV_HEADS, HEAD_DIM
    )
    values = jnp.dot(hidden, w_value, preferred_element_type=jnp.float32).astype(jnp.bfloat16)
    query_rot, query_pull = jax.vjp(lambda a: rotate(a, cos_table, sin_table), query_raw)
    key_rot, key_pull = jax.vjp(lambda a: rotate(a, cos_table, sin_table), key_raw)
    queries = query_rot.astype(jnp.bfloat16).reshape(rows_here, KV_HEADS, group, HEAD_DIM)
    keys = key_rot.astype(jnp.bfloat16).reshape(rows_here, width_kv)
    key_all, value_all = (
        lax.all_gather(keys, "ctx", axis=0, tiled=True),
        lax.all_gather(values, "ctx", axis=0, tiled=True),
    )
    attended, log_total = attention_forward(queries, key_all, value_all, query_pos, key_pos, block)
    attended_low = attended.reshape(rows_here, width_q).astype(jnp.bfloat16)
    middle = inputs + jnp.dot(attended_low, w_out, preferred_element_type=jnp.float32)
    hidden_two_f, norm_two_pull = jax.vjp(normalize, middle, gain_full[1])
    hidden_two = hidden_two_f.astype(jnp.bfloat16)
    gate = jnp.dot(hidden_two, w_gate, preferred_element_type=jnp.float32)
    upward = jnp.dot(hidden_two, w_up, preferred_element_type=jnp.float32)
    activ_f, swiglu_pull = jax.vjp(swiglu, gate, upward)
    activ = activ_f.astype(jnp.bfloat16)
    result = middle + jnp.dot(activ, w_down, preferred_element_type=jnp.float32)
    grad_result = cotangent[0]
    grad_down = jnp.einsum("tf,td->fd", activ, grad_result, preferred_element_type=jnp.float32)
    grad_activ = jnp.einsum("td,fd->tf", grad_result, w_down, preferred_element_type=jnp.float32)
    grad_gate_f, grad_up_f = swiglu_pull(grad_activ)
    grad_gate = grad_gate_f.astype(jnp.bfloat16)
    grad_upward = grad_up_f.astype(jnp.bfloat16)
    grad_w_gate = jnp.einsum("td,tf->df", hidden_two, grad_gate, preferred_element_type=jnp.float32)
    grad_w_up = jnp.einsum("td,tf->df", hidden_two, grad_upward, preferred_element_type=jnp.float32)
    grad_hidden_two = jnp.einsum("tf,df->td", grad_gate, w_gate, preferred_element_type=jnp.float32)
    grad_hidden_two = grad_hidden_two + jnp.einsum(
        "tf,df->td", grad_upward, w_up, preferred_element_type=jnp.float32
    )
    grad_middle_norm, grad_gain_two = norm_two_pull(grad_hidden_two)
    grad_middle = grad_result.astype(jnp.float32) + grad_middle_norm
    grad_branch = grad_middle.astype(jnp.bfloat16)
    grad_w_out = jnp.einsum(
        "tq,td->qd", attended_low, grad_branch, preferred_element_type=jnp.float32
    )
    grad_attended = jnp.einsum(
        "td,qd->tq", grad_branch, w_out, preferred_element_type=jnp.float32
    ).astype(jnp.bfloat16)
    grad_attended = grad_attended.reshape(rows_here, KV_HEADS, group, HEAD_DIM)
    grad_query_rot, grad_key_all, grad_value_all = attention_backward(
        queries, key_all, value_all, query_pos, key_pos, block, log_total, grad_attended, attended
    )
    grad_key_rot, grad_value_f = (
        lax.psum_scatter(
            grad_key_all.astype(jnp.bfloat16), "ctx", scatter_dimension=0, tiled=True
        ).astype(jnp.float32),
        lax.psum_scatter(
            grad_value_all.astype(jnp.bfloat16), "ctx", scatter_dimension=0, tiled=True
        ).astype(jnp.float32),
    )
    grad_query_raw = query_pull(grad_query_rot.reshape(rows_here, HEADS, HEAD_DIM) * scaling)[0]
    grad_key_raw = key_pull(grad_key_rot.reshape(rows_here, KV_HEADS, HEAD_DIM) * scaling)[0]
    grad_query = grad_query_raw.reshape(rows_here, width_q).astype(jnp.bfloat16)
    grad_key = grad_key_raw.reshape(rows_here, width_kv).astype(jnp.bfloat16)
    grad_value = grad_value_f.astype(jnp.bfloat16)
    grad_w_query = jnp.einsum("td,tq->dq", hidden, grad_query, preferred_element_type=jnp.float32)
    grad_w_key = jnp.einsum("td,tq->dq", hidden, grad_key, preferred_element_type=jnp.float32)
    grad_w_value = jnp.einsum("td,tq->dq", hidden, grad_value, preferred_element_type=jnp.float32)
    grad_hidden = jnp.einsum("tq,dq->td", grad_query, w_query, preferred_element_type=jnp.float32)
    grad_hidden = grad_hidden + jnp.einsum(
        "tq,dq->td", grad_key, w_key, preferred_element_type=jnp.float32
    )
    grad_hidden = grad_hidden + jnp.einsum(
        "tq,dq->td", grad_value, w_value, preferred_element_type=jnp.float32
    )
    grad_inputs_norm, grad_gain_one = norm_one_pull(grad_hidden)
    grad_inputs = grad_middle + grad_inputs_norm
    grad_att_flat = jnp.concatenate(
        [
            grad_w_query.reshape(-1),
            grad_w_key.reshape(-1),
            grad_w_value.reshape(-1),
            grad_w_out.reshape(-1),
        ]
    )
    grad_ff_flat = jnp.concatenate(
        [grad_w_gate.reshape(-1), grad_w_up.reshape(-1), grad_down.reshape(-1)]
    )
    width_own = D // ctx_count
    gain_terms = jnp.stack([grad_gain_one, grad_gain_two]).reshape(2, ctx_count, width_own)
    gain_terms = jnp.transpose(gain_terms, (1, 0, 2)).reshape(ctx_count, 2 * width_own)
    gain_terms = jnp.broadcast_to(
        gain_terms[None], (batch_count, ctx_count, 2 * width_own)
    ).reshape(batch_count * ctx_count, 2 * width_own)
    att_part, ff_part, gain_part = (
        lax.psum_scatter(
            grad_att_flat.astype(jnp.bfloat16), "batch", scatter_dimension=0, tiled=True
        ).astype(jnp.float32),
        lax.psum_scatter(
            grad_ff_flat.astype(jnp.bfloat16), "batch", scatter_dimension=0, tiled=True
        ).astype(jnp.float32),
        lax.psum_scatter(
            gain_terms.astype(jnp.bfloat16), "batch", scatter_dimension=0, tiled=True
        ).astype(jnp.float32),
    )
    grad_att_own, grad_ff_own, gain_own = (
        lax.psum_scatter(
            att_part.astype(jnp.bfloat16), "ctx", scatter_dimension=0, tiled=True
        ).astype(jnp.float32),
        lax.psum_scatter(
            ff_part.astype(jnp.bfloat16), "ctx", scatter_dimension=0, tiled=True
        ).astype(jnp.float32),
        lax.psum_scatter(
            gain_part.astype(jnp.bfloat16), "ctx", scatter_dimension=0, tiled=True
        ).astype(jnp.float32),
    )
    grad_gain_own = gain_own.reshape(2, width_own)
    return (
        result.astype(jnp.bfloat16)[None],
        grad_inputs[None],
        grad_att_own,
        grad_ff_own,
        grad_gain_own,
    )


CHUNK = 4


def sort_rows(spans_ref, own_ref, other_ref, sorted_ref, span):
    for m, ref in enumerate((own_ref, other_ref)):
        for z in range(4):
            for j in range(2):
                start = pl.multiple_of(spans_ref[m, z, j] * span, span)
                sorted_ref[pl.ds(start, span), :] = ref[z, j * span : (j + 1) * span, :]


def group_rows(ref, part, span, head):
    group = HEADS // KV_HEADS
    rows = ref[part * span : (part + 1) * span, :]
    columns = [
        rows[:, (head * group + j) * HEAD_DIM : (head * group + j + 1) * HEAD_DIM]
        for j in range(group)
    ]
    return jnp.concatenate(columns, 0)


def seen(position, step, span, rows, cols):
    row = lax.broadcasted_iota(jnp.int32, (rows, cols), 0) % span
    col = lax.broadcasted_iota(jnp.int32, (rows, cols), 1)
    return col + step * cols <= row + position * span


def attend_kernel(
    spans_ref, q_ref, own_ref, other_ref, out_ref, lse_ref, sorted_ref, q_scr, top_ref, sum_ref, acc_ref
):
    group = HEADS // KV_HEADS
    span = q_ref.shape[0] // 2
    width_kv = KV_HEADS * HEAD_DIM
    rows, cols = group * span, CHUNK * span
    sort_rows(spans_ref, own_ref, other_ref, sorted_ref, span)
    for part in range(2):
        position = spans_ref[0, 4, part]
        for g in range(KV_HEADS):
            q_scr[g] = group_rows(q_ref, part, span, g) * jnp.bfloat16(HEAD_DIM**-0.5)
        top_ref[...] = jnp.full(top_ref.shape, NEG, jnp.float32)
        sum_ref[...] = jnp.zeros(sum_ref.shape, jnp.float32)
        acc_ref[...] = jnp.zeros(acc_ref.shape, jnp.float32)

        def step(i, unused):
            visible = seen(position, i, span, rows, cols)
            base = pl.multiple_of(i * cols, cols)
            for g in range(KV_HEADS):
                k = sorted_ref[pl.ds(base, cols), g * HEAD_DIM : (g + 1) * HEAD_DIM]
                v = sorted_ref[
                    pl.ds(base, cols), width_kv + g * HEAD_DIM : width_kv + (g + 1) * HEAD_DIM
                ]
                s = lax.dot_general(
                    q_scr[g], k, (((1,), (1,)), ((), ())), preferred_element_type=jnp.float32
                )
                s = jnp.where(visible, s, NEG)
                old = top_ref[g]
                top = jnp.maximum(old, jnp.max(s, 1, keepdims=True))
                weights = jnp.where(visible, jnp.exp(s - top), 0.0)
                factor = jnp.exp(old - top)
                top_ref[g] = top
                sum_ref[g] = sum_ref[g] * factor + jnp.sum(weights, 1, keepdims=True)
                acc_ref[g] = acc_ref[g] * factor + jnp.dot(
                    weights.astype(jnp.bfloat16), v, preferred_element_type=jnp.float32
                )
            return 0

        lax.fori_loop(0, (position + CHUNK) // CHUNK, step, 0)
        for g in range(KV_HEADS):
            out = acc_ref[g] / sum_ref[g]
            lse_ref[part * KV_HEADS + g] = top_ref[g] + jnp.log(sum_ref[g])
            for j in range(group):
                h = g * group + j
                out_ref[part * span : (part + 1) * span, h * HEAD_DIM : (h + 1) * HEAD_DIM] = out[
                    j * span : (j + 1) * span
                ]


def attend(spans, queries, own, other):
    rows, width = queries.shape
    group = HEADS // KV_HEADS
    stacked = group * rows // 2
    vmem = pl.BlockSpec(memory_space=pltpu.VMEM)
    return pl.pallas_call(
        attend_kernel,
        out_shape=(
            jax.ShapeDtypeStruct((rows, width), jnp.float32),
            jax.ShapeDtypeStruct((2 * KV_HEADS, stacked, 1), jnp.float32),
        ),
        in_specs=[pl.BlockSpec(memory_space=pltpu.SMEM), vmem, vmem, vmem],
        out_specs=(vmem, vmem),
        scratch_shapes=[
            pltpu.VMEM((8 * rows, own.shape[2]), jnp.bfloat16),
            pltpu.VMEM((KV_HEADS, stacked, HEAD_DIM), jnp.bfloat16),
            pltpu.VMEM((KV_HEADS, stacked, 1), jnp.float32),
            pltpu.VMEM((KV_HEADS, stacked, 1), jnp.float32),
            pltpu.VMEM((KV_HEADS, stacked, HEAD_DIM), jnp.float32),
        ],
        compiler_params=pltpu.CompilerParams(vmem_limit_bytes=24 * 2**20),
        cost_estimate=pl.CostEstimate(flops=10**6, bytes_accessed=10**5, transcendentals=0),
        name="attend",
    )(spans, queries, own, other)


def attend_back_kernel(
    spans_ref, q_ref, own_ref, other_ref, out_ref, lse_ref, grad_ref,
    dq_ref, own_grad_ref, other_grad_ref,
    sorted_ref, q_scr, grad_scr, delta_ref, dq_scr, dk_scr, dv_scr,
):
    group = HEADS // KV_HEADS
    span = q_ref.shape[0] // 2
    width_kv = KV_HEADS * HEAD_DIM
    rows, cols = group * span, CHUNK * span
    sort_rows(spans_ref, own_ref, other_ref, sorted_ref, span)
    dk_scr[...] = jnp.zeros(dk_scr.shape, jnp.float32)
    dv_scr[...] = jnp.zeros(dv_scr.shape, jnp.float32)
    for part in range(2):
        position = spans_ref[0, 4, part]
        for g in range(KV_HEADS):
            q_scr[g] = group_rows(q_ref, part, span, g) * jnp.bfloat16(HEAD_DIM**-0.5)
            grad = group_rows(grad_ref, part, span, g)
            grad_scr[g] = grad
            delta_ref[g] = jnp.sum(
                grad.astype(jnp.float32) * group_rows(out_ref, part, span, g), 1, keepdims=True
            )
        dq_scr[...] = jnp.zeros(dq_scr.shape, jnp.float32)

        def step(i, unused):
            visible = seen(position, i, span, rows, cols)
            base = pl.multiple_of(i * cols, cols)
            for g in range(KV_HEADS):
                k = sorted_ref[pl.ds(base, cols), g * HEAD_DIM : (g + 1) * HEAD_DIM]
                v = sorted_ref[
                    pl.ds(base, cols), width_kv + g * HEAD_DIM : width_kv + (g + 1) * HEAD_DIM
                ]
                q, grad = q_scr[g], grad_scr[g]
                s = lax.dot_general(
                    q, k, (((1,), (1,)), ((), ())), preferred_element_type=jnp.float32
                )
                probs = jnp.where(visible, jnp.exp(s - lse_ref[part * KV_HEADS + g]), 0.0)
                grad_probs = lax.dot_general(
                    grad, v, (((1,), (1,)), ((), ())), preferred_element_type=jnp.float32
                )
                grad_s = (probs * (grad_probs - delta_ref[g])).astype(jnp.bfloat16)
                dq_scr[g] += jnp.dot(grad_s, k, preferred_element_type=jnp.float32)
                dk_scr[g, pl.ds(base, cols), :] += lax.dot_general(
                    grad_s, q, (((0,), (0,)), ((), ())), preferred_element_type=jnp.float32
                )
                dv_scr[g, pl.ds(base, cols), :] += lax.dot_general(
                    probs.astype(jnp.bfloat16), grad, (((0,), (0,)), ((), ())),
                    preferred_element_type=jnp.float32,
                )
            return 0

        lax.fori_loop(0, (position + CHUNK) // CHUNK, step, 0)
        for g in range(KV_HEADS):
            dq = dq_scr[g] * HEAD_DIM**-0.5
            for j in range(group):
                h = g * group + j
                dq_ref[part * span : (part + 1) * span, h * HEAD_DIM : (h + 1) * HEAD_DIM] = dq[
                    j * span : (j + 1) * span
                ]
    for m, ref in enumerate((own_grad_ref, other_grad_ref)):
        for z in range(4):
            for j in range(2):
                start = pl.multiple_of(spans_ref[m, z, j] * span, span)
                parts = [scr[g, pl.ds(start, span), :] for scr in (dk_scr, dv_scr) for g in range(KV_HEADS)]
                ref[z, j * span : (j + 1) * span, :] = jnp.concatenate(parts, 1).astype(jnp.bfloat16)


def attend_back(spans, queries, own, other, out, lse, grad):
    rows, width = queries.shape
    group = HEADS // KV_HEADS
    stacked = group * rows // 2
    wide = own.shape[2]
    vmem = pl.BlockSpec(memory_space=pltpu.VMEM)
    return pl.pallas_call(
        attend_back_kernel,
        out_shape=(
            jax.ShapeDtypeStruct((rows, width), jnp.float32),
            jax.ShapeDtypeStruct((4, rows, wide), jnp.bfloat16),
            jax.ShapeDtypeStruct((4, rows, wide), jnp.bfloat16),
        ),
        in_specs=[pl.BlockSpec(memory_space=pltpu.SMEM)] + [vmem] * 6,
        out_specs=(vmem, vmem, vmem),
        scratch_shapes=[
            pltpu.VMEM((8 * rows, wide), jnp.bfloat16),
            pltpu.VMEM((KV_HEADS, stacked, HEAD_DIM), jnp.bfloat16),
            pltpu.VMEM((KV_HEADS, stacked, HEAD_DIM), jnp.bfloat16),
            pltpu.VMEM((KV_HEADS, stacked, 1), jnp.float32),
            pltpu.VMEM((KV_HEADS, stacked, HEAD_DIM), jnp.float32),
            pltpu.VMEM((KV_HEADS, 8 * rows, HEAD_DIM), jnp.float32),
            pltpu.VMEM((KV_HEADS, 8 * rows, HEAD_DIM), jnp.float32),
        ],
        compiler_params=pltpu.CompilerParams(vmem_limit_bytes=32 * 2**20),
        cost_estimate=pl.CostEstimate(flops=10**6, bytes_accessed=10**5, transcendentals=0),
        name="attend_back",
    )(spans, queries, own, other, out, lse, grad)


TILE = 16
GU_TILES = 10
DOWN_TILES = 4
STEP = 256


def contract_last(a, w):
    return lax.dot_general(a, w, (((1,), (1,)), ((), ())), preferred_element_type=jnp.float32)


def contract_first(a, w):
    return lax.dot_general(a, w, (((0,), (0,)), ((), ())), preferred_element_type=jnp.float32)


def ff_kernel(gate_rt, up_rt, place_ref, mid_ref, gain_ref, grad_ref, target_ref, spread_ref, *refs):
    pieces, refs = refs[:10], refs[10:]
    out_ref, spread_out, act_ref, dgate_ref, dup_ref, dmid_ref, branch_ref, dgain_ref = refs[:8]
    w_scr, total_scr, back_scr, gwide_scr, sems = refs[8:]
    core = place_ref[0, 0]
    rows, width = mid_ref.shape
    half_out = DOWN_TILES * 128
    gu_rt = target_ref.shape[1] // TILE
    part = w_scr.shape[1] // 8
    copies = []
    for k in range(2):
        half = core if k == 0 else 1 - core
        spots = [(1, 0, 2), (2, 0, 2), (3, 0, 2), (4, 0, 1), (4, 1, 1)]
        for i, (n, j, parts) in enumerate(spots):
            start = (place_ref[0, n] * 2 + j) * part
            source = pieces[5 * k + i]
            target = w_scr.at[half, pl.ds(start, parts * part)]
            copies.append(pltpu.make_async_copy(source, target, sems.at[5 * k + i]))
    for copy in copies:
        copy.start()
    mid = mid_ref[...]
    scale = lax.rsqrt(jnp.mean(mid * mid, -1, keepdims=True) + EPS)
    hidden = (mid * scale * gain_ref[...]).astype(jnp.bfloat16)
    grad = grad_ref[...]
    gwide_scr[...] = jnp.zeros(gwide_scr.shape, gwide_scr.dtype)
    gwide_scr[:, :width] = grad
    total_scr[...] = jnp.zeros(total_scr.shape, jnp.float32)
    back_scr[...] = jnp.zeros(back_scr.shape, jnp.float32)
    spread_out[...] = jnp.dot(hidden, spread_ref[...], preferred_element_type=jnp.float32).astype(
        jnp.bfloat16
    )
    for copy in copies:
        copy.wait()
    kind = target_ref[...]
    gate_cols, up_first = gate_rt * TILE, up_rt * TILE
    for_gate = jnp.where(kind[:, :gate_cols] == 1, spread_out[:, :gate_cols].astype(jnp.float32), 0.0)
    for_gate = for_gate.astype(jnp.bfloat16)
    for_up = jnp.where(kind[:, up_first:] == 2, spread_out[:, up_first:].astype(jnp.float32), 0.0)
    for_up = for_up.astype(jnp.bfloat16)

    def gu_block(half, column, first, last):
        parts = [
            jnp.concatenate(
                [w_scr[half, r * GU_TILES + column + j] for r in range(first, last)], 0
            )
            for j in range(STEP // 128)
        ]
        return jnp.concatenate(parts, 1)

    def down_block(k, n):
        base = gu_rt * GU_TILES + n * (STEP // TILE * DOWN_TILES)
        parts = [
            jnp.concatenate([w_scr[k, base + r * DOWN_TILES + j] for r in range(STEP // TILE)], 0)
            for j in range(DOWN_TILES)
        ]
        return jnp.concatenate(parts, 1)

    def step(n, unused):
        half = n // (GU_TILES * 128 // STEP)
        column = n % (GU_TILES * 128 // STEP) * (STEP // 128)
        here = pl.ds(pl.multiple_of(n * STEP, STEP), STEP)
        w_gate = gu_block(half, column, 0, gate_rt)
        w_up = gu_block(half, column, up_rt, gu_rt)
        gate = jnp.dot(for_gate, w_gate, preferred_element_type=jnp.float32)
        up = jnp.dot(for_up, w_up, preferred_element_type=jnp.float32)
        sig = 1.0 / (1.0 + jnp.exp(-gate))
        silu = gate * sig
        slope = up * (sig + silu * (1.0 - sig))
        act = (silu * up).astype(jnp.bfloat16)
        act_ref[:, here] = act
        d_act = jnp.zeros((rows, STEP), jnp.float32)
        for k in range(2):
            w_down = down_block(k, n)
            cols = slice(k * half_out, (k + 1) * half_out)
            total_scr[:, cols] += jnp.dot(act, w_down, preferred_element_type=jnp.float32)
            d_act = d_act + contract_last(gwide_scr[:, cols], w_down)
        d_gate = (d_act * slope).astype(jnp.bfloat16)
        d_up = (d_act * silu).astype(jnp.bfloat16)
        dgate_ref[:, here] = d_gate
        dup_ref[:, here] = d_up
        back_gate = contract_last(d_gate, w_gate)
        back_up = contract_last(d_up, w_up)
        back_scr[:, :gate_cols] += jnp.where(kind[:, :gate_cols] == 1, back_gate, 0.0)
        back_scr[:, up_first:] += jnp.where(kind[:, up_first:] == 2, back_up, 0.0)
        return 0

    lax.fori_loop(0, 2 * GU_TILES * 128 // STEP, step, 0)
    out_ref[...] = (mid + total_scr[:, :width]).astype(jnp.bfloat16)
    back = back_scr[...]
    high = back.astype(jnp.bfloat16)
    low = (back - high.astype(jnp.float32)).astype(jnp.bfloat16)
    d_hidden = contract_last(high, spread_ref[...]) + contract_last(low, spread_ref[...])
    normed = mid * scale
    dgain_ref[...] = jnp.sum(d_hidden * normed, 0, keepdims=True)
    e = d_hidden * gain_ref[...]
    d_mid = grad.astype(jnp.float32) + scale * (e - normed * jnp.mean(e * normed, -1, keepdims=True))
    dmid_ref[...] = d_mid
    branch_ref[...] = d_mid.astype(jnp.bfloat16)


def feed_forward(core, middle, gain, grad, kind, spread, mine, other, gu_rt, gate_rt, up_rt):
    rows, width = middle.shape
    count = gu_rt * GU_TILES + FF // TILE * DOWN_TILES
    pieces = [a.reshape(-1, TILE, 128) for a in (*mine, *other)]
    padded = gu_rt * TILE
    vmem = pl.BlockSpec(memory_space=pltpu.VMEM)
    hbm = pl.BlockSpec(memory_space=pl.ANY)
    bf, f32 = jnp.bfloat16, jnp.float32
    shape = jax.ShapeDtypeStruct
    return pl.pallas_call(
        functools.partial(ff_kernel, gate_rt, up_rt),
        out_shape=(
            shape((rows, width), bf),
            shape((rows, padded), bf),
            shape((rows, FF), bf),
            shape((rows, FF), bf),
            shape((rows, FF), bf),
            shape((rows, width), f32),
            shape((rows, width), bf),
            shape((1, width), f32),
        ),
        in_specs=[pl.BlockSpec(memory_space=pltpu.SMEM)] + [vmem] * 5 + [hbm] * 10,
        out_specs=[vmem] * 8,
        scratch_shapes=[
            pltpu.VMEM((2, count, TILE, 128), bf),
            pltpu.VMEM((rows, 2 * DOWN_TILES * 128), f32),
            pltpu.VMEM((rows, padded), f32),
            pltpu.VMEM((rows, 2 * DOWN_TILES * 128), bf),
            pltpu.SemaphoreType.DMA((10,)),
        ],
        compiler_params=pltpu.CompilerParams(vmem_limit_bytes=40 * 2**20),
        cost_estimate=pl.CostEstimate(flops=10**6, bytes_accessed=10**5, transcendentals=0),
        name="feed_forward",
    )(
        core, middle, gain, grad, kind, spread, *pieces,
    )


def ff_terms_kernel(
    gate_rt, up_rt, half_ref, kind_ref, spread_ref, act_ref, dgate_ref, dup_ref, gwide_ref, *refs
):
    got_ref = refs[0] if len(refs) == 2 else None
    out_ref = refs[-1]
    half = half_ref[0, 0]
    gu_cols = GU_TILES * 128
    gu_here = pl.ds(pl.multiple_of(half * gu_cols, gu_cols), gu_cols)
    padded = spread_ref.shape[1]
    block = 128
    gu_total = padded // TILE * GU_TILES

    def put(terms, base):
        tiles_wide = terms.shape[1] // 128
        for r in range(terms.shape[0] // TILE):
            for ct in range(tiles_wide):
                tile = terms[r * TILE : (r + 1) * TILE, ct * 128 : (ct + 1) * 128]
                at = base + r * tiles_wide + ct
                if got_ref is not None:
                    tile = tile + got_ref[at].astype(jnp.float32)
                out_ref[at] = tile.astype(jnp.bfloat16)

    def part(j, number, d_ref):
        here = pl.ds(pl.multiple_of(j * block, block), block)
        rows_in = jnp.where(kind_ref[:, here] == number, spread_ref[:, here].astype(jnp.float32), 0.0)
        return contract_first(rows_in.astype(jnp.bfloat16), d_ref[:, gu_here])

    def base_of(j):
        return j * (block // TILE * GU_TILES)

    mixed = (gate_rt * TILE - 1) // block

    def gate_step(j, unused):
        put(part(j, 1, dgate_ref), base_of(j))
        return 0

    def up_step(j, unused):
        put(part(j, 2, dup_ref), base_of(j))
        return 0

    lax.fori_loop(0, up_rt * TILE // block, gate_step, 0)
    for j in range(up_rt * TILE // block, mixed + 1):
        put(part(j, 1, dgate_ref) + part(j, 2, dup_ref), base_of(j))
    lax.fori_loop(mixed + 1, padded // block, up_step, 0)
    down_cols = DOWN_TILES * 128
    down_here = pl.ds(pl.multiple_of(half * down_cols, down_cols), down_cols)

    def down_step(j, unused):
        here = pl.ds(pl.multiple_of(j * STEP, STEP), STEP)
        terms = contract_first(act_ref[:, here], gwide_ref[:, down_here])
        put(terms, gu_total + j * (STEP // TILE * DOWN_TILES))
        return 0

    lax.fori_loop(0, FF // STEP, down_step, 0)


def ff_terms(half, kind, spread, act, d_gate, d_up, grad_wide, gate_rt, up_rt, got=None):
    vmem = pl.BlockSpec(memory_space=pltpu.VMEM)
    count = spread.shape[1] // TILE * GU_TILES + FF // TILE * DOWN_TILES
    operands = [kind, spread, act, d_gate, d_up, grad_wide]
    if got is not None:
        operands.append(got)
    return pl.pallas_call(
        functools.partial(ff_terms_kernel, gate_rt, up_rt),
        out_shape=jax.ShapeDtypeStruct((count, TILE, 128), jnp.bfloat16),
        in_specs=[pl.BlockSpec(memory_space=pltpu.SMEM)] + [vmem] * len(operands),
        out_specs=vmem,
        compiler_params=pltpu.CompilerParams(vmem_limit_bytes=32 * 2**20),
        cost_estimate=pl.CostEstimate(flops=10**6, bytes_accessed=10**5, transcendentals=0),
        name="ff_terms",
    )(half, *operands)


BF = jnp.bfloat16
F32 = jnp.float32
LANES = 128
GU_PAD = 96
X_PAIRS = [(j, j ^ 1) for j in range(4)]
Y_PAIRS = [(j, j ^ 2) for j in range(4)]
CORE_PAIRS = [(j, j ^ 1) for j in range(8)]
EXTRA = 2


def up_pairs(first, last):
    return [(2 * z + c, 2 * z + 2 + c) for z in range(first, last) for c in range(2)]


def down_pairs(first, last):
    return [(2 * z + 2 + c, 2 * z + c) for z in range(first, last) for c in range(2)]


def swap_x(a):
    return lax.ppermute(a, "batch", X_PAIRS)


def swap_y(a):
    return lax.ppermute(a, "batch", Y_PAIRS)


def swap_core(a):
    return lax.ppermute(a, "ctx", CORE_PAIRS)


def tiles(a):
    rows, cols = a.shape
    a = a.reshape(rows // 8, 8, cols // LANES, LANES)
    return a.transpose(0, 2, 1, 3).reshape(rows * cols // (8 * LANES), 8, LANES)


def untile(a, cols):
    rows = a.shape[0] * 8 * LANES // cols
    a = a.reshape(rows // 8, cols // LANES, 8, LANES)
    return a.transpose(0, 2, 1, 3).reshape(rows, cols)


def pad_to(a, rows, cols):
    return jnp.pad(a, ((0, rows - a.shape[0]), (0, cols - a.shape[1])))


def halves_of(a):
    half = a.shape[1] // 2
    return jnp.stack([tiles(a[:, :half]), tiles(a[:, half:])])


def deep_halves_of(a):
    rows, cols = a.shape
    a = a.reshape(rows // TILE, TILE, 2, cols // (2 * LANES), LANES)
    return a.transpose(2, 0, 3, 1, 4).reshape(2, rows * cols // (2 * LANES), LANES)


def deep_whole_of(pair, cols):
    rows = pair.shape[1] * LANES * 2 // cols
    a = pair.reshape(2, rows // TILE, cols // (2 * LANES), TILE, LANES)
    return a.transpose(1, 3, 0, 2, 4).reshape(rows, cols)


def whole_of(pair, cols):
    return jnp.concatenate([untile(pair[0], cols // 2), untile(pair[1], cols // 2)], 1)


def gather_line(a, z):
    u1 = lax.ppermute(a, "ctx", up_pairs(0, 3))
    d1 = lax.ppermute(a, "ctx", down_pairs(0, 3))
    u2 = lax.ppermute(u1, "ctx", up_pairs(1, 3))
    d2 = lax.ppermute(d1, "ctx", down_pairs(0, 2))
    u3 = lax.ppermute(u2, "ctx", up_pairs(2, 3))
    d3 = lax.ppermute(d2, "ctx", down_pairs(0, 1))
    seven = jnp.stack([u3, u2, u1, a, d1, d2, d3])
    return lax.dynamic_slice_in_dim(seven, 3 - z, 4, 0)


def line_pairs(hops):
    return [(2 * z + c, 2 * (z + hops) + c) for z in range(4) for c in range(2) if 0 <= z + hops < 4]


def gather_direct(a, z):
    got = {k: lax.ppermute(a, "ctx", line_pairs(k)) for k in (1, -1, 2, -2, 3, -3)}
    seven = jnp.stack([got[3], got[2], got[1], a, got[-1], got[-2], got[-3]])
    return lax.dynamic_slice_in_dim(seven, 3 - z, 4, 0)


def scatter_direct(t, z):
    total = lax.dynamic_index_in_dim(t, z, 0, keepdims=False).astype(F32)
    for k in (3, -3, 2, -2, 1, -1):
        block = lax.dynamic_index_in_dim(t, jnp.clip(z + k, 0, 3), 0, keepdims=False)
        got = lax.ppermute(block, "ctx", line_pairs(k)).astype(F32)
        total = total + jnp.where((z - k >= 0) & (z - k < 4), got, 0.0)
    return total


def gather_near(a):
    return swap_x(a), swap_y(a)


def gather_far(from_x, from_y):
    return swap_y(from_x[:2]), swap_x(from_y[2:])


def place(pieces, b, start, stop):
    shape = pieces[0][2].shape
    whole = jnp.zeros((4, 4, shape[1], stop - start) + shape[3:], BF)
    for step, row, piece in pieces:
        whole = lax.dynamic_update_slice(
            whole, piece[None, :, :, start:stop], (b ^ step, row) + (0,) * (len(shape) - 1)
        )
    return whole


def add(*terms):
    total = terms[0].astype(F32)
    for term in terms[1:]:
        total = total + term.astype(F32)
    return total.astype(BF)


def scatter_blocks(g, b):
    return [lax.dynamic_index_in_dim(g, b ^ k, 0, keepdims=False) for k in range(4)]


def scatter_far(blocks):
    return swap_x(blocks[3][:2]), swap_y(blocks[3][2:])


def scatter_near(blocks, far_x, far_y):
    xs, ys = blocks[1], blocks[2]
    return (
        swap_x(jnp.concatenate([xs[:2], add(xs[2:], far_y)], 0)),
        swap_y(jnp.concatenate([add(ys[:2], far_x), ys[2:]], 0)),
    )


def scatter_steps(t, z):
    def block(k):
        return lax.dynamic_index_in_dim(t, jnp.clip(z + k, 0, 3), 0, keepdims=False)

    up = down = None
    for k in (3, 2, 1):
        up_block, down_block = block(k), block(-k)
        if k < 3:
            up_block, down_block = add(up_block, up), add(down_block, down)
        up = lax.ppermute(up_block, "ctx", up_pairs(0, 4 - k))
        down = lax.ppermute(down_block, "ctx", down_pairs(k - 1, 3))
        up, down = yield up, down
        up = jnp.where((z > 0) & (z <= 4 - k), up, 0)
        down = jnp.where((z >= k - 1) & (z < 3), down, 0)
    yield block(0).astype(F32) + up.astype(F32) + down.astype(F32)


def split_high(a, parts):
    out = []
    for unused in range(parts):
        high = lax.reduce_precision(a, 8, 7)
        out.append(high.astype(BF))
        a = a - high
    return out


def local_block(tokens, attention_weights, feedforward_weights, norm_gains, span_order, cotangent):
    rows_here = tokens.shape[1]
    halves = rows_here // 2
    width_q = HEADS * HEAD_DIM
    width_kv = KV_HEADS * HEAD_DIM
    wide = 2 * 512
    b = lax.axis_index("batch")
    place_ctx = lax.axis_index("ctx")
    z = place_ctx // 2
    c = place_ctx % 2
    device = b * 8 + place_ctx
    own_gain = D // 8

    def pick(first, second):
        return jnp.where(c == 0, first, second)

    def merge(mine, other):
        return pick(
            jnp.concatenate([mine, other], -1), jnp.concatenate([other, mine], -1)
        )

    def half_of(a, k):
        half = a.shape[-1] // 2
        return jnp.where((c ^ k) == 0, a[..., :half], a[..., half:])

    def pair_up(shard):
        mine = pick(shard[0], shard[1])
        other = swap_core(pick(shard[1], shard[0]))
        return pick(jnp.stack([mine, other]), jnp.stack([other, mine]))

    att_rows = attention_weights.shape[0] // D
    att_shard = halves_of(pad_to(attention_weights.reshape(att_rows, D), att_rows, wide))
    gain_parts = jnp.stack(split_high(norm_gains, 3), 1)
    gain_rows = jnp.pad(gain_parts, ((0, 0), (0, 8 * EXTRA - 3), (0, LANES - own_gain)))
    gain_rows = gain_rows.reshape(2, EXTRA, 8, LANES)
    att_chip = pair_up(jnp.concatenate([att_shard, gain_rows], 1))
    att_line = gather_direct(att_chip, z)

    gu_rows = feedforward_weights.shape[0] // FF
    down_rows = feedforward_weights.shape[0] // D
    mixed = 2 * D // gu_rows
    rest = 2 * D - mixed * gu_rows
    rest_pad = -(-rest // TILE) * TILE
    gu_shard = deep_halves_of(pad_to(feedforward_weights.reshape(gu_rows, FF), GU_PAD, FF))
    down_shard = deep_halves_of(pad_to(feedforward_weights.reshape(down_rows, D), down_rows, wide))
    mixed_down = pad_to(
        feedforward_weights[rest * FF :].reshape(-1, D), down_rows - rest * FF // D, wide
    )
    mixed_shard = jnp.concatenate(
        [
            deep_halves_of(
                pad_to(feedforward_weights[: rest * FF].reshape(rest, FF), rest_pad, FF)
            ),
            deep_halves_of(mixed_down),
        ],
        1,
    )
    ff_shard = jnp.where(device < mixed, gu_shard, jnp.where(device == mixed, mixed_shard, down_shard))
    ff_body = ff_shard.shape[1]
    ff_chip, att_line = lax.optimization_barrier((pair_up(ff_shard), att_line))
    ff_line = gather_line(ff_chip, z)
    ff_line_other = swap_core(ff_line)

    att_x, att_y = gather_near(att_line)
    att_first, att_second = gather_far(att_x, att_y)
    att_pieces = (
        (0, 0, att_line), (1, 0, att_x), (2, 0, att_y), (3, 0, att_first), (3, 2, att_second)
    )
    att_body = att_rows * wide // (2 * 8 * LANES)
    att_mine = place(att_pieces, b, 0, att_body).reshape(-1, 8, LANES)
    gain_mine = place(att_pieces, b, att_body, att_body + EXTRA)
    att_other = swap_core(att_mine)
    gain_other = swap_core(gain_mine)

    def gain_from(a):
        parts = a[0, :, :, 0, :3, :own_gain].astype(F32)
        return (parts[:, :, 0] + parts[:, :, 1] + parts[:, :, 2]).reshape(D)

    gain_m, gain_o = gain_from(gain_mine), gain_from(gain_other)
    gain_full = jnp.stack([pick(gain_m, gain_o), pick(gain_o, gain_m)])

    gu_total = mixed * GU_PAD + rest_pad

    pad_row = jnp.arange(gu_total, dtype=jnp.int32)
    true_row = pad_row // GU_PAD * gu_rows + pad_row % GU_PAD
    real = pad_row % GU_PAD < gu_rows
    is_gate = real & (true_row < D)
    is_up = real & (true_row >= D)
    spread = ((true_row % D)[None, :] == jnp.arange(D, dtype=jnp.int32)[:, None]) & real[None, :]
    spread = spread.astype(BF)
    third = D // 3
    order3 = jnp.arange(D, dtype=jnp.int32)
    perm3 = (order3[:, None] == (order3 % third * 3 + order3 // third)[None, :]).astype(BF)

    offsets = jnp.arange(halves, dtype=jnp.int32)
    query_pos = (span_order[0][:, None] * halves + offsets[None, :]).reshape(rows_here)
    cos_table, sin_table = rope_tables(query_pos)

    inputs = tokens[0].astype(F32)
    hidden_f, norm_one_pull = jax.vjp(normalize, inputs, gain_full[0])
    hidden = hidden_f.astype(BF)
    hidden3 = jnp.dot(hidden, perm3, preferred_element_type=F32).astype(BF)
    hidden3 = hidden3.reshape(rows_here, 3, third)
    att_m, att_o = untile(att_mine, wide // 2), untile(att_other, wide // 2)
    cut_k, cut_v, cut_o = D, D + third, D + 2 * third

    def project(a, start, stop):
        return merge(
            jnp.dot(a, att_m[start:stop], preferred_element_type=F32),
            jnp.dot(a, att_o[start:stop], preferred_element_type=F32),
        )

    def thirds(start, stop):
        out = project(hidden3.transpose(1, 0, 2).reshape(3 * rows_here, third), start, stop)
        out = out.reshape(3, rows_here, wide)
        return out[0, :, :third] + out[1, :, third : 2 * third] + out[2, :, 2 * third : 3 * third]

    query_raw = project(hidden, 0, D)[:, :width_q].reshape(rows_here, HEADS, HEAD_DIM)
    key_raw = thirds(cut_k, cut_v).reshape(rows_here, KV_HEADS, HEAD_DIM)
    values = thirds(cut_v, cut_o).astype(BF)
    query_rot, query_pull = jax.vjp(lambda a: rotate(a, cos_table, sin_table), query_raw)
    key_rot, key_pull = jax.vjp(lambda a: rotate(a, cos_table, sin_table), key_raw)
    queries = query_rot.astype(BF).reshape(rows_here, width_q)
    keys = key_rot.astype(BF).reshape(rows_here, width_kv)

    span_rows = jnp.pad(span_order.astype(BF), ((0, 15), (0, 2 * width_kv - 2)))
    key_value = jnp.concatenate([jnp.concatenate([keys, values], 1), span_rows], 0)
    ff_near = gather_near(ff_line)
    line_mine = gather_direct(key_value, z)
    ff_near, line_mine = lax.optimization_barrier((ff_near, line_mine))
    line_other = swap_core(line_mine)
    ff_far = gather_far(*ff_near)
    spans = jnp.stack([line_mine[:, rows_here, :2], line_other[:, rows_here, :2]]).astype(jnp.int32)
    spans = jnp.concatenate([spans, jnp.broadcast_to(span_order[None], (2, 1, 2))], 1)
    attended, log_total = attend(spans, queries, line_mine, line_other)
    ff_far, attended = lax.optimization_barrier((ff_far, attended))
    ff_mine = (ff_line, *ff_near, *ff_far)
    ff_other = (ff_line_other, *(swap_core(piece) for piece in ff_mine[1:]))
    attended_low = attended.astype(BF)
    middle = inputs + project(attended_low, cut_o, cut_o + D)[:, :D]
    gate_end = -(-D // gu_rows) * GU_PAD
    up_start = D // gu_rows * GU_PAD
    grad_wide = jnp.pad(cotangent[0], ((0, 0), (0, wide - D)))
    kind = (is_gate.astype(jnp.int32) + 2 * is_up.astype(jnp.int32))[None]
    result, spread_two, activ, grad_gate, grad_upward, grad_middle, grad_branch, grad_gain_two = (
        feed_forward(
            jnp.stack([c, b, b ^ 1, b ^ 2, b ^ 3])[None], middle, gain_full[1:2], cotangent[0], kind, spread,
            ff_mine, ff_other,
            gu_total // TILE, gate_end // TILE, up_start // TILE,
        )
    )
    grad_gain_two = grad_gain_two[0]

    def times_transposed(a, w):
        return lax.dot_general(a, w, (((1,), (1,)), ((), ())), preferred_element_type=F32)

    def transposed_times(a, w):
        return lax.dot_general(a, w, (((0,), (0,)), ((), ())), preferred_element_type=F32)

    def terms_of_half(half, got=None):
        return ff_terms(
            half.reshape(1, 1), kind, spread_two, activ, grad_gate, grad_upward, grad_wide,
            gate_end // TILE, up_start // TILE, got,
        )

    ff_send, grad_branch = lax.optimization_barrier((terms_of_half(1 - c), grad_branch))
    ff_from = swap_core(ff_send)
    branch_wide = jnp.pad(grad_branch, ((0, 0), (0, wide - D)))

    def project_back(a, start, stop):
        return times_transposed(half_of(a, 0), att_m[start:stop]) + times_transposed(
            half_of(a, 1), att_o[start:stop]
        )

    grad_attended = project_back(branch_wide, cut_o, cut_o + D).astype(BF)
    ff_sum, grad_attended = lax.optimization_barrier((terms_of_half(c, ff_from), grad_attended))
    ff_blocks = scatter_blocks(ff_sum.reshape(4, 4, 2, ff_body, LANES), b)
    ff_far = scatter_far(ff_blocks)
    grad_query_rot, both_mine, both_other = attend_back(
        spans, queries, line_mine, line_other, attended, log_total, grad_attended
    )
    ff_far, both_other = lax.optimization_barrier((ff_far, both_other))
    both_from = swap_core(both_other)
    ff_near = scatter_near(ff_blocks, *ff_far)
    both_own = scatter_direct(add(both_mine, both_from), z)
    ff_near, both_own = lax.optimization_barrier((ff_near, both_own))
    ff_steps = scatter_steps(add(ff_blocks[0], *ff_near), z)
    ff_step = next(ff_steps)
    grad_key_rot, grad_value_f = both_own[:, :width_kv], both_own[:, width_kv:]
    grad_query_raw = query_pull(grad_query_rot.reshape(rows_here, HEADS, HEAD_DIM))[0]
    grad_key_raw = key_pull(grad_key_rot.reshape(rows_here, KV_HEADS, HEAD_DIM))[0]
    grad_query = grad_query_raw.reshape(rows_here, width_q).astype(BF)
    grad_key = grad_key_raw.reshape(rows_here, width_kv).astype(BF)
    grad_value = grad_value_f.astype(BF)

    def spots(a):
        return jnp.concatenate(
            [jnp.pad(a, ((0, 0), (q * third, wide - (q + 1) * third))) for q in range(3)], 0
        )

    query_wide = jnp.pad(grad_query, ((0, 0), (0, wide - D)))
    key_spots, value_spots = spots(grad_key), spots(grad_value)
    hidden_rows = hidden3.transpose(1, 0, 2).reshape(3 * rows_here, third)
    back_three = project_back(key_spots, cut_k, cut_v) + project_back(value_spots, cut_v, cut_o)
    back_three = back_three.reshape(3, rows_here, third).transpose(1, 0, 2).reshape(rows_here, D)
    grad_hidden = project_back(query_wide, 0, D) + times_transposed(
        jnp.concatenate(split_high(back_three, 2), 1), jnp.concatenate([perm3, perm3], 1)
    )
    grad_inputs_norm, grad_gain_one = norm_one_pull(grad_hidden)
    grad_inputs = grad_middle + grad_inputs_norm

    gain_terms = jnp.stack([grad_gain_one, grad_gain_two]).reshape(2, 8, own_gain)
    gain_terms = jnp.pad(
        jnp.stack(split_high(gain_terms, 2), 2),
        ((0, 0), (0, 0), (0, 8 * EXTRA - 2), (0, LANES - own_gain)),
    ).reshape(2, 4, 2, EXTRA, 8, LANES)

    def att_terms(k):
        terms = jnp.concatenate(
            [
                transposed_times(hidden, half_of(query_wide, k)).astype(BF),
                transposed_times(hidden_rows, half_of(key_spots, k)).astype(BF),
                transposed_times(hidden_rows, half_of(value_spots, k)).astype(BF),
                transposed_times(attended_low, half_of(branch_wide, k)).astype(BF),
            ],
            0,
        )
        gain = jnp.where((c ^ k) == 0, gain_terms[0], gain_terms[1])
        gain = jnp.broadcast_to(gain[None], (4, 4, 2, EXTRA, 8, LANES))
        return jnp.concatenate([tiles(terms).reshape(4, 4, 2, att_body, 8, LANES), gain], 3)

    ff_step, att_send = lax.optimization_barrier((ff_step, att_terms(1)))
    ff_step = ff_steps.send(ff_step)
    att_from = swap_core(att_send)
    att_blocks = scatter_blocks(add(att_terms(0), att_from), b)
    ff_step, att_blocks = lax.optimization_barrier((ff_step, att_blocks))
    ff_step = ff_steps.send(ff_step)
    att_far = scatter_far(att_blocks)
    ff_step, att_far = lax.optimization_barrier((ff_step, att_far))
    ff_own = ff_steps.send(ff_step)
    att_near = scatter_near(att_blocks, *att_far)
    att_own = scatter_direct(add(att_blocks[0], *att_near), z)

    def settle(own):
        mine = pick(own[0], own[1])
        other = swap_core(pick(own[1], own[0]))
        return pick(jnp.stack([mine, other]), jnp.stack([other, mine]))

    ff_done = settle(ff_own)
    att_done = settle(att_own)
    gain_own = att_done[:, att_body, 0, :own_gain] + att_done[:, att_body, 1, :own_gain]
    att_flat = whole_of(att_done[:, :att_body], wide)[:, :D].reshape(-1)
    gu_flat = deep_whole_of(ff_done, FF)[:gu_rows].reshape(-1)
    down_flat = deep_whole_of(ff_done, wide)[:, :D].reshape(-1)
    cut = rest_pad * FF // (2 * LANES)
    mixed_flat = jnp.concatenate(
        [
            deep_whole_of(ff_done[:, :cut], FF)[:rest].reshape(-1),
            deep_whole_of(ff_done[:, cut:], wide)[:, :D].reshape(-1),
        ]
    )
    ff_flat = jnp.where(device < mixed, gu_flat, jnp.where(device == mixed, mixed_flat, down_flat))
    return (
        result[None],
        grad_inputs[None],
        att_flat,
        ff_flat,
        gain_own,
    )


def solution(mesh):
    fits = mesh.shape["batch"] == 4 and mesh.shape["ctx"] == 8
    local = local_block if fits else local_any
    placed = (
        P("batch", "ctx", None),
        P(("batch", "ctx")),
        P(("batch", "ctx")),
        P(None, "ctx"),
        P("batch", "ctx"),
        P("batch", "ctx", None),
    )
    return jax.shard_map(
        local,
        mesh=mesh,
        in_specs=placed,
        out_specs=(
            P("batch", "ctx", None),
            P("batch", "ctx", None),
            P(("batch", "ctx")),
            P(("batch", "ctx")),
            P(None, "ctx"),
        ),
        check_vma=False,
    )
```

```python
import functools
import math

import jax
import jax.numpy as jnp
from jax import lax
from jax.experimental import pallas as pl
from jax.experimental.pallas import tpu as pltpu
from jax.sharding import PartitionSpec as P

D = 960
HEADS = 15
KV_HEADS = 5
HEAD_DIM = 64
FF = 2560


ROPE_BASE = 100000.0
EPS = 1e-05
NEG = -1e30


def normalize(values, gain):
    return values * lax.rsqrt(jnp.mean(values * values, -1, keepdims=True) + EPS) * gain


def swiglu(gate, upward):
    return jax.nn.silu(gate) * upward


def rope_tables(positions):
    halves = HEAD_DIM // 2
    inverse_freq = ROPE_BASE ** (-jnp.arange(halves, dtype=jnp.float32) / halves)
    angles = positions.astype(jnp.float32)[:, None] * inverse_freq[None, :]
    return (jnp.cos(angles), jnp.sin(angles))


def rotate(values, cos_table, sin_table):
    halves = HEAD_DIM // 2
    first = values[..., :halves]
    second = values[..., halves:]
    cos_table = cos_table[:, None, :]
    sin_table = sin_table[:, None, :]
    return jnp.concatenate(
        [first * cos_table - second * sin_table, second * cos_table + first * sin_table], -1
    )


def split_flat(flat, shapes):
    pieces = []
    offset = 0
    for rows_in, cols_in in shapes:
        pieces.append(flat[offset : offset + rows_in * cols_in].reshape(rows_in, cols_in))
        offset += rows_in * cols_in
    return pieces


def unpack(att_flat, ff_flat):
    width_q = HEADS * HEAD_DIM
    width_kv = KV_HEADS * HEAD_DIM
    att_parts = split_flat(att_flat, [(D, width_q), (D, width_kv), (D, width_kv), (width_q, D)])
    ff_parts = split_flat(ff_flat, [(D, FF), (D, FF), (FF, D)])
    return (att_parts, ff_parts)


def score_block(queries, key_block, query_pos, key_pos):
    keys_three = key_block.reshape(key_block.shape[0], KV_HEADS, HEAD_DIM)
    scores = jnp.einsum(
        "qhgd,khd->hgqk", queries, keys_three, preferred_element_type=jnp.float32
    ) * HEAD_DIM ** (-0.5)
    visible = key_pos[None, None, None, :] <= query_pos[None, None, :, None]
    return (scores, visible)


def attention_forward(queries, key_all, value_all, query_pos, key_pos, block):
    rows_here = queries.shape[0]
    group = HEADS // KV_HEADS
    count = key_all.shape[0] // block
    key_blocks = key_all.reshape(count, block, key_all.shape[1])
    value_blocks = value_all.reshape(count, block, value_all.shape[1])
    pos_blocks = key_pos.reshape(count, block)

    def online_step(carry, item):
        top, total, accum = carry
        key_block, value_block, pos_block = item
        scores, visible = score_block(queries, key_block, query_pos, pos_block)
        scores = jnp.where(visible, scores, NEG)
        new_top = jnp.maximum(top, jnp.max(scores, -1))
        weights = jnp.where(visible, jnp.exp(scores - new_top[..., None]), 0.0)
        factor = jnp.exp(top - new_top)
        total = total * factor + jnp.sum(weights, -1)
        values_three = value_block.reshape(block, KV_HEADS, HEAD_DIM)
        accum = accum * jnp.transpose(factor, (2, 0, 1))[..., None]
        accum = accum + jnp.einsum(
            "hgqk,khd->qhgd",
            weights.astype(jnp.bfloat16),
            values_three,
            preferred_element_type=jnp.float32,
        )
        return ((new_top, total, accum), None)

    start_top = jnp.full((KV_HEADS, group, rows_here), NEG, jnp.float32)
    start_total = jnp.zeros((KV_HEADS, group, rows_here), jnp.float32)
    start_out = jnp.zeros((rows_here, KV_HEADS, group, HEAD_DIM), jnp.float32)
    (top, total, accum), unused = lax.scan(
        online_step, (start_top, start_total, start_out), (key_blocks, value_blocks, pos_blocks)
    )
    log_total = top + jnp.log(total)
    attended = accum / jnp.transpose(total, (2, 0, 1))[..., None]
    return (attended, log_total)


def attention_backward(
    queries, key_all, value_all, query_pos, key_pos, block, log_total, grad_out, attended
):
    rows_here = queries.shape[0]
    group = HEADS // KV_HEADS
    width_kv = key_all.shape[1]
    count = key_all.shape[0] // block
    items = (
        key_all.reshape(count, block, width_kv),
        value_all.reshape(count, block, width_kv),
        key_pos.reshape(count, block),
    )
    delta = jnp.transpose(jnp.sum(grad_out.astype(jnp.float32) * attended, -1), (1, 2, 0))

    def grad_step(grad_query, item):
        key_block, value_block, pos_block = item
        scores, visible = score_block(queries, key_block, query_pos, pos_block)
        probs = jnp.where(visible, jnp.exp(scores - log_total[..., None]), 0.0)
        values_three = value_block.reshape(block, KV_HEADS, HEAD_DIM)
        grad_probs = jnp.einsum(
            "qhgd,khd->hgqk", grad_out, values_three, preferred_element_type=jnp.float32
        )
        grad_scores = (probs * (grad_probs - delta[..., None])).astype(jnp.bfloat16)
        keys_three = key_block.reshape(block, KV_HEADS, HEAD_DIM)
        grad_query = grad_query + jnp.einsum(
            "hgqk,khd->qhgd", grad_scores, keys_three, preferred_element_type=jnp.float32
        )
        grad_key = jnp.einsum(
            "hgqk,qhgd->khd", grad_scores, queries, preferred_element_type=jnp.float32
        )
        grad_value = jnp.einsum(
            "hgqk,qhgd->khd",
            probs.astype(jnp.bfloat16),
            grad_out,
            preferred_element_type=jnp.float32,
        )
        return (
            grad_query,
            (grad_key.reshape(block, width_kv), grad_value.reshape(block, width_kv)),
        )

    start_query = jnp.zeros((rows_here, KV_HEADS, group, HEAD_DIM), jnp.float32)
    grad_query, (grad_keys, grad_values) = lax.scan(grad_step, start_query, items)
    return (
        grad_query,
        grad_keys.reshape(count * block, width_kv),
        grad_values.reshape(count * block, width_kv),
    )


def local_any(tokens, attention_weights, feedforward_weights, norm_gains, span_order, cotangent):
    ctx_count = lax.axis_size("ctx")
    batch_count = lax.axis_size("batch")
    rows_here = tokens.shape[1]
    halves = rows_here // 2
    length = rows_here * ctx_count
    group = HEADS // KV_HEADS
    width_q = HEADS * HEAD_DIM
    width_kv = KV_HEADS * HEAD_DIM
    block = math.gcd(length, 512)
    scaling = HEAD_DIM ** (-0.5)
    att_full, ff_full = (
        lax.all_gather(attention_weights, ("batch", "ctx"), axis=0, tiled=True),
        lax.all_gather(feedforward_weights, ("batch", "ctx"), axis=0, tiled=True),
    )
    gain_full = lax.all_gather(norm_gains, "ctx", axis=1, tiled=True)
    order_full = lax.all_gather(span_order, "ctx", axis=1, tiled=True)
    offsets = jnp.arange(halves, dtype=jnp.int32)
    key_pos = (order_full[0][:, None] * halves + offsets[None, :]).reshape(length)
    query_pos = (span_order[0][:, None] * halves + offsets[None, :]).reshape(rows_here)
    cos_table, sin_table = rope_tables(query_pos)
    (w_query, w_key, w_value, w_out), (w_gate, w_up, w_down) = unpack(att_full, ff_full)
    inputs = tokens[0].astype(jnp.float32)
    hidden_f, norm_one_pull = jax.vjp(normalize, inputs, gain_full[0])
    hidden = hidden_f.astype(jnp.bfloat16)
    query_raw = jnp.dot(hidden, w_query, preferred_element_type=jnp.float32).reshape(
        rows_here, HEADS, HEAD_DIM
    )
    key_raw = jnp.dot(hidden, w_key, preferred_element_type=jnp.float32).reshape(
        rows_here, KV_HEADS, HEAD_DIM
    )
    values = jnp.dot(hidden, w_value, preferred_element_type=jnp.float32).astype(jnp.bfloat16)
    query_rot, query_pull = jax.vjp(lambda a: rotate(a, cos_table, sin_table), query_raw)
    key_rot, key_pull = jax.vjp(lambda a: rotate(a, cos_table, sin_table), key_raw)
    queries = query_rot.astype(jnp.bfloat16).reshape(rows_here, KV_HEADS, group, HEAD_DIM)
    keys = key_rot.astype(jnp.bfloat16).reshape(rows_here, width_kv)
    key_all, value_all = (
        lax.all_gather(keys, "ctx", axis=0, tiled=True),
        lax.all_gather(values, "ctx", axis=0, tiled=True),
    )
    attended, log_total = attention_forward(queries, key_all, value_all, query_pos, key_pos, block)
    attended_low = attended.reshape(rows_here, width_q).astype(jnp.bfloat16)
    middle = inputs + jnp.dot(attended_low, w_out, preferred_element_type=jnp.float32)
    hidden_two_f, norm_two_pull = jax.vjp(normalize, middle, gain_full[1])
    hidden_two = hidden_two_f.astype(jnp.bfloat16)
    gate = jnp.dot(hidden_two, w_gate, preferred_element_type=jnp.float32)
    upward = jnp.dot(hidden_two, w_up, preferred_element_type=jnp.float32)
    activ_f, swiglu_pull = jax.vjp(swiglu, gate, upward)
    activ = activ_f.astype(jnp.bfloat16)
    result = middle + jnp.dot(activ, w_down, preferred_element_type=jnp.float32)
    grad_result = cotangent[0]
    grad_down = jnp.einsum("tf,td->fd", activ, grad_result, preferred_element_type=jnp.float32)
    grad_activ = jnp.einsum("td,fd->tf", grad_result, w_down, preferred_element_type=jnp.float32)
    grad_gate_f, grad_up_f = swiglu_pull(grad_activ)
    grad_gate = grad_gate_f.astype(jnp.bfloat16)
    grad_upward = grad_up_f.astype(jnp.bfloat16)
    grad_w_gate = jnp.einsum("td,tf->df", hidden_two, grad_gate, preferred_element_type=jnp.float32)
    grad_w_up = jnp.einsum("td,tf->df", hidden_two, grad_upward, preferred_element_type=jnp.float32)
    grad_hidden_two = jnp.einsum("tf,df->td", grad_gate, w_gate, preferred_element_type=jnp.float32)
    grad_hidden_two = grad_hidden_two + jnp.einsum(
        "tf,df->td", grad_upward, w_up, preferred_element_type=jnp.float32
    )
    grad_middle_norm, grad_gain_two = norm_two_pull(grad_hidden_two)
    grad_middle = grad_result.astype(jnp.float32) + grad_middle_norm
    grad_branch = grad_middle.astype(jnp.bfloat16)
    grad_w_out = jnp.einsum(
        "tq,td->qd", attended_low, grad_branch, preferred_element_type=jnp.float32
    )
    grad_attended = jnp.einsum(
        "td,qd->tq", grad_branch, w_out, preferred_element_type=jnp.float32
    ).astype(jnp.bfloat16)
    grad_attended = grad_attended.reshape(rows_here, KV_HEADS, group, HEAD_DIM)
    grad_query_rot, grad_key_all, grad_value_all = attention_backward(
        queries, key_all, value_all, query_pos, key_pos, block, log_total, grad_attended, attended
    )
    grad_key_rot, grad_value_f = (
        lax.psum_scatter(
            grad_key_all.astype(jnp.bfloat16), "ctx", scatter_dimension=0, tiled=True
        ).astype(jnp.float32),
        lax.psum_scatter(
            grad_value_all.astype(jnp.bfloat16), "ctx", scatter_dimension=0, tiled=True
        ).astype(jnp.float32),
    )
    grad_query_raw = query_pull(grad_query_rot.reshape(rows_here, HEADS, HEAD_DIM) * scaling)[0]
    grad_key_raw = key_pull(grad_key_rot.reshape(rows_here, KV_HEADS, HEAD_DIM) * scaling)[0]
    grad_query = grad_query_raw.reshape(rows_here, width_q).astype(jnp.bfloat16)
    grad_key = grad_key_raw.reshape(rows_here, width_kv).astype(jnp.bfloat16)
    grad_value = grad_value_f.astype(jnp.bfloat16)
    grad_w_query = jnp.einsum("td,tq->dq", hidden, grad_query, preferred_element_type=jnp.float32)
    grad_w_key = jnp.einsum("td,tq->dq", hidden, grad_key, preferred_element_type=jnp.float32)
    grad_w_value = jnp.einsum("td,tq->dq", hidden, grad_value, preferred_element_type=jnp.float32)
    grad_hidden = jnp.einsum("tq,dq->td", grad_query, w_query, preferred_element_type=jnp.float32)
    grad_hidden = grad_hidden + jnp.einsum(
        "tq,dq->td", grad_key, w_key, preferred_element_type=jnp.float32
    )
    grad_hidden = grad_hidden + jnp.einsum(
        "tq,dq->td", grad_value, w_value, preferred_element_type=jnp.float32
    )
    grad_inputs_norm, grad_gain_one = norm_one_pull(grad_hidden)
    grad_inputs = grad_middle + grad_inputs_norm
    grad_att_flat = jnp.concatenate(
        [
            grad_w_query.reshape(-1),
            grad_w_key.reshape(-1),
            grad_w_value.reshape(-1),
            grad_w_out.reshape(-1),
        ]
    )
    grad_ff_flat = jnp.concatenate(
        [grad_w_gate.reshape(-1), grad_w_up.reshape(-1), grad_down.reshape(-1)]
    )
    width_own = D // ctx_count
    gain_terms = jnp.stack([grad_gain_one, grad_gain_two]).reshape(2, ctx_count, width_own)
    gain_terms = jnp.transpose(gain_terms, (1, 0, 2)).reshape(ctx_count, 2 * width_own)
    gain_terms = jnp.broadcast_to(
        gain_terms[None], (batch_count, ctx_count, 2 * width_own)
    ).reshape(batch_count * ctx_count, 2 * width_own)
    att_part, ff_part, gain_part = (
        lax.psum_scatter(
            grad_att_flat.astype(jnp.bfloat16), "batch", scatter_dimension=0, tiled=True
        ).astype(jnp.float32),
        lax.psum_scatter(
            grad_ff_flat.astype(jnp.bfloat16), "batch", scatter_dimension=0, tiled=True
        ).astype(jnp.float32),
        lax.psum_scatter(
            gain_terms.astype(jnp.bfloat16), "batch", scatter_dimension=0, tiled=True
        ).astype(jnp.float32),
    )
    grad_att_own, grad_ff_own, gain_own = (
        lax.psum_scatter(
            att_part.astype(jnp.bfloat16), "ctx", scatter_dimension=0, tiled=True
        ).astype(jnp.float32),
        lax.psum_scatter(
            ff_part.astype(jnp.bfloat16), "ctx", scatter_dimension=0, tiled=True
        ).astype(jnp.float32),
        lax.psum_scatter(
            gain_part.astype(jnp.bfloat16), "ctx", scatter_dimension=0, tiled=True
        ).astype(jnp.float32),
    )
    grad_gain_own = gain_own.reshape(2, width_own)
    return (
        result.astype(jnp.bfloat16)[None],
        grad_inputs[None],
        grad_att_own,
        grad_ff_own,
        grad_gain_own,
    )


CHUNK = 4


def sort_rows(spans_ref, own_ref, other_ref, sorted_ref, span):
    for m, ref in enumerate((own_ref, other_ref)):
        for z in range(4):
            for j in range(2):
                start = pl.multiple_of(spans_ref[m, z, j] * span, span)
                sorted_ref[pl.ds(start, span), :] = ref[z, j * span : (j + 1) * span, :]


def group_rows(ref, part, span, head):
    group = HEADS // KV_HEADS
    rows = ref[part * span : (part + 1) * span, :]
    columns = [
        rows[:, (head * group + j) * HEAD_DIM : (head * group + j + 1) * HEAD_DIM]
        for j in range(group)
    ]
    return jnp.concatenate(columns, 0)


def seen(position, step, span, rows, cols):
    row = lax.broadcasted_iota(jnp.int32, (rows, cols), 0) % span
    col = lax.broadcasted_iota(jnp.int32, (rows, cols), 1)
    return col + step * cols <= row + position * span


def attend_kernel(
    spans_ref, q_ref, own_ref, other_ref, out_ref, lse_ref, sorted_ref, q_scr, top_ref, sum_ref, acc_ref
):
    group = HEADS // KV_HEADS
    span = q_ref.shape[0] // 2
    width_kv = KV_HEADS * HEAD_DIM
    rows, cols = group * span, CHUNK * span
    sort_rows(spans_ref, own_ref, other_ref, sorted_ref, span)
    for part in range(2):
        position = spans_ref[0, 4, part]
        for g in range(KV_HEADS):
            q_scr[g] = group_rows(q_ref, part, span, g) * jnp.bfloat16(HEAD_DIM**-0.5)
        top_ref[...] = jnp.full(top_ref.shape, NEG, jnp.float32)
        sum_ref[...] = jnp.zeros(sum_ref.shape, jnp.float32)
        acc_ref[...] = jnp.zeros(acc_ref.shape, jnp.float32)

        def step(i, unused):
            visible = seen(position, i, span, rows, cols)
            base = pl.multiple_of(i * cols, cols)
            for g in range(KV_HEADS):
                k = sorted_ref[pl.ds(base, cols), g * HEAD_DIM : (g + 1) * HEAD_DIM]
                v = sorted_ref[
                    pl.ds(base, cols), width_kv + g * HEAD_DIM : width_kv + (g + 1) * HEAD_DIM
                ]
                s = lax.dot_general(
                    q_scr[g], k, (((1,), (1,)), ((), ())), preferred_element_type=jnp.float32
                )
                s = jnp.where(visible, s, NEG)
                old = top_ref[g]
                top = jnp.maximum(old, jnp.max(s, 1, keepdims=True))
                weights = jnp.where(visible, jnp.exp(s - top), 0.0)
                factor = jnp.exp(old - top)
                top_ref[g] = top
                sum_ref[g] = sum_ref[g] * factor + jnp.sum(weights, 1, keepdims=True)
                acc_ref[g] = acc_ref[g] * factor + jnp.dot(
                    weights.astype(jnp.bfloat16), v, preferred_element_type=jnp.float32
                )
            return 0

        lax.fori_loop(0, (position + CHUNK) // CHUNK, step, 0)
        for g in range(KV_HEADS):
            out = acc_ref[g] / sum_ref[g]
            lse_ref[part * KV_HEADS + g] = top_ref[g] + jnp.log(sum_ref[g])
            for j in range(group):
                h = g * group + j
                out_ref[part * span : (part + 1) * span, h * HEAD_DIM : (h + 1) * HEAD_DIM] = out[
                    j * span : (j + 1) * span
                ]


def attend(spans, queries, own, other):
    rows, width = queries.shape
    group = HEADS // KV_HEADS
    stacked = group * rows // 2
    vmem = pl.BlockSpec(memory_space=pltpu.VMEM)
    return pl.pallas_call(
        attend_kernel,
        out_shape=(
            jax.ShapeDtypeStruct((rows, width), jnp.float32),
            jax.ShapeDtypeStruct((2 * KV_HEADS, stacked, 1), jnp.float32),
        ),
        in_specs=[pl.BlockSpec(memory_space=pltpu.SMEM), vmem, vmem, vmem],
        out_specs=(vmem, vmem),
        scratch_shapes=[
            pltpu.VMEM((8 * rows, own.shape[2]), jnp.bfloat16),
            pltpu.VMEM((KV_HEADS, stacked, HEAD_DIM), jnp.bfloat16),
            pltpu.VMEM((KV_HEADS, stacked, 1), jnp.float32),
            pltpu.VMEM((KV_HEADS, stacked, 1), jnp.float32),
            pltpu.VMEM((KV_HEADS, stacked, HEAD_DIM), jnp.float32),
        ],
        compiler_params=pltpu.CompilerParams(vmem_limit_bytes=24 * 2**20),
        cost_estimate=pl.CostEstimate(flops=10**6, bytes_accessed=10**5, transcendentals=0),
        name="attend",
    )(spans, queries, own, other)


def attend_back_kernel(
    spans_ref, q_ref, own_ref, other_ref, out_ref, lse_ref, grad_ref,
    dq_ref, own_grad_ref, other_grad_ref,
    sorted_ref, q_scr, grad_scr, delta_ref, dq_scr, dk_scr, dv_scr,
):
    group = HEADS // KV_HEADS
    span = q_ref.shape[0] // 2
    width_kv = KV_HEADS * HEAD_DIM
    rows, cols = group * span, CHUNK * span
    sort_rows(spans_ref, own_ref, other_ref, sorted_ref, span)
    dk_scr[...] = jnp.zeros(dk_scr.shape, jnp.float32)
    dv_scr[...] = jnp.zeros(dv_scr.shape, jnp.float32)
    for part in range(2):
        position = spans_ref[0, 4, part]
        for g in range(KV_HEADS):
            q_scr[g] = group_rows(q_ref, part, span, g) * jnp.bfloat16(HEAD_DIM**-0.5)
            grad = group_rows(grad_ref, part, span, g)
            grad_scr[g] = grad
            delta_ref[g] = jnp.sum(
                grad.astype(jnp.float32) * group_rows(out_ref, part, span, g), 1, keepdims=True
            )
        dq_scr[...] = jnp.zeros(dq_scr.shape, jnp.float32)

        def step(i, unused):
            visible = seen(position, i, span, rows, cols)
            base = pl.multiple_of(i * cols, cols)
            for g in range(KV_HEADS):
                k = sorted_ref[pl.ds(base, cols), g * HEAD_DIM : (g + 1) * HEAD_DIM]
                v = sorted_ref[
                    pl.ds(base, cols), width_kv + g * HEAD_DIM : width_kv + (g + 1) * HEAD_DIM
                ]
                q, grad = q_scr[g], grad_scr[g]
                s = lax.dot_general(
                    q, k, (((1,), (1,)), ((), ())), preferred_element_type=jnp.float32
                )
                probs = jnp.where(visible, jnp.exp(s - lse_ref[part * KV_HEADS + g]), 0.0)
                grad_probs = lax.dot_general(
                    grad, v, (((1,), (1,)), ((), ())), preferred_element_type=jnp.float32
                )
                grad_s = (probs * (grad_probs - delta_ref[g])).astype(jnp.bfloat16)
                dq_scr[g] += jnp.dot(grad_s, k, preferred_element_type=jnp.float32)
                dk_scr[g, pl.ds(base, cols), :] += lax.dot_general(
                    grad_s, q, (((0,), (0,)), ((), ())), preferred_element_type=jnp.float32
                )
                dv_scr[g, pl.ds(base, cols), :] += lax.dot_general(
                    probs.astype(jnp.bfloat16), grad, (((0,), (0,)), ((), ())),
                    preferred_element_type=jnp.float32,
                )
            return 0

        lax.fori_loop(0, (position + CHUNK) // CHUNK, step, 0)
        for g in range(KV_HEADS):
            dq = dq_scr[g] * HEAD_DIM**-0.5
            for j in range(group):
                h = g * group + j
                dq_ref[part * span : (part + 1) * span, h * HEAD_DIM : (h + 1) * HEAD_DIM] = dq[
                    j * span : (j + 1) * span
                ]
    for m, ref in enumerate((own_grad_ref, other_grad_ref)):
        for z in range(4):
            for j in range(2):
                start = pl.multiple_of(spans_ref[m, z, j] * span, span)
                parts = [scr[g, pl.ds(start, span), :] for scr in (dk_scr, dv_scr) for g in range(KV_HEADS)]
                ref[z, j * span : (j + 1) * span, :] = jnp.concatenate(parts, 1).astype(jnp.bfloat16)


def attend_back(spans, queries, own, other, out, lse, grad):
    rows, width = queries.shape
    group = HEADS // KV_HEADS
    stacked = group * rows // 2
    wide = own.shape[2]
    vmem = pl.BlockSpec(memory_space=pltpu.VMEM)
    return pl.pallas_call(
        attend_back_kernel,
        out_shape=(
            jax.ShapeDtypeStruct((rows, width), jnp.float32),
            jax.ShapeDtypeStruct((4, rows, wide), jnp.bfloat16),
            jax.ShapeDtypeStruct((4, rows, wide), jnp.bfloat16),
        ),
        in_specs=[pl.BlockSpec(memory_space=pltpu.SMEM)] + [vmem] * 6,
        out_specs=(vmem, vmem, vmem),
        scratch_shapes=[
            pltpu.VMEM((8 * rows, wide), jnp.bfloat16),
            pltpu.VMEM((KV_HEADS, stacked, HEAD_DIM), jnp.bfloat16),
            pltpu.VMEM((KV_HEADS, stacked, HEAD_DIM), jnp.bfloat16),
            pltpu.VMEM((KV_HEADS, stacked, 1), jnp.float32),
            pltpu.VMEM((KV_HEADS, stacked, HEAD_DIM), jnp.float32),
            pltpu.VMEM((KV_HEADS, 8 * rows, HEAD_DIM), jnp.float32),
            pltpu.VMEM((KV_HEADS, 8 * rows, HEAD_DIM), jnp.float32),
        ],
        compiler_params=pltpu.CompilerParams(vmem_limit_bytes=32 * 2**20),
        cost_estimate=pl.CostEstimate(flops=10**6, bytes_accessed=10**5, transcendentals=0),
        name="attend_back",
    )(spans, queries, own, other, out, lse, grad)


TILE = 16
GU_TILES = 10
DOWN_TILES = 4
STEP = 256


def contract_last(a, w):
    return lax.dot_general(a, w, (((1,), (1,)), ((), ())), preferred_element_type=jnp.float32)


def contract_first(a, w):
    return lax.dot_general(a, w, (((0,), (0,)), ((), ())), preferred_element_type=jnp.float32)


def ff_kernel(gate_rt, up_rt, place_ref, mid_ref, gain_ref, grad_ref, target_ref, spread_ref, *refs):
    pieces, refs = refs[:10], refs[10:]
    out_ref, spread_out, act_ref, dgate_ref, dup_ref, dmid_ref, branch_ref, dgain_ref = refs[:8]
    w_scr, total_scr, back_scr, gwide_scr, sems = refs[8:]
    core = place_ref[0, 0]
    rows, width = mid_ref.shape
    half_out = DOWN_TILES * 128
    gu_rt = target_ref.shape[1] // TILE
    part = w_scr.shape[1] // 8
    copies = []
    for k in range(2):
        half = core if k == 0 else 1 - core
        spots = [(1, 0, 2), (2, 0, 2), (3, 0, 2), (4, 0, 1), (4, 1, 1)]
        for i, (n, j, parts) in enumerate(spots):
            start = (place_ref[0, n] * 2 + j) * part
            source = pieces[5 * k + i]
            target = w_scr.at[half, pl.ds(start, parts * part)]
            copies.append(pltpu.make_async_copy(source, target, sems.at[5 * k + i]))
    for copy in copies:
        copy.start()
    mid = mid_ref[...]
    scale = lax.rsqrt(jnp.mean(mid * mid, -1, keepdims=True) + EPS)
    hidden = (mid * scale * gain_ref[...]).astype(jnp.bfloat16)
    grad = grad_ref[...]
    gwide_scr[...] = jnp.zeros(gwide_scr.shape, gwide_scr.dtype)
    gwide_scr[:, :width] = grad
    total_scr[...] = jnp.zeros(total_scr.shape, jnp.float32)
    back_scr[...] = jnp.zeros(back_scr.shape, jnp.float32)
    spread_out[...] = jnp.dot(hidden, spread_ref[...], preferred_element_type=jnp.float32).astype(
        jnp.bfloat16
    )
    for copy in copies:
        copy.wait()
    kind = target_ref[...]
    gate_cols, up_first = gate_rt * TILE, up_rt * TILE
    for_gate = jnp.where(kind[:, :gate_cols] == 1, spread_out[:, :gate_cols].astype(jnp.float32), 0.0)
    for_gate = for_gate.astype(jnp.bfloat16)
    for_up = jnp.where(kind[:, up_first:] == 2, spread_out[:, up_first:].astype(jnp.float32), 0.0)
    for_up = for_up.astype(jnp.bfloat16)

    def gu_block(half, column, first, last):
        parts = [
            jnp.concatenate(
                [w_scr[half, r * GU_TILES + column + j] for r in range(first, last)], 0
            )
            for j in range(STEP // 128)
        ]
        return jnp.concatenate(parts, 1)

    def down_block(k, n):
        base = gu_rt * GU_TILES + n * (STEP // TILE * DOWN_TILES)
        parts = [
            jnp.concatenate([w_scr[k, base + r * DOWN_TILES + j] for r in range(STEP // TILE)], 0)
            for j in range(DOWN_TILES)
        ]
        return jnp.concatenate(parts, 1)

    def step(n, unused):
        half = n // (GU_TILES * 128 // STEP)
        column = n % (GU_TILES * 128 // STEP) * (STEP // 128)
        here = pl.ds(pl.multiple_of(n * STEP, STEP), STEP)
        w_gate = gu_block(half, column, 0, gate_rt)
        w_up = gu_block(half, column, up_rt, gu_rt)
        gate = jnp.dot(for_gate, w_gate, preferred_element_type=jnp.float32)
        up = jnp.dot(for_up, w_up, preferred_element_type=jnp.float32)
        sig = 1.0 / (1.0 + jnp.exp(-gate))
        silu = gate * sig
        slope = up * (sig + silu * (1.0 - sig))
        act = (silu * up).astype(jnp.bfloat16)
        act_ref[:, here] = act
        d_act = jnp.zeros((rows, STEP), jnp.float32)
        for k in range(2):
            w_down = down_block(k, n)
            cols = slice(k * half_out, (k + 1) * half_out)
            total_scr[:, cols] += jnp.dot(act, w_down, preferred_element_type=jnp.float32)
            d_act = d_act + contract_last(gwide_scr[:, cols], w_down)
        d_gate = (d_act * slope).astype(jnp.bfloat16)
        d_up = (d_act * silu).astype(jnp.bfloat16)
        dgate_ref[:, here] = d_gate
        dup_ref[:, here] = d_up
        back_gate = contract_last(d_gate, w_gate)
        back_up = contract_last(d_up, w_up)
        back_scr[:, :gate_cols] += jnp.where(kind[:, :gate_cols] == 1, back_gate, 0.0)
        back_scr[:, up_first:] += jnp.where(kind[:, up_first:] == 2, back_up, 0.0)
        return 0

    lax.fori_loop(0, 2 * GU_TILES * 128 // STEP, step, 0)
    out_ref[...] = (mid + total_scr[:, :width]).astype(jnp.bfloat16)
    back = back_scr[...]
    high = back.astype(jnp.bfloat16)
    low = (back - high.astype(jnp.float32)).astype(jnp.bfloat16)
    d_hidden = contract_last(high, spread_ref[...]) + contract_last(low, spread_ref[...])
    normed = mid * scale
    dgain_ref[...] = jnp.sum(d_hidden * normed, 0, keepdims=True)
    e = d_hidden * gain_ref[...]
    d_mid = grad.astype(jnp.float32) + scale * (e - normed * jnp.mean(e * normed, -1, keepdims=True))
    dmid_ref[...] = d_mid
    branch_ref[...] = d_mid.astype(jnp.bfloat16)


def feed_forward(core, middle, gain, grad, kind, spread, mine, other, gu_rt, gate_rt, up_rt):
    rows, width = middle.shape
    count = gu_rt * GU_TILES + FF // TILE * DOWN_TILES
    pieces = [a.reshape(-1, TILE, 128) for a in (*mine, *other)]
    padded = gu_rt * TILE
    vmem = pl.BlockSpec(memory_space=pltpu.VMEM)
    hbm = pl.BlockSpec(memory_space=pl.ANY)
    bf, f32 = jnp.bfloat16, jnp.float32
    shape = jax.ShapeDtypeStruct
    return pl.pallas_call(
        functools.partial(ff_kernel, gate_rt, up_rt),
        out_shape=(
            shape((rows, width), bf),
            shape((rows, padded), bf),
            shape((rows, FF), bf),
            shape((rows, FF), bf),
            shape((rows, FF), bf),
            shape((rows, width), f32),
            shape((rows, width), bf),
            shape((1, width), f32),
        ),
        in_specs=[pl.BlockSpec(memory_space=pltpu.SMEM)] + [vmem] * 5 + [hbm] * 10,
        out_specs=[vmem] * 8,
        scratch_shapes=[
            pltpu.VMEM((2, count, TILE, 128), bf),
            pltpu.VMEM((rows, 2 * DOWN_TILES * 128), f32),
            pltpu.VMEM((rows, padded), f32),
            pltpu.VMEM((rows, 2 * DOWN_TILES * 128), bf),
            pltpu.SemaphoreType.DMA((10,)),
        ],
        compiler_params=pltpu.CompilerParams(vmem_limit_bytes=40 * 2**20),
        cost_estimate=pl.CostEstimate(flops=10**6, bytes_accessed=10**5, transcendentals=0),
        name="feed_forward",
    )(
        core, middle, gain, grad, kind, spread, *pieces,
    )


def ff_terms_kernel(
    gate_rt, up_rt, half_ref, kind_ref, spread_ref, act_ref, dgate_ref, dup_ref, gwide_ref, out_ref
):
    half = half_ref[0, 0]
    gu_cols = GU_TILES * 128
    gu_here = pl.ds(pl.multiple_of(half * gu_cols, gu_cols), gu_cols)
    padded = spread_ref.shape[1]
    block = 256
    gu_total = padded // TILE * GU_TILES

    def put(terms, base):
        tiles_wide = terms.shape[1] // 128
        for r in range(terms.shape[0] // TILE):
            for ct in range(tiles_wide):
                tile = terms[r * TILE : (r + 1) * TILE, ct * 128 : (ct + 1) * 128]
                at = base + r * tiles_wide + ct
                out_ref[at] = tile.astype(jnp.bfloat16)

    def part(j, number, d_ref):
        here = pl.ds(pl.multiple_of(j * block, block), block)
        rows_in = jnp.where(kind_ref[:, here] == number, spread_ref[:, here].astype(jnp.float32), 0.0)
        return contract_first(rows_in.astype(jnp.bfloat16), d_ref[:, gu_here])

    def base_of(j):
        return j * (block // TILE * GU_TILES)

    mixed = (gate_rt * TILE - 1) // block

    def gate_step(j, unused):
        put(part(j, 1, dgate_ref), base_of(j))
        return 0

    def up_step(j, unused):
        put(part(j, 2, dup_ref), base_of(j))
        return 0

    lax.fori_loop(0, up_rt * TILE // block, gate_step, 0)
    for j in range(up_rt * TILE // block, mixed + 1):
        put(part(j, 1, dgate_ref) + part(j, 2, dup_ref), base_of(j))
    lax.fori_loop(mixed + 1, padded // block, up_step, 0)
    down_cols = DOWN_TILES * 128
    down_here = pl.ds(pl.multiple_of(half * down_cols, down_cols), down_cols)

    def down_step(j, unused):
        here = pl.ds(pl.multiple_of(j * STEP, STEP), STEP)
        terms = contract_first(act_ref[:, here], gwide_ref[:, down_here])
        put(terms, gu_total + j * (STEP // TILE * DOWN_TILES))
        return 0

    lax.fori_loop(0, FF // STEP, down_step, 0)


def ff_terms(half, kind, spread, act, d_gate, d_up, grad_wide, gate_rt, up_rt):
    vmem = pl.BlockSpec(memory_space=pltpu.VMEM)
    count = spread.shape[1] // TILE * GU_TILES + FF // TILE * DOWN_TILES
    operands = [kind, spread, act, d_gate, d_up, grad_wide]
    return pl.pallas_call(
        functools.partial(ff_terms_kernel, gate_rt, up_rt),
        out_shape=jax.ShapeDtypeStruct((count, TILE, 128), jnp.bfloat16),
        in_specs=[pl.BlockSpec(memory_space=pltpu.SMEM)] + [vmem] * len(operands),
        out_specs=vmem,
        compiler_params=pltpu.CompilerParams(vmem_limit_bytes=32 * 2**20),
        cost_estimate=pl.CostEstimate(flops=10**6, bytes_accessed=10**5, transcendentals=0),
        name="ff_terms",
    )(half, *operands)


def flat_wide(in_ref, out_ref, rows):
    for half in range(2):
        for rt in range(-(-rows // TILE)):
            count = min(TILE, rows - rt * TILE)
            for ct in range(GU_TILES):
                start = (rt * GU_TILES + ct) * TILE
                to = rt * TILE * 2 * GU_TILES + half * GU_TILES + ct
                out_ref[pl.ds(to, count, stride=2 * GU_TILES), :] = in_ref[
                    half, start : start + count, :
                ]


def flat_narrow(in_ref, out_ref, rows, in_start, out_start, tile):
    pairs = tile // 2
    left = lax.broadcasted_iota(jnp.int32, (pairs, 128), 1) < 64
    for rt in range(rows // tile):
        even, odd = [], []
        for ct in range(2 * DOWN_TILES):
            half, column = divmod(ct, DOWN_TILES)
            start = in_start + (rt * DOWN_TILES + column) * tile
            even.append(in_ref[half, pl.ds(start, pairs, stride=2), :])
            odd.append(pltpu.roll(in_ref[half, pl.ds(start + 1, pairs, stride=2), :], 64, 1))
        lines = even[:7] + [jnp.where(left, even[7], odd[0])]
        lines += [jnp.where(left, odd[j - 1], odd[j]) for j in range(1, 8)]
        for i, line in enumerate(lines):
            out_ref[pl.ds(out_start + 15 * pairs * rt + i, pairs, stride=15), :] = line


def ff_flat_kernel(rest, variant_ref, in_ref, out_ref):
    variant = variant_ref[0, 0]
    total = out_ref.shape[0]

    @pl.when(variant == 0)
    def gate_or_up():
        flat_wide(in_ref, out_ref, total // (2 * GU_TILES))

    @pl.when(variant == 1)
    def mixed():
        flat_wide(in_ref, out_ref, rest)
        done = rest * 2 * GU_TILES
        first = -(-rest // TILE) * TILE * GU_TILES
        flat_narrow(in_ref, out_ref, (total - done) * 2 // 15, first, done, TILE)

    @pl.when(variant == 2)
    def down():
        flat_narrow(in_ref, out_ref, total * 2 // 15, 0, 0, TILE)


def att_flat_kernel(in_ref, out_ref):
    flat_narrow(in_ref, out_ref, out_ref.shape[0] * 2 // 15, 0, 0, 8)


def flat_call(kernel, size, *operands):
    vmem = pl.BlockSpec(memory_space=pltpu.VMEM)
    smem = [pl.BlockSpec(memory_space=pltpu.SMEM)] * (len(operands) - 1)
    out = pl.pallas_call(
        kernel,
        out_shape=jax.ShapeDtypeStruct((size // 128, 128), jnp.float32),
        in_specs=smem + [vmem],
        out_specs=vmem,
        compiler_params=pltpu.CompilerParams(vmem_limit_bytes=16 * 2**20),
        cost_estimate=pl.CostEstimate(flops=10**6, bytes_accessed=10**5, transcendentals=0),
        name="flatten",
    )(*operands)
    return out.reshape(size)


BF = jnp.bfloat16
F32 = jnp.float32
LANES = 128
GU_PAD = 96
X_PAIRS = [(j, j ^ 1) for j in range(4)]
Y_PAIRS = [(j, j ^ 2) for j in range(4)]
CORE_PAIRS = [(j, j ^ 1) for j in range(8)]
EXTRA = 2


def up_pairs(first, last):
    return [(2 * z + c, 2 * z + 2 + c) for z in range(first, last) for c in range(2)]


def down_pairs(first, last):
    return [(2 * z + 2 + c, 2 * z + c) for z in range(first, last) for c in range(2)]


def swap_x(a):
    return lax.ppermute(a, "batch", X_PAIRS)


def swap_y(a):
    return lax.ppermute(a, "batch", Y_PAIRS)


def swap_core(a):
    return lax.ppermute(a, "ctx", CORE_PAIRS)


def tiles(a):
    rows, cols = a.shape
    a = a.reshape(rows // 8, 8, cols // LANES, LANES)
    return a.transpose(0, 2, 1, 3).reshape(rows * cols // (8 * LANES), 8, LANES)


def untile(a, cols):
    rows = a.shape[0] * 8 * LANES // cols
    a = a.reshape(rows // 8, cols // LANES, 8, LANES)
    return a.transpose(0, 2, 1, 3).reshape(rows, cols)


def pad_to(a, rows, cols):
    return jnp.pad(a, ((0, rows - a.shape[0]), (0, cols - a.shape[1])))


def halves_of(a):
    half = a.shape[1] // 2
    return jnp.stack([tiles(a[:, :half]), tiles(a[:, half:])])


def deep_halves_of(a):
    rows, cols = a.shape
    a = a.reshape(rows // TILE, TILE, 2, cols // (2 * LANES), LANES)
    return a.transpose(2, 0, 3, 1, 4).reshape(2, rows * cols // (2 * LANES), LANES)


def gather_line(a, z, before_last=lambda parts: parts):
    u1 = lax.ppermute(a, "ctx", up_pairs(0, 3))
    d1 = lax.ppermute(a, "ctx", down_pairs(0, 3))
    u2 = lax.ppermute(u1, "ctx", up_pairs(1, 3))
    d2 = lax.ppermute(d1, "ctx", down_pairs(0, 2))
    u2, d2 = before_last((u2, d2))
    u3 = lax.ppermute(u2, "ctx", up_pairs(2, 3))
    d3 = lax.ppermute(d2, "ctx", down_pairs(0, 1))
    seven = jnp.stack([u3, u2, u1, a, d1, d2, d3])
    return lax.dynamic_slice_in_dim(seven, 3 - z, 4, 0)


def line_pairs(hops):
    return [(2 * z + c, 2 * (z + hops) + c) for z in range(4) for c in range(2) if 0 <= z + hops < 4]


def gather_direct(a, z):
    got = {k: lax.ppermute(a, "ctx", line_pairs(k)) for k in (1, -1, 2, -2, 3, -3)}
    seven = jnp.stack([got[3], got[2], got[1], a, got[-1], got[-2], got[-3]])
    return lax.dynamic_slice_in_dim(seven, 3 - z, 4, 0)


def scatter_direct(t, z):
    total = lax.dynamic_index_in_dim(t, z, 0, keepdims=False).astype(F32)
    for k in (3, -3, 2, -2, 1, -1):
        block = lax.dynamic_index_in_dim(t, jnp.clip(z + k, 0, 3), 0, keepdims=False)
        got = lax.ppermute(block, "ctx", line_pairs(k)).astype(F32)
        total = total + jnp.where((z - k >= 0) & (z - k < 4), got, 0.0)
    return total


def gather_near(a):
    return swap_x(a), swap_y(a)


def gather_far(from_x, from_y):
    return swap_y(from_x[:2]), swap_x(from_y[2:])


def place(pieces, b, start, stop):
    shape = pieces[0][2].shape
    whole = jnp.zeros((4, 4, shape[1], stop - start) + shape[3:], BF)
    for step, row, piece in pieces:
        whole = lax.dynamic_update_slice(
            whole, piece[None, :, :, start:stop], (b ^ step, row) + (0,) * (len(shape) - 1)
        )
    return whole


def add(*terms):
    total = terms[0].astype(F32)
    for term in terms[1:]:
        total = total + term.astype(F32)
    return total.astype(BF)


def scatter_blocks(arrays, b):
    return [
        [lax.dynamic_index_in_dim(a, b ^ k, 0, keepdims=False) for a in arrays] for k in range(4)
    ]


def scatter_far(terms):
    return add(*(t[:2] for t in terms)), add(*(t[2:] for t in terms))


def scatter_near(blocks, far_x, far_y):
    xs, ys = blocks[1], blocks[2]
    x_parts = add(*(t[:2] for t in xs)), add(*(t[2:] for t in xs), far_y)
    y_parts = add(*(t[:2] for t in ys), far_x), add(*(t[2:] for t in ys))
    return swap_x(jnp.concatenate(x_parts, 0)), swap_y(jnp.concatenate(y_parts, 0))


def scatter_steps(t, z):
    def block(k):
        return lax.dynamic_index_in_dim(t, jnp.clip(z + k, 0, 3), 0, keepdims=False)

    up = down = None
    for k in (3, 2, 1):
        up_block, down_block = block(k), block(-k)
        if k < 3:
            up_block, down_block = add(up_block, up), add(down_block, down)
        up = lax.ppermute(up_block, "ctx", up_pairs(0, 4 - k))
        down = lax.ppermute(down_block, "ctx", down_pairs(k - 1, 3))
        up, down = yield up, down
        up = jnp.where((z > 0) & (z <= 4 - k), up, 0)
        down = jnp.where((z >= k - 1) & (z < 3), down, 0)
    yield block(0).astype(F32) + up.astype(F32) + down.astype(F32)


def split_high(a, parts):
    out = []
    for unused in range(parts):
        high = lax.reduce_precision(a, 8, 7)
        out.append(high.astype(BF))
        a = a - high
    return out


def local_block(tokens, attention_weights, feedforward_weights, norm_gains, span_order, cotangent):
    rows_here = tokens.shape[1]
    halves = rows_here // 2
    width_q = HEADS * HEAD_DIM
    width_kv = KV_HEADS * HEAD_DIM
    wide = 2 * 512
    b = lax.axis_index("batch")
    place_ctx = lax.axis_index("ctx")
    z = place_ctx // 2
    c = place_ctx % 2
    device = b * 8 + place_ctx
    own_gain = D // 8

    def pick(first, second):
        return jnp.where(c == 0, first, second)

    def merge(mine, other):
        return pick(
            jnp.concatenate([mine, other], -1), jnp.concatenate([other, mine], -1)
        )

    def half_of(a, k):
        half = a.shape[-1] // 2
        return jnp.where((c ^ k) == 0, a[..., :half], a[..., half:])

    def pair_up(shard):
        mine = pick(shard[0], shard[1])
        other = swap_core(pick(shard[1], shard[0]))
        return pick(jnp.stack([mine, other]), jnp.stack([other, mine]))

    att_rows = attention_weights.shape[0] // D
    att_shard = halves_of(pad_to(attention_weights.reshape(att_rows, D), att_rows, wide))
    gain_parts = jnp.stack(split_high(norm_gains, 3), 1)
    gain_rows = jnp.pad(gain_parts, ((0, 0), (0, 8 * EXTRA - 3), (0, LANES - own_gain)))
    gain_rows = gain_rows.reshape(2, EXTRA, 8, LANES)
    att_chip = pair_up(jnp.concatenate([att_shard, gain_rows], 1))
    att_line = gather_direct(att_chip, z)

    gu_rows = feedforward_weights.shape[0] // FF
    down_rows = feedforward_weights.shape[0] // D
    mixed = 2 * D // gu_rows
    rest = 2 * D - mixed * gu_rows
    rest_pad = -(-rest // TILE) * TILE
    gu_shard = deep_halves_of(pad_to(feedforward_weights.reshape(gu_rows, FF), GU_PAD, FF))
    down_shard = deep_halves_of(pad_to(feedforward_weights.reshape(down_rows, D), down_rows, wide))
    mixed_down = pad_to(
        feedforward_weights[rest * FF :].reshape(-1, D), down_rows - rest * FF // D, wide
    )
    mixed_shard = jnp.concatenate(
        [
            deep_halves_of(
                pad_to(feedforward_weights[: rest * FF].reshape(rest, FF), rest_pad, FF)
            ),
            deep_halves_of(mixed_down),
        ],
        1,
    )
    ff_shard = jnp.where(device < mixed, gu_shard, jnp.where(device == mixed, mixed_shard, down_shard))
    ff_body = ff_shard.shape[1]
    ff_chip, att_line = lax.optimization_barrier((pair_up(ff_shard), att_line))
    ff_line = gather_line(ff_chip, z)
    ff_line_other = swap_core(ff_line)

    att_x, att_y = gather_near(att_line)
    gu_total = mixed * GU_PAD + rest_pad
    pad_row = jnp.arange(gu_total, dtype=jnp.int32)
    true_row = pad_row // GU_PAD * gu_rows + pad_row % GU_PAD
    real = pad_row % GU_PAD < gu_rows
    is_gate = real & (true_row < D)
    is_up = real & (true_row >= D)
    spread = ((true_row % D)[None, :] == jnp.arange(D, dtype=jnp.int32)[:, None]) & real[None, :]
    spread = spread.astype(BF)
    third = D // 3
    order3 = jnp.arange(D, dtype=jnp.int32)
    perm3 = (order3[:, None] == (order3 % third * 3 + order3 // third)[None, :]).astype(BF)

    att_first, att_second = gather_far(att_x, att_y)
    att_pieces = (
        (0, 0, att_line), (1, 0, att_x), (2, 0, att_y), (3, 0, att_first), (3, 2, att_second)
    )
    att_body = att_rows * wide // (2 * 8 * LANES)
    att_mine = place(att_pieces, b, 0, att_body).reshape(-1, 8, LANES)
    gain_mine = place(att_pieces, b, att_body, att_body + EXTRA)
    att_other = swap_core(att_mine)
    gain_other = swap_core(gain_mine)

    def gain_from(a):
        parts = a[0, :, :, 0, :3, :own_gain].astype(F32)
        return (parts[:, :, 0] + parts[:, :, 1] + parts[:, :, 2]).reshape(D)

    gain_m, gain_o = gain_from(gain_mine), gain_from(gain_other)
    gain_full = jnp.stack([pick(gain_m, gain_o), pick(gain_o, gain_m)])


    offsets = jnp.arange(halves, dtype=jnp.int32)
    query_pos = (span_order[0][:, None] * halves + offsets[None, :]).reshape(rows_here)
    cos_table, sin_table = rope_tables(query_pos)

    inputs = tokens[0].astype(F32)
    hidden_f, norm_one_pull = jax.vjp(normalize, inputs, gain_full[0])
    hidden = hidden_f.astype(BF)
    hidden3 = jnp.dot(hidden, perm3, preferred_element_type=F32).astype(BF)
    hidden3 = hidden3.reshape(rows_here, 3, third)
    att_m, att_o = untile(att_mine, wide // 2), untile(att_other, wide // 2)
    cut_k, cut_v, cut_o = D, D + third, D + 2 * third

    def project(a, start, stop):
        return merge(
            jnp.dot(a, att_m[start:stop], preferred_element_type=F32),
            jnp.dot(a, att_o[start:stop], preferred_element_type=F32),
        )

    def thirds(start, stop):
        out = project(hidden3.transpose(1, 0, 2).reshape(3 * rows_here, third), start, stop)
        out = out.reshape(3, rows_here, wide)
        return out[0, :, :third] + out[1, :, third : 2 * third] + out[2, :, 2 * third : 3 * third]

    query_raw = project(hidden, 0, D)[:, :width_q].reshape(rows_here, HEADS, HEAD_DIM)
    key_raw = thirds(cut_k, cut_v).reshape(rows_here, KV_HEADS, HEAD_DIM)
    values = thirds(cut_v, cut_o).astype(BF)
    query_rot, query_pull = jax.vjp(lambda a: rotate(a, cos_table, sin_table), query_raw)
    key_rot, key_pull = jax.vjp(lambda a: rotate(a, cos_table, sin_table), key_raw)
    queries = query_rot.astype(BF).reshape(rows_here, width_q)
    keys = key_rot.astype(BF).reshape(rows_here, width_kv)

    span_rows = jnp.pad(span_order.astype(BF), ((0, 15), (0, 2 * width_kv - 2)))
    key_value = jnp.concatenate([jnp.concatenate([keys, values], 1), span_rows], 0)
    ff_near = gather_near(ff_line)
    waited = []

    def wait_for_near(parts):
        near, parts = lax.optimization_barrier((ff_near, parts))
        waited.append(near)
        return parts

    line_mine = gather_line(key_value, z, wait_for_near)
    ff_near = waited[0]
    line_mine, queries, spread = lax.optimization_barrier((line_mine, queries, spread))
    line_other = swap_core(line_mine)
    ff_far = gather_far(*ff_near)
    spans = jnp.stack([line_mine[:, rows_here, :2], line_other[:, rows_here, :2]]).astype(jnp.int32)
    spans = jnp.concatenate([spans, jnp.broadcast_to(span_order[None], (2, 1, 2))], 1)
    attended, log_total = attend(spans, queries, line_mine, line_other)
    ff_far, attended = lax.optimization_barrier((ff_far, attended))
    ff_mine = (ff_line, *ff_near, *ff_far)
    ff_other = (ff_line_other, *(swap_core(piece) for piece in ff_mine[1:]))
    attended_low = attended.astype(BF)
    middle = inputs + project(attended_low, cut_o, cut_o + D)[:, :D]
    gate_end = -(-D // gu_rows) * GU_PAD
    up_start = D // gu_rows * GU_PAD
    grad_wide = jnp.pad(cotangent[0], ((0, 0), (0, wide - D)))
    kind = (is_gate.astype(jnp.int32) + 2 * is_up.astype(jnp.int32))[None]
    result, spread_two, activ, grad_gate, grad_upward, grad_middle, grad_branch, grad_gain_two = (
        feed_forward(
            jnp.stack([c, b, b ^ 1, b ^ 2, b ^ 3])[None], middle, gain_full[1:2], cotangent[0], kind, spread,
            ff_mine, ff_other,
            gu_total // TILE, gate_end // TILE, up_start // TILE,
        )
    )
    grad_gain_two = grad_gain_two[0]

    def times_transposed(a, w):
        return lax.dot_general(a, w, (((1,), (1,)), ((), ())), preferred_element_type=F32)

    def transposed_times(a, w):
        return lax.dot_general(a, w, (((0,), (0,)), ((), ())), preferred_element_type=F32)

    def terms_of_half(half, rows_in):
        return ff_terms(
            half.reshape(1, 1), kind, rows_in, activ, grad_gate, grad_upward, grad_wide,
            gate_end // TILE, up_start // TILE,
        )

    ff_send, spread_two, grad_branch = lax.optimization_barrier(
        (terms_of_half(1 - c, spread_two), spread_two, grad_branch)
    )
    ff_from = swap_core(ff_send)
    ff_keep = terms_of_half(c, spread_two)
    ff_blocks = scatter_blocks(
        [a.reshape(4, 4, 2, ff_body, LANES) for a in (ff_keep, ff_from)], b
    )
    branch_wide = jnp.pad(grad_branch, ((0, 0), (0, wide - D)))

    def project_back(a, start, stop):
        return times_transposed(half_of(a, 0), att_m[start:stop]) + times_transposed(
            half_of(a, 1), att_o[start:stop]
        )

    grad_attended = project_back(branch_wide, cut_o, cut_o + D).astype(BF)
    ff_far, grad_attended = lax.optimization_barrier((scatter_far(ff_blocks[3]), grad_attended))
    ff_far = swap_x(ff_far[0]), swap_y(ff_far[1])
    grad_query_rot, both_mine, both_other = attend_back(
        spans, queries, line_mine, line_other, attended, log_total, grad_attended
    )
    ff_far, both_other = lax.optimization_barrier((ff_far, both_other))
    both_from = swap_core(both_other)
    ff_near = scatter_near(ff_blocks, *ff_far)
    both_own = scatter_direct(add(both_mine, both_from), z)
    ff_near, both_own = lax.optimization_barrier((ff_near, both_own))
    ff_steps = scatter_steps(add(*ff_blocks[0], *ff_near), z)
    ff_step = next(ff_steps)
    grad_key_rot, grad_value_f = both_own[:, :width_kv], both_own[:, width_kv:]
    grad_query_raw = query_pull(grad_query_rot.reshape(rows_here, HEADS, HEAD_DIM))[0]
    grad_key_raw = key_pull(grad_key_rot.reshape(rows_here, KV_HEADS, HEAD_DIM))[0]
    grad_query = grad_query_raw.reshape(rows_here, width_q).astype(BF)
    grad_key = grad_key_raw.reshape(rows_here, width_kv).astype(BF)
    grad_value = grad_value_f.astype(BF)

    def spots(a):
        return jnp.concatenate(
            [jnp.pad(a, ((0, 0), (q * third, wide - (q + 1) * third))) for q in range(3)], 0
        )

    query_wide = jnp.pad(grad_query, ((0, 0), (0, wide - D)))
    key_spots, value_spots = spots(grad_key), spots(grad_value)
    hidden_rows = hidden3.transpose(1, 0, 2).reshape(3 * rows_here, third)
    back_three = project_back(key_spots, cut_k, cut_v) + project_back(value_spots, cut_v, cut_o)
    back_three = back_three.reshape(3, rows_here, third).transpose(1, 0, 2).reshape(rows_here, D)
    ff_step, back_three = lax.optimization_barrier((ff_step, back_three))
    ff_step = ff_steps.send(ff_step)
    grad_hidden = project_back(query_wide, 0, D) + times_transposed(
        jnp.concatenate(split_high(back_three, 2), 1), jnp.concatenate([perm3, perm3], 1)
    )
    ff_step, grad_hidden = lax.optimization_barrier((ff_step, grad_hidden))
    ff_step = ff_steps.send(ff_step)
    grad_inputs_norm, grad_gain_one = norm_one_pull(grad_hidden)
    grad_inputs = grad_middle + grad_inputs_norm

    gain_terms = jnp.stack([grad_gain_one, grad_gain_two]).reshape(2, 8, own_gain)
    gain_terms = jnp.pad(
        jnp.stack(split_high(gain_terms, 2), 2),
        ((0, 0), (0, 0), (0, 8 * EXTRA - 2), (0, LANES - own_gain)),
    ).reshape(2, 4, 2, EXTRA, 8, LANES)

    def att_terms(k):
        terms = jnp.concatenate(
            [
                transposed_times(hidden, half_of(query_wide, k)).astype(BF),
                transposed_times(hidden_rows, half_of(key_spots, k)).astype(BF),
                transposed_times(hidden_rows, half_of(value_spots, k)).astype(BF),
                transposed_times(attended_low, half_of(branch_wide, k)).astype(BF),
            ],
            0,
        )
        gain = jnp.where((c ^ k) == 0, gain_terms[0], gain_terms[1])
        gain = jnp.broadcast_to(gain[None], (4, 4, 2, EXTRA, 8, LANES))
        return jnp.concatenate([tiles(terms).reshape(4, 4, 2, att_body, 8, LANES), gain], 3)

    att_from = swap_core(att_terms(1))
    att_blocks = scatter_blocks((att_terms(0), att_from), b)
    att_far = scatter_far(att_blocks[3])
    att_far = swap_x(att_far[0]), swap_y(att_far[1])
    ff_step, att_far = lax.optimization_barrier((ff_step, att_far))
    ff_own = ff_steps.send(ff_step)
    att_near = scatter_near(att_blocks, *att_far)

    def settle(own):
        mine = pick(own[0], own[1])
        other = swap_core(pick(own[1], own[0]))
        return pick(jnp.stack([mine, other]), jnp.stack([other, mine]))

    ff_done = settle(ff_own)
    variant = jnp.where(device < mixed, 0, jnp.where(device == mixed, 1, 2)).astype(jnp.int32)
    ff_flat = flat_call(
        functools.partial(ff_flat_kernel, rest), feedforward_weights.shape[0],
        variant.reshape(1, 1), ff_done,
    )
    ff_flat, att_near = lax.optimization_barrier((ff_flat, att_near))
    att_own = scatter_direct(add(*att_blocks[0], *att_near), z)
    att_done = settle(att_own)
    gain_own = att_done[:, att_body, 0, :own_gain] + att_done[:, att_body, 1, :own_gain]
    att_flat = flat_call(
        att_flat_kernel, attention_weights.shape[0], att_done.reshape(2, -1, LANES)
    )
    return (
        result[None],
        grad_inputs[None],
        att_flat,
        ff_flat,
        gain_own,
    )


def solution(mesh):
    fits = mesh.shape["batch"] == 4 and mesh.shape["ctx"] == 8
    local = local_block if fits else local_any
    placed = (
        P("batch", "ctx", None),
        P(("batch", "ctx")),
        P(("batch", "ctx")),
        P(None, "ctx"),
        P("batch", "ctx"),
        P("batch", "ctx", None),
    )
    return jax.shard_map(
        local,
        mesh=mesh,
        in_specs=placed,
        out_specs=(
            P("batch", "ctx", None),
            P("batch", "ctx", None),
            P(("batch", "ctx")),
            P(("batch", "ctx")),
            P(None, "ctx"),
        ),
        check_vma=False,
    )
```

```python
import functools
import math

import jax
import jax.numpy as jnp
from jax import lax
from jax.experimental import pallas as pl
from jax.experimental.pallas import tpu as pltpu
from jax.sharding import PartitionSpec as P

D = 960
HEADS = 15
KV_HEADS = 5
HEAD_DIM = 64
FF = 2560


ROPE_BASE = 100000.0
EPS = 1e-05
NEG = -1e30


def normalize(values, gain):
    return values * lax.rsqrt(jnp.mean(values * values, -1, keepdims=True) + EPS) * gain


def swiglu(gate, upward):
    return jax.nn.silu(gate) * upward


def rope_tables(positions):
    halves = HEAD_DIM // 2
    inverse_freq = ROPE_BASE ** (-jnp.arange(halves, dtype=jnp.float32) / halves)
    angles = positions.astype(jnp.float32)[:, None] * inverse_freq[None, :]
    return (jnp.cos(angles), jnp.sin(angles))


def rotate(values, cos_table, sin_table):
    halves = HEAD_DIM // 2
    first = values[..., :halves]
    second = values[..., halves:]
    cos_table = cos_table[:, None, :]
    sin_table = sin_table[:, None, :]
    return jnp.concatenate(
        [first * cos_table - second * sin_table, second * cos_table + first * sin_table], -1
    )


def split_flat(flat, shapes):
    pieces = []
    offset = 0
    for rows_in, cols_in in shapes:
        pieces.append(flat[offset : offset + rows_in * cols_in].reshape(rows_in, cols_in))
        offset += rows_in * cols_in
    return pieces


def unpack(att_flat, ff_flat):
    width_q = HEADS * HEAD_DIM
    width_kv = KV_HEADS * HEAD_DIM
    att_parts = split_flat(att_flat, [(D, width_q), (D, width_kv), (D, width_kv), (width_q, D)])
    ff_parts = split_flat(ff_flat, [(D, FF), (D, FF), (FF, D)])
    return (att_parts, ff_parts)


def score_block(queries, key_block, query_pos, key_pos):
    keys_three = key_block.reshape(key_block.shape[0], KV_HEADS, HEAD_DIM)
    scores = jnp.einsum(
        "qhgd,khd->hgqk", queries, keys_three, preferred_element_type=jnp.float32
    ) * HEAD_DIM ** (-0.5)
    visible = key_pos[None, None, None, :] <= query_pos[None, None, :, None]
    return (scores, visible)


def attention_forward(queries, key_all, value_all, query_pos, key_pos, block):
    rows_here = queries.shape[0]
    group = HEADS // KV_HEADS
    count = key_all.shape[0] // block
    key_blocks = key_all.reshape(count, block, key_all.shape[1])
    value_blocks = value_all.reshape(count, block, value_all.shape[1])
    pos_blocks = key_pos.reshape(count, block)

    def online_step(carry, item):
        top, total, accum = carry
        key_block, value_block, pos_block = item
        scores, visible = score_block(queries, key_block, query_pos, pos_block)
        scores = jnp.where(visible, scores, NEG)
        new_top = jnp.maximum(top, jnp.max(scores, -1))
        weights = jnp.where(visible, jnp.exp(scores - new_top[..., None]), 0.0)
        factor = jnp.exp(top - new_top)
        total = total * factor + jnp.sum(weights, -1)
        values_three = value_block.reshape(block, KV_HEADS, HEAD_DIM)
        accum = accum * jnp.transpose(factor, (2, 0, 1))[..., None]
        accum = accum + jnp.einsum(
            "hgqk,khd->qhgd",
            weights.astype(jnp.bfloat16),
            values_three,
            preferred_element_type=jnp.float32,
        )
        return ((new_top, total, accum), None)

    start_top = jnp.full((KV_HEADS, group, rows_here), NEG, jnp.float32)
    start_total = jnp.zeros((KV_HEADS, group, rows_here), jnp.float32)
    start_out = jnp.zeros((rows_here, KV_HEADS, group, HEAD_DIM), jnp.float32)
    (top, total, accum), unused = lax.scan(
        online_step, (start_top, start_total, start_out), (key_blocks, value_blocks, pos_blocks)
    )
    log_total = top + jnp.log(total)
    attended = accum / jnp.transpose(total, (2, 0, 1))[..., None]
    return (attended, log_total)


def attention_backward(
    queries, key_all, value_all, query_pos, key_pos, block, log_total, grad_out, attended
):
    rows_here = queries.shape[0]
    group = HEADS // KV_HEADS
    width_kv = key_all.shape[1]
    count = key_all.shape[0] // block
    items = (
        key_all.reshape(count, block, width_kv),
        value_all.reshape(count, block, width_kv),
        key_pos.reshape(count, block),
    )
    delta = jnp.transpose(jnp.sum(grad_out.astype(jnp.float32) * attended, -1), (1, 2, 0))

    def grad_step(grad_query, item):
        key_block, value_block, pos_block = item
        scores, visible = score_block(queries, key_block, query_pos, pos_block)
        probs = jnp.where(visible, jnp.exp(scores - log_total[..., None]), 0.0)
        values_three = value_block.reshape(block, KV_HEADS, HEAD_DIM)
        grad_probs = jnp.einsum(
            "qhgd,khd->hgqk", grad_out, values_three, preferred_element_type=jnp.float32
        )
        grad_scores = (probs * (grad_probs - delta[..., None])).astype(jnp.bfloat16)
        keys_three = key_block.reshape(block, KV_HEADS, HEAD_DIM)
        grad_query = grad_query + jnp.einsum(
            "hgqk,khd->qhgd", grad_scores, keys_three, preferred_element_type=jnp.float32
        )
        grad_key = jnp.einsum(
            "hgqk,qhgd->khd", grad_scores, queries, preferred_element_type=jnp.float32
        )
        grad_value = jnp.einsum(
            "hgqk,qhgd->khd",
            probs.astype(jnp.bfloat16),
            grad_out,
            preferred_element_type=jnp.float32,
        )
        return (
            grad_query,
            (grad_key.reshape(block, width_kv), grad_value.reshape(block, width_kv)),
        )

    start_query = jnp.zeros((rows_here, KV_HEADS, group, HEAD_DIM), jnp.float32)
    grad_query, (grad_keys, grad_values) = lax.scan(grad_step, start_query, items)
    return (
        grad_query,
        grad_keys.reshape(count * block, width_kv),
        grad_values.reshape(count * block, width_kv),
    )


def local_any(tokens, attention_weights, feedforward_weights, norm_gains, span_order, cotangent):
    ctx_count = lax.axis_size("ctx")
    batch_count = lax.axis_size("batch")
    rows_here = tokens.shape[1]
    halves = rows_here // 2
    length = rows_here * ctx_count
    group = HEADS // KV_HEADS
    width_q = HEADS * HEAD_DIM
    width_kv = KV_HEADS * HEAD_DIM
    block = math.gcd(length, 512)
    scaling = HEAD_DIM ** (-0.5)
    att_full, ff_full = (
        lax.all_gather(attention_weights, ("batch", "ctx"), axis=0, tiled=True),
        lax.all_gather(feedforward_weights, ("batch", "ctx"), axis=0, tiled=True),
    )
    gain_full = lax.all_gather(norm_gains, "ctx", axis=1, tiled=True)
    order_full = lax.all_gather(span_order, "ctx", axis=1, tiled=True)
    offsets = jnp.arange(halves, dtype=jnp.int32)
    key_pos = (order_full[0][:, None] * halves + offsets[None, :]).reshape(length)
    query_pos = (span_order[0][:, None] * halves + offsets[None, :]).reshape(rows_here)
    cos_table, sin_table = rope_tables(query_pos)
    (w_query, w_key, w_value, w_out), (w_gate, w_up, w_down) = unpack(att_full, ff_full)
    inputs = tokens[0].astype(jnp.float32)
    hidden_f, norm_one_pull = jax.vjp(normalize, inputs, gain_full[0])
    hidden = hidden_f.astype(jnp.bfloat16)
    query_raw = jnp.dot(hidden, w_query, preferred_element_type=jnp.float32).reshape(
        rows_here, HEADS, HEAD_DIM
    )
    key_raw = jnp.dot(hidden, w_key, preferred_element_type=jnp.float32).reshape(
        rows_here, KV_HEADS, HEAD_DIM
    )
    values = jnp.dot(hidden, w_value, preferred_element_type=jnp.float32).astype(jnp.bfloat16)
    query_rot, query_pull = jax.vjp(lambda a: rotate(a, cos_table, sin_table), query_raw)
    key_rot, key_pull = jax.vjp(lambda a: rotate(a, cos_table, sin_table), key_raw)
    queries = query_rot.astype(jnp.bfloat16).reshape(rows_here, KV_HEADS, group, HEAD_DIM)
    keys = key_rot.astype(jnp.bfloat16).reshape(rows_here, width_kv)
    key_all, value_all = (
        lax.all_gather(keys, "ctx", axis=0, tiled=True),
        lax.all_gather(values, "ctx", axis=0, tiled=True),
    )
    attended, log_total = attention_forward(queries, key_all, value_all, query_pos, key_pos, block)
    attended_low = attended.reshape(rows_here, width_q).astype(jnp.bfloat16)
    middle = inputs + jnp.dot(attended_low, w_out, preferred_element_type=jnp.float32)
    hidden_two_f, norm_two_pull = jax.vjp(normalize, middle, gain_full[1])
    hidden_two = hidden_two_f.astype(jnp.bfloat16)
    gate = jnp.dot(hidden_two, w_gate, preferred_element_type=jnp.float32)
    upward = jnp.dot(hidden_two, w_up, preferred_element_type=jnp.float32)
    activ_f, swiglu_pull = jax.vjp(swiglu, gate, upward)
    activ = activ_f.astype(jnp.bfloat16)
    result = middle + jnp.dot(activ, w_down, preferred_element_type=jnp.float32)
    grad_result = cotangent[0]
    grad_down = jnp.einsum("tf,td->fd", activ, grad_result, preferred_element_type=jnp.float32)
    grad_activ = jnp.einsum("td,fd->tf", grad_result, w_down, preferred_element_type=jnp.float32)
    grad_gate_f, grad_up_f = swiglu_pull(grad_activ)
    grad_gate = grad_gate_f.astype(jnp.bfloat16)
    grad_upward = grad_up_f.astype(jnp.bfloat16)
    grad_w_gate = jnp.einsum("td,tf->df", hidden_two, grad_gate, preferred_element_type=jnp.float32)
    grad_w_up = jnp.einsum("td,tf->df", hidden_two, grad_upward, preferred_element_type=jnp.float32)
    grad_hidden_two = jnp.einsum("tf,df->td", grad_gate, w_gate, preferred_element_type=jnp.float32)
    grad_hidden_two = grad_hidden_two + jnp.einsum(
        "tf,df->td", grad_upward, w_up, preferred_element_type=jnp.float32
    )
    grad_middle_norm, grad_gain_two = norm_two_pull(grad_hidden_two)
    grad_middle = grad_result.astype(jnp.float32) + grad_middle_norm
    grad_branch = grad_middle.astype(jnp.bfloat16)
    grad_w_out = jnp.einsum(
        "tq,td->qd", attended_low, grad_branch, preferred_element_type=jnp.float32
    )
    grad_attended = jnp.einsum(
        "td,qd->tq", grad_branch, w_out, preferred_element_type=jnp.float32
    ).astype(jnp.bfloat16)
    grad_attended = grad_attended.reshape(rows_here, KV_HEADS, group, HEAD_DIM)
    grad_query_rot, grad_key_all, grad_value_all = attention_backward(
        queries, key_all, value_all, query_pos, key_pos, block, log_total, grad_attended, attended
    )
    grad_key_rot, grad_value_f = (
        lax.psum_scatter(
            grad_key_all.astype(jnp.bfloat16), "ctx", scatter_dimension=0, tiled=True
        ).astype(jnp.float32),
        lax.psum_scatter(
            grad_value_all.astype(jnp.bfloat16), "ctx", scatter_dimension=0, tiled=True
        ).astype(jnp.float32),
    )
    grad_query_raw = query_pull(grad_query_rot.reshape(rows_here, HEADS, HEAD_DIM) * scaling)[0]
    grad_key_raw = key_pull(grad_key_rot.reshape(rows_here, KV_HEADS, HEAD_DIM) * scaling)[0]
    grad_query = grad_query_raw.reshape(rows_here, width_q).astype(jnp.bfloat16)
    grad_key = grad_key_raw.reshape(rows_here, width_kv).astype(jnp.bfloat16)
    grad_value = grad_value_f.astype(jnp.bfloat16)
    grad_w_query = jnp.einsum("td,tq->dq", hidden, grad_query, preferred_element_type=jnp.float32)
    grad_w_key = jnp.einsum("td,tq->dq", hidden, grad_key, preferred_element_type=jnp.float32)
    grad_w_value = jnp.einsum("td,tq->dq", hidden, grad_value, preferred_element_type=jnp.float32)
    grad_hidden = jnp.einsum("tq,dq->td", grad_query, w_query, preferred_element_type=jnp.float32)
    grad_hidden = grad_hidden + jnp.einsum(
        "tq,dq->td", grad_key, w_key, preferred_element_type=jnp.float32
    )
    grad_hidden = grad_hidden + jnp.einsum(
        "tq,dq->td", grad_value, w_value, preferred_element_type=jnp.float32
    )
    grad_inputs_norm, grad_gain_one = norm_one_pull(grad_hidden)
    grad_inputs = grad_middle + grad_inputs_norm
    grad_att_flat = jnp.concatenate(
        [
            grad_w_query.reshape(-1),
            grad_w_key.reshape(-1),
            grad_w_value.reshape(-1),
            grad_w_out.reshape(-1),
        ]
    )
    grad_ff_flat = jnp.concatenate(
        [grad_w_gate.reshape(-1), grad_w_up.reshape(-1), grad_down.reshape(-1)]
    )
    width_own = D // ctx_count
    gain_terms = jnp.stack([grad_gain_one, grad_gain_two]).reshape(2, ctx_count, width_own)
    gain_terms = jnp.transpose(gain_terms, (1, 0, 2)).reshape(ctx_count, 2 * width_own)
    gain_terms = jnp.broadcast_to(
        gain_terms[None], (batch_count, ctx_count, 2 * width_own)
    ).reshape(batch_count * ctx_count, 2 * width_own)
    att_part, ff_part, gain_part = (
        lax.psum_scatter(
            grad_att_flat.astype(jnp.bfloat16), "batch", scatter_dimension=0, tiled=True
        ).astype(jnp.float32),
        lax.psum_scatter(
            grad_ff_flat.astype(jnp.bfloat16), "batch", scatter_dimension=0, tiled=True
        ).astype(jnp.float32),
        lax.psum_scatter(
            gain_terms.astype(jnp.bfloat16), "batch", scatter_dimension=0, tiled=True
        ).astype(jnp.float32),
    )
    grad_att_own, grad_ff_own, gain_own = (
        lax.psum_scatter(
            att_part.astype(jnp.bfloat16), "ctx", scatter_dimension=0, tiled=True
        ).astype(jnp.float32),
        lax.psum_scatter(
            ff_part.astype(jnp.bfloat16), "ctx", scatter_dimension=0, tiled=True
        ).astype(jnp.float32),
        lax.psum_scatter(
            gain_part.astype(jnp.bfloat16), "ctx", scatter_dimension=0, tiled=True
        ).astype(jnp.float32),
    )
    grad_gain_own = gain_own.reshape(2, width_own)
    return (
        result.astype(jnp.bfloat16)[None],
        grad_inputs[None],
        grad_att_own,
        grad_ff_own,
        grad_gain_own,
    )


CHUNK = 4


def sort_rows(spans_ref, own_ref, other_ref, sorted_ref, span):
    for m, ref in enumerate((own_ref, other_ref)):
        for z in range(4):
            for j in range(2):
                start = pl.multiple_of(spans_ref[m, z, j] * span, span)
                sorted_ref[pl.ds(start, span), :] = ref[z, j * span : (j + 1) * span, :]


def group_rows(ref, part, span, head):
    group = HEADS // KV_HEADS
    rows = ref[part * span : (part + 1) * span, :]
    columns = [
        rows[:, (head * group + j) * HEAD_DIM : (head * group + j + 1) * HEAD_DIM]
        for j in range(group)
    ]
    return jnp.concatenate(columns, 0)


def seen(position, step, span, rows, cols):
    row = lax.broadcasted_iota(jnp.int32, (rows, cols), 0) % span
    col = lax.broadcasted_iota(jnp.int32, (rows, cols), 1)
    return col + step * cols <= row + position * span


def attend_kernel(
    spans_ref, q_ref, own_ref, other_ref, out_ref, lse_ref, sorted_ref, q_scr, top_ref, sum_ref, acc_ref
):
    group = HEADS // KV_HEADS
    span = q_ref.shape[0] // 2
    width_kv = KV_HEADS * HEAD_DIM
    rows, cols = group * span, CHUNK * span
    sort_rows(spans_ref, own_ref, other_ref, sorted_ref, span)
    for part in range(2):
        position = spans_ref[0, 4, part]
        for g in range(KV_HEADS):
            q_scr[g] = group_rows(q_ref, part, span, g) * jnp.bfloat16(HEAD_DIM**-0.5)
        top_ref[...] = jnp.full(top_ref.shape, NEG, jnp.float32)
        sum_ref[...] = jnp.zeros(sum_ref.shape, jnp.float32)
        acc_ref[...] = jnp.zeros(acc_ref.shape, jnp.float32)

        def step(i, unused):
            visible = seen(position, i, span, rows, cols)
            base = pl.multiple_of(i * cols, cols)
            for g in range(KV_HEADS):
                k = sorted_ref[pl.ds(base, cols), g * HEAD_DIM : (g + 1) * HEAD_DIM]
                v = sorted_ref[
                    pl.ds(base, cols), width_kv + g * HEAD_DIM : width_kv + (g + 1) * HEAD_DIM
                ]
                s = lax.dot_general(
                    q_scr[g], k, (((1,), (1,)), ((), ())), preferred_element_type=jnp.float32
                )
                s = jnp.where(visible, s, NEG)
                old = top_ref[g]
                top = jnp.maximum(old, jnp.max(s, 1, keepdims=True))
                weights = jnp.where(visible, jnp.exp(s - top), 0.0)
                factor = jnp.exp(old - top)
                top_ref[g] = top
                sum_ref[g] = sum_ref[g] * factor + jnp.sum(weights, 1, keepdims=True)
                acc_ref[g] = acc_ref[g] * factor + jnp.dot(
                    weights.astype(jnp.bfloat16), v, preferred_element_type=jnp.float32
                )
            return 0

        lax.fori_loop(0, (position + CHUNK) // CHUNK, step, 0)
        for g in range(KV_HEADS):
            out = acc_ref[g] / sum_ref[g]
            lse_ref[part * KV_HEADS + g] = top_ref[g] + jnp.log(sum_ref[g])
            for j in range(group):
                h = g * group + j
                out_ref[part * span : (part + 1) * span, h * HEAD_DIM : (h + 1) * HEAD_DIM] = out[
                    j * span : (j + 1) * span
                ]


def attend(spans, queries, own, other):
    rows, width = queries.shape
    group = HEADS // KV_HEADS
    stacked = group * rows // 2
    vmem = pl.BlockSpec(memory_space=pltpu.VMEM)
    return pl.pallas_call(
        attend_kernel,
        out_shape=(
            jax.ShapeDtypeStruct((rows, width), jnp.float32),
            jax.ShapeDtypeStruct((2 * KV_HEADS, stacked, 1), jnp.float32),
        ),
        in_specs=[pl.BlockSpec(memory_space=pltpu.SMEM), vmem, vmem, vmem],
        out_specs=(vmem, vmem),
        scratch_shapes=[
            pltpu.VMEM((8 * rows, own.shape[2]), jnp.bfloat16),
            pltpu.VMEM((KV_HEADS, stacked, HEAD_DIM), jnp.bfloat16),
            pltpu.VMEM((KV_HEADS, stacked, 1), jnp.float32),
            pltpu.VMEM((KV_HEADS, stacked, 1), jnp.float32),
            pltpu.VMEM((KV_HEADS, stacked, HEAD_DIM), jnp.float32),
        ],
        compiler_params=pltpu.CompilerParams(vmem_limit_bytes=24 * 2**20),
        cost_estimate=pl.CostEstimate(flops=10**6, bytes_accessed=10**5, transcendentals=0),
        name="attend",
    )(spans, queries, own, other)


def attend_back_kernel(
    spans_ref, q_ref, own_ref, other_ref, out_ref, lse_ref, grad_ref,
    dq_ref, own_grad_ref, other_grad_ref,
    sorted_ref, q_scr, grad_scr, delta_ref, dq_scr, dk_scr, dv_scr,
):
    group = HEADS // KV_HEADS
    span = q_ref.shape[0] // 2
    width_kv = KV_HEADS * HEAD_DIM
    rows, cols = group * span, CHUNK * span
    sort_rows(spans_ref, own_ref, other_ref, sorted_ref, span)
    dk_scr[...] = jnp.zeros(dk_scr.shape, jnp.float32)
    dv_scr[...] = jnp.zeros(dv_scr.shape, jnp.float32)
    for part in range(2):
        position = spans_ref[0, 4, part]
        for g in range(KV_HEADS):
            q_scr[g] = group_rows(q_ref, part, span, g) * jnp.bfloat16(HEAD_DIM**-0.5)
            grad = group_rows(grad_ref, part, span, g)
            grad_scr[g] = grad
            delta_ref[g] = jnp.sum(
                grad.astype(jnp.float32) * group_rows(out_ref, part, span, g), 1, keepdims=True
            )
        dq_scr[...] = jnp.zeros(dq_scr.shape, jnp.float32)

        def step(i, unused):
            visible = seen(position, i, span, rows, cols)
            base = pl.multiple_of(i * cols, cols)
            for g in range(KV_HEADS):
                k = sorted_ref[pl.ds(base, cols), g * HEAD_DIM : (g + 1) * HEAD_DIM]
                v = sorted_ref[
                    pl.ds(base, cols), width_kv + g * HEAD_DIM : width_kv + (g + 1) * HEAD_DIM
                ]
                q, grad = q_scr[g], grad_scr[g]
                s = lax.dot_general(
                    q, k, (((1,), (1,)), ((), ())), preferred_element_type=jnp.float32
                )
                probs = jnp.where(visible, jnp.exp(s - lse_ref[part * KV_HEADS + g]), 0.0)
                grad_probs = lax.dot_general(
                    grad, v, (((1,), (1,)), ((), ())), preferred_element_type=jnp.float32
                )
                grad_s = (probs * (grad_probs - delta_ref[g])).astype(jnp.bfloat16)
                dq_scr[g] += jnp.dot(grad_s, k, preferred_element_type=jnp.float32)
                dk_scr[g, pl.ds(base, cols), :] += lax.dot_general(
                    grad_s, q, (((0,), (0,)), ((), ())), preferred_element_type=jnp.float32
                )
                dv_scr[g, pl.ds(base, cols), :] += lax.dot_general(
                    probs.astype(jnp.bfloat16), grad, (((0,), (0,)), ((), ())),
                    preferred_element_type=jnp.float32,
                )
            return 0

        lax.fori_loop(0, (position + CHUNK) // CHUNK, step, 0)
        for g in range(KV_HEADS):
            dq = dq_scr[g] * HEAD_DIM**-0.5
            for j in range(group):
                h = g * group + j
                dq_ref[part * span : (part + 1) * span, h * HEAD_DIM : (h + 1) * HEAD_DIM] = dq[
                    j * span : (j + 1) * span
                ]
    for m, ref in enumerate((own_grad_ref, other_grad_ref)):
        for z in range(4):
            for j in range(2):
                start = pl.multiple_of(spans_ref[m, z, j] * span, span)
                parts = [scr[g, pl.ds(start, span), :] for scr in (dk_scr, dv_scr) for g in range(KV_HEADS)]
                ref[z, j * span : (j + 1) * span, :] = jnp.concatenate(parts, 1).astype(jnp.bfloat16)


def attend_back(spans, queries, own, other, out, lse, grad):
    rows, width = queries.shape
    group = HEADS // KV_HEADS
    stacked = group * rows // 2
    wide = own.shape[2]
    vmem = pl.BlockSpec(memory_space=pltpu.VMEM)
    return pl.pallas_call(
        attend_back_kernel,
        out_shape=(
            jax.ShapeDtypeStruct((rows, width), jnp.float32),
            jax.ShapeDtypeStruct((4, rows, wide), jnp.bfloat16),
            jax.ShapeDtypeStruct((4, rows, wide), jnp.bfloat16),
        ),
        in_specs=[pl.BlockSpec(memory_space=pltpu.SMEM)] + [vmem] * 6,
        out_specs=(vmem, vmem, vmem),
        scratch_shapes=[
            pltpu.VMEM((8 * rows, wide), jnp.bfloat16),
            pltpu.VMEM((KV_HEADS, stacked, HEAD_DIM), jnp.bfloat16),
            pltpu.VMEM((KV_HEADS, stacked, HEAD_DIM), jnp.bfloat16),
            pltpu.VMEM((KV_HEADS, stacked, 1), jnp.float32),
            pltpu.VMEM((KV_HEADS, stacked, HEAD_DIM), jnp.float32),
            pltpu.VMEM((KV_HEADS, 8 * rows, HEAD_DIM), jnp.float32),
            pltpu.VMEM((KV_HEADS, 8 * rows, HEAD_DIM), jnp.float32),
        ],
        compiler_params=pltpu.CompilerParams(vmem_limit_bytes=32 * 2**20),
        cost_estimate=pl.CostEstimate(flops=10**6, bytes_accessed=10**5, transcendentals=0),
        name="attend_back",
    )(spans, queries, own, other, out, lse, grad)


TILE = 16
GU_TILES = 10
DOWN_TILES = 4
STEP = 256


def contract_last(a, w):
    return lax.dot_general(a, w, (((1,), (1,)), ((), ())), preferred_element_type=jnp.float32)


def contract_first(a, w):
    return lax.dot_general(a, w, (((0,), (0,)), ((), ())), preferred_element_type=jnp.float32)


def ff_kernel(gate_rt, up_rt, place_ref, mid_ref, gain_ref, grad_ref, target_ref, spread_ref, *refs):
    pieces, refs = refs[:10], refs[10:]
    out_ref, spread_out, act_ref, dgate_ref, dup_ref, dmid_ref, branch_ref, dgain_ref = refs[:8]
    w_scr, total_scr, back_scr, gwide_scr, sems = refs[8:]
    core = place_ref[0, 0]
    rows, width = mid_ref.shape
    half_out = DOWN_TILES * 128
    gu_rt = target_ref.shape[1] // TILE
    part = w_scr.shape[1] // 8
    copies = []
    for k in range(2):
        half = core if k == 0 else 1 - core
        spots = [(1, 0, 2), (2, 0, 2), (3, 0, 2), (4, 0, 1), (4, 1, 1)]
        for i, (n, j, parts) in enumerate(spots):
            start = (place_ref[0, n] * 2 + j) * part
            source = pieces[5 * k + i]
            target = w_scr.at[half, pl.ds(start, parts * part)]
            copies.append(pltpu.make_async_copy(source, target, sems.at[5 * k + i]))
    for copy in copies:
        copy.start()
    mid = mid_ref[...]
    scale = lax.rsqrt(jnp.mean(mid * mid, -1, keepdims=True) + EPS)
    hidden = (mid * scale * gain_ref[...]).astype(jnp.bfloat16)
    grad = grad_ref[...]
    gwide_scr[...] = jnp.zeros(gwide_scr.shape, gwide_scr.dtype)
    gwide_scr[:, :width] = grad
    total_scr[...] = jnp.zeros(total_scr.shape, jnp.float32)
    back_scr[...] = jnp.zeros(back_scr.shape, jnp.float32)
    spread_out[...] = jnp.dot(hidden, spread_ref[...], preferred_element_type=jnp.float32).astype(
        jnp.bfloat16
    )
    for copy in copies:
        copy.wait()
    kind = target_ref[...]
    gate_cols, up_first = gate_rt * TILE, up_rt * TILE
    for_gate = jnp.where(kind[:, :gate_cols] == 1, spread_out[:, :gate_cols].astype(jnp.float32), 0.0)
    for_gate = for_gate.astype(jnp.bfloat16)
    for_up = jnp.where(kind[:, up_first:] == 2, spread_out[:, up_first:].astype(jnp.float32), 0.0)
    for_up = for_up.astype(jnp.bfloat16)

    def gu_block(half, column, first, last):
        parts = [
            jnp.concatenate(
                [w_scr[half, r * GU_TILES + column + j] for r in range(first, last)], 0
            )
            for j in range(STEP // 128)
        ]
        return jnp.concatenate(parts, 1)

    def down_block(k, n):
        base = gu_rt * GU_TILES + n * (STEP // TILE * DOWN_TILES)
        parts = [
            jnp.concatenate([w_scr[k, base + r * DOWN_TILES + j] for r in range(STEP // TILE)], 0)
            for j in range(DOWN_TILES)
        ]
        return jnp.concatenate(parts, 1)

    def step(n, unused):
        half = n // (GU_TILES * 128 // STEP)
        column = n % (GU_TILES * 128 // STEP) * (STEP // 128)
        here = pl.ds(pl.multiple_of(n * STEP, STEP), STEP)
        w_gate = gu_block(half, column, 0, gate_rt)
        w_up = gu_block(half, column, up_rt, gu_rt)
        gate = jnp.dot(for_gate, w_gate, preferred_element_type=jnp.float32)
        up = jnp.dot(for_up, w_up, preferred_element_type=jnp.float32)
        sig = 1.0 / (1.0 + jnp.exp(-gate))
        silu = gate * sig
        slope = up * (sig + silu * (1.0 - sig))
        act = (silu * up).astype(jnp.bfloat16)
        act_ref[:, here] = act
        d_act = jnp.zeros((rows, STEP), jnp.float32)
        for k in range(2):
            w_down = down_block(k, n)
            cols = slice(k * half_out, (k + 1) * half_out)
            total_scr[:, cols] += jnp.dot(act, w_down, preferred_element_type=jnp.float32)
            d_act = d_act + contract_last(gwide_scr[:, cols], w_down)
        d_gate = (d_act * slope).astype(jnp.bfloat16)
        d_up = (d_act * silu).astype(jnp.bfloat16)
        dgate_ref[:, here] = d_gate
        dup_ref[:, here] = d_up
        back_gate = contract_last(d_gate, w_gate)
        back_up = contract_last(d_up, w_up)
        back_scr[:, :gate_cols] += jnp.where(kind[:, :gate_cols] == 1, back_gate, 0.0)
        back_scr[:, up_first:] += jnp.where(kind[:, up_first:] == 2, back_up, 0.0)
        return 0

    lax.fori_loop(0, 2 * GU_TILES * 128 // STEP, step, 0)
    out_ref[...] = (mid + total_scr[:, :width]).astype(jnp.bfloat16)
    back = back_scr[...]
    high = back.astype(jnp.bfloat16)
    low = (back - high.astype(jnp.float32)).astype(jnp.bfloat16)
    d_hidden = contract_last(high, spread_ref[...]) + contract_last(low, spread_ref[...])
    normed = mid * scale
    dgain_ref[...] = jnp.sum(d_hidden * normed, 0, keepdims=True)
    e = d_hidden * gain_ref[...]
    d_mid = grad.astype(jnp.float32) + scale * (e - normed * jnp.mean(e * normed, -1, keepdims=True))
    dmid_ref[...] = d_mid
    branch_ref[...] = d_mid.astype(jnp.bfloat16)


def feed_forward(core, middle, gain, grad, kind, spread, mine, other, gu_rt, gate_rt, up_rt):
    rows, width = middle.shape
    count = gu_rt * GU_TILES + FF // TILE * DOWN_TILES
    pieces = [a.reshape(-1, TILE, 128) for a in (*mine, *other)]
    padded = gu_rt * TILE
    vmem = pl.BlockSpec(memory_space=pltpu.VMEM)
    hbm = pl.BlockSpec(memory_space=pl.ANY)
    bf, f32 = jnp.bfloat16, jnp.float32
    shape = jax.ShapeDtypeStruct
    return pl.pallas_call(
        functools.partial(ff_kernel, gate_rt, up_rt),
        out_shape=(
            shape((rows, width), bf),
            shape((rows, padded), bf),
            shape((rows, FF), bf),
            shape((rows, FF), bf),
            shape((rows, FF), bf),
            shape((rows, width), f32),
            shape((rows, width), bf),
            shape((1, width), f32),
        ),
        in_specs=[pl.BlockSpec(memory_space=pltpu.SMEM)] + [vmem] * 5 + [hbm] * 10,
        out_specs=[vmem] * 8,
        scratch_shapes=[
            pltpu.VMEM((2, count, TILE, 128), bf),
            pltpu.VMEM((rows, 2 * DOWN_TILES * 128), f32),
            pltpu.VMEM((rows, padded), f32),
            pltpu.VMEM((rows, 2 * DOWN_TILES * 128), bf),
            pltpu.SemaphoreType.DMA((10,)),
        ],
        compiler_params=pltpu.CompilerParams(vmem_limit_bytes=40 * 2**20),
        cost_estimate=pl.CostEstimate(flops=10**6, bytes_accessed=10**5, transcendentals=0),
        name="feed_forward",
    )(
        core, middle, gain, grad, kind, spread, *pieces,
    )


def ff_terms_kernel(
    gate_rt, up_rt, half_ref, kind_ref, spread_ref, act_ref, dgate_ref, dup_ref, gwide_ref, out_ref
):
    half = half_ref[0, 0]
    gu_cols = GU_TILES * 128
    gu_here = pl.ds(pl.multiple_of(half * gu_cols, gu_cols), gu_cols)
    padded = spread_ref.shape[1]
    block = 256
    gu_total = padded // TILE * GU_TILES

    def put(terms, base):
        tiles_wide = terms.shape[1] // 128
        for r in range(terms.shape[0] // TILE):
            for ct in range(tiles_wide):
                tile = terms[r * TILE : (r + 1) * TILE, ct * 128 : (ct + 1) * 128]
                at = base + r * tiles_wide + ct
                out_ref[at] = tile.astype(jnp.bfloat16)

    def part(j, number, d_ref):
        here = pl.ds(pl.multiple_of(j * block, block), block)
        rows_in = jnp.where(kind_ref[:, here] == number, spread_ref[:, here].astype(jnp.float32), 0.0)
        return contract_first(rows_in.astype(jnp.bfloat16), d_ref[:, gu_here])

    def base_of(j):
        return j * (block // TILE * GU_TILES)

    mixed = (gate_rt * TILE - 1) // block

    def gate_step(j, unused):
        put(part(j, 1, dgate_ref), base_of(j))
        return 0

    def up_step(j, unused):
        put(part(j, 2, dup_ref), base_of(j))
        return 0

    lax.fori_loop(0, up_rt * TILE // block, gate_step, 0)
    for j in range(up_rt * TILE // block, mixed + 1):
        put(part(j, 1, dgate_ref) + part(j, 2, dup_ref), base_of(j))
    lax.fori_loop(mixed + 1, padded // block, up_step, 0)
    down_cols = DOWN_TILES * 128
    down_here = pl.ds(pl.multiple_of(half * down_cols, down_cols), down_cols)

    def down_step(j, unused):
        here = pl.ds(pl.multiple_of(j * STEP, STEP), STEP)
        terms = contract_first(act_ref[:, here], gwide_ref[:, down_here])
        put(terms, gu_total + j * (STEP // TILE * DOWN_TILES))
        return 0

    lax.fori_loop(0, FF // STEP, down_step, 0)


def ff_terms(half, kind, spread, act, d_gate, d_up, grad_wide, gate_rt, up_rt):
    vmem = pl.BlockSpec(memory_space=pltpu.VMEM)
    count = spread.shape[1] // TILE * GU_TILES + FF // TILE * DOWN_TILES
    operands = [kind, spread, act, d_gate, d_up, grad_wide]
    return pl.pallas_call(
        functools.partial(ff_terms_kernel, gate_rt, up_rt),
        out_shape=jax.ShapeDtypeStruct((count, TILE, 128), jnp.bfloat16),
        in_specs=[pl.BlockSpec(memory_space=pltpu.SMEM)] + [vmem] * len(operands),
        out_specs=vmem,
        compiler_params=pltpu.CompilerParams(vmem_limit_bytes=32 * 2**20),
        cost_estimate=pl.CostEstimate(flops=10**6, bytes_accessed=10**5, transcendentals=0),
        name="ff_terms",
    )(half, *operands)


def flat_wide(in_ref, out_ref, rows):
    for half in range(2):
        for rt in range(-(-rows // TILE)):
            count = min(TILE, rows - rt * TILE)
            for ct in range(GU_TILES):
                start = (rt * GU_TILES + ct) * TILE
                to = rt * TILE * 2 * GU_TILES + half * GU_TILES + ct
                out_ref[pl.ds(to, count, stride=2 * GU_TILES), :] = in_ref[
                    half, start : start + count, :
                ]


def flat_narrow(in_ref, out_ref, rows, in_start, out_start, tile):
    pairs = tile // 2
    left = lax.broadcasted_iota(jnp.int32, (pairs, 128), 1) < 64
    for rt in range(rows // tile):
        even, odd = [], []
        for ct in range(2 * DOWN_TILES):
            half, column = divmod(ct, DOWN_TILES)
            start = in_start + (rt * DOWN_TILES + column) * tile
            even.append(in_ref[half, pl.ds(start, pairs, stride=2), :])
            odd.append(pltpu.roll(in_ref[half, pl.ds(start + 1, pairs, stride=2), :], 64, 1))
        lines = even[:7] + [jnp.where(left, even[7], odd[0])]
        lines += [jnp.where(left, odd[j - 1], odd[j]) for j in range(1, 8)]
        for i, line in enumerate(lines):
            out_ref[pl.ds(out_start + 15 * pairs * rt + i, pairs, stride=15), :] = line


def ff_flat_kernel(rest, variant_ref, in_ref, out_ref):
    variant = variant_ref[0, 0]
    total = out_ref.shape[0]

    @pl.when(variant == 0)
    def gate_or_up():
        flat_wide(in_ref, out_ref, total // (2 * GU_TILES))

    @pl.when(variant == 1)
    def mixed():
        flat_wide(in_ref, out_ref, rest)
        done = rest * 2 * GU_TILES
        first = -(-rest // TILE) * TILE * GU_TILES
        flat_narrow(in_ref, out_ref, (total - done) * 2 // 15, first, done, TILE)

    @pl.when(variant == 2)
    def down():
        flat_narrow(in_ref, out_ref, total * 2 // 15, 0, 0, TILE)


def att_flat_kernel(in_ref, out_ref):
    flat_narrow(in_ref, out_ref, out_ref.shape[0] * 2 // 15, 0, 0, 8)


def flat_call(kernel, size, *operands):
    vmem = pl.BlockSpec(memory_space=pltpu.VMEM)
    smem = [pl.BlockSpec(memory_space=pltpu.SMEM)] * (len(operands) - 1)
    out = pl.pallas_call(
        kernel,
        out_shape=jax.ShapeDtypeStruct((size // 128, 128), jnp.float32),
        in_specs=smem + [vmem],
        out_specs=vmem,
        compiler_params=pltpu.CompilerParams(vmem_limit_bytes=16 * 2**20),
        cost_estimate=pl.CostEstimate(flops=10**6, bytes_accessed=10**5, transcendentals=0),
        name="flatten",
    )(*operands)
    return out.reshape(size)


def input_grad_kernel(
    x_ref, gain_ref, mid_ref, q_own, q_other, k_own, k_other, v_own, v_other, w_own, w_other, perm_ref,
    out_ref, dgain_ref,
):
    rows, width = x_ref.shape
    third = width // 3
    x = x_ref[...].astype(jnp.float32)
    scale = lax.rsqrt(jnp.mean(x * x, -1, keepdims=True) + EPS)
    normed = x * scale
    cut_v = width + third

    def back(own, other, start, stop):
        return contract_last(own[...], w_own[start:stop, :]) + contract_last(
            other[...], w_other[start:stop, :]
        )

    three = back(k_own, k_other, width, cut_v) + back(v_own, v_other, cut_v, cut_v + third)
    three = jnp.concatenate([three[q * rows : (q + 1) * rows] for q in range(3)], 1)
    high = three.astype(jnp.bfloat16)
    low = (three - high.astype(jnp.float32)).astype(jnp.bfloat16)
    d_hidden = back(q_own, q_other, 0, width)
    d_hidden = d_hidden + contract_last(high, perm_ref[...]) + contract_last(low, perm_ref[...])
    dgain_ref[...] = jnp.sum(d_hidden * normed, 0, keepdims=True)
    e = d_hidden * gain_ref[...]
    out_ref[...] = mid_ref[...] + scale * (e - normed * jnp.mean(e * normed, -1, keepdims=True))


def input_grad(x, gain, d_mid, q_halves, k_halves, v_halves, weights, perm):
    rows, width = x.shape
    vmem = pl.BlockSpec(memory_space=pltpu.VMEM)
    return pl.pallas_call(
        input_grad_kernel,
        out_shape=(
            jax.ShapeDtypeStruct((rows, width), jnp.float32),
            jax.ShapeDtypeStruct((1, width), jnp.float32),
        ),
        in_specs=[vmem] * 12,
        out_specs=(vmem, vmem),
        compiler_params=pltpu.CompilerParams(vmem_limit_bytes=28 * 2**20),
        cost_estimate=pl.CostEstimate(flops=10**6, bytes_accessed=10**5, transcendentals=0),
        name="input_grad",
    )(x, gain, d_mid, *q_halves, *k_halves, *v_halves, *weights, perm)


BF = jnp.bfloat16
F32 = jnp.float32
LANES = 128
GU_PAD = 96
X_PAIRS = [(j, j ^ 1) for j in range(4)]
Y_PAIRS = [(j, j ^ 2) for j in range(4)]
CORE_PAIRS = [(j, j ^ 1) for j in range(8)]
LINES = [[0, 2, 4, 6], [1, 3, 5, 7]]
EXTRA = 2


def up_pairs(first, last):
    return [(2 * z + c, 2 * z + 2 + c) for z in range(first, last) for c in range(2)]


def down_pairs(first, last):
    return [(2 * z + 2 + c, 2 * z + c) for z in range(first, last) for c in range(2)]


def swap_x(a):
    return lax.ppermute(a, "batch", X_PAIRS)


def swap_y(a):
    return lax.ppermute(a, "batch", Y_PAIRS)


def swap_core(a):
    return lax.ppermute(a, "ctx", CORE_PAIRS)


def tiles(a):
    rows, cols = a.shape
    a = a.reshape(rows // 8, 8, cols // LANES, LANES)
    return a.transpose(0, 2, 1, 3).reshape(rows * cols // (8 * LANES), 8, LANES)


def untile(a, cols):
    rows = a.shape[0] * 8 * LANES // cols
    a = a.reshape(rows // 8, cols // LANES, 8, LANES)
    return a.transpose(0, 2, 1, 3).reshape(rows, cols)


def pad_to(a, rows, cols):
    return jnp.pad(a, ((0, rows - a.shape[0]), (0, cols - a.shape[1])))


def halves_of(a):
    half = a.shape[1] // 2
    return jnp.stack([tiles(a[:, :half]), tiles(a[:, half:])])


def deep_halves_of(a):
    rows, cols = a.shape
    a = a.reshape(rows // TILE, TILE, 2, cols // (2 * LANES), LANES)
    return a.transpose(2, 0, 3, 1, 4).reshape(2, rows * cols // (2 * LANES), LANES)


def gather_line(a, z, before_last=lambda parts: parts):
    u1 = lax.ppermute(a, "ctx", up_pairs(0, 3))
    d1 = lax.ppermute(a, "ctx", down_pairs(0, 3))
    u2 = lax.ppermute(u1, "ctx", up_pairs(1, 3))
    d2 = lax.ppermute(d1, "ctx", down_pairs(0, 2))
    u2, d2 = before_last((u2, d2))
    u3 = lax.ppermute(u2, "ctx", up_pairs(2, 3))
    d3 = lax.ppermute(d2, "ctx", down_pairs(0, 1))
    seven = jnp.stack([u3, u2, u1, a, d1, d2, d3])
    return lax.dynamic_slice_in_dim(seven, 3 - z, 4, 0)


def line_pairs(hops):
    return [(2 * z + c, 2 * (z + hops) + c) for z in range(4) for c in range(2) if 0 <= z + hops < 4]


def gather_direct(a, z):
    got = {k: lax.ppermute(a, "ctx", line_pairs(k)) for k in (1, -1, 2, -2, 3, -3)}
    seven = jnp.stack([got[3], got[2], got[1], a, got[-1], got[-2], got[-3]])
    return lax.dynamic_slice_in_dim(seven, 3 - z, 4, 0)


def send_line(t, z, hops):
    out = []
    for k in hops:
        block = lax.dynamic_index_in_dim(t, jnp.clip(z + k, 0, 3), 0, keepdims=False)
        out.append(lax.ppermute(block, "ctx", line_pairs(k)))
    return out


def sum_line(t, z, got):
    total = lax.dynamic_index_in_dim(t, z, 0, keepdims=False).astype(F32)
    for k, block in got:
        total = total + jnp.where((z - k >= 0) & (z - k < 4), block.astype(F32), 0.0)
    return total


def scatter_direct(t, z):
    hops = (3, -3, 2, -2, 1, -1)
    return sum_line(t, z, zip(hops, send_line(t, z, hops)))


def gather_near(a):
    return swap_x(a), swap_y(a)


def gather_far(from_x, from_y):
    return swap_y(from_x[:2]), swap_x(from_y[2:])


def place(pieces, b, start, stop):
    shape = pieces[0][2].shape
    whole = jnp.zeros((4, 4, shape[1], stop - start) + shape[3:], BF)
    for step, row, piece in pieces:
        whole = lax.dynamic_update_slice(
            whole, piece[None, :, :, start:stop], (b ^ step, row) + (0,) * (len(shape) - 1)
        )
    return whole


def add(*terms):
    total = terms[0].astype(F32)
    for term in terms[1:]:
        total = total + term.astype(F32)
    return total.astype(BF)


def scatter_blocks(arrays, b):
    return [
        [lax.dynamic_index_in_dim(a, b ^ k, 0, keepdims=False) for a in arrays] for k in range(4)
    ]


def scatter_far(terms):
    return add(*(t[:2] for t in terms)), add(*(t[2:] for t in terms))


def scatter_near(blocks, far_x, far_y):
    xs, ys = blocks[1], blocks[2]
    x_parts = add(*(t[:2] for t in xs)), add(*(t[2:] for t in xs), far_y)
    y_parts = add(*(t[:2] for t in ys), far_x), add(*(t[2:] for t in ys))
    return swap_x(jnp.concatenate(x_parts, 0)), swap_y(jnp.concatenate(y_parts, 0))


def split_high(a, parts):
    out = []
    for unused in range(parts):
        high = lax.reduce_precision(a, 8, 7)
        out.append(high.astype(BF))
        a = a - high
    return out


def local_block(tokens, attention_weights, feedforward_weights, norm_gains, span_order, cotangent):
    rows_here = tokens.shape[1]
    halves = rows_here // 2
    width_q = HEADS * HEAD_DIM
    width_kv = KV_HEADS * HEAD_DIM
    wide = 2 * 512
    b = lax.axis_index("batch")
    place_ctx = lax.axis_index("ctx")
    z = place_ctx // 2
    c = place_ctx % 2
    device = b * 8 + place_ctx
    own_gain = D // 8

    def pick(first, second):
        return jnp.where(c == 0, first, second)

    def merge(mine, other):
        return pick(
            jnp.concatenate([mine, other], -1), jnp.concatenate([other, mine], -1)
        )

    def half_of(a, k):
        half = a.shape[-1] // 2
        return jnp.where((c ^ k) == 0, a[..., :half], a[..., half:])

    def pair_up(shard):
        mine = pick(shard[0], shard[1])
        other = swap_core(pick(shard[1], shard[0]))
        return pick(jnp.stack([mine, other]), jnp.stack([other, mine]))

    att_rows = attention_weights.shape[0] // D
    att_shard = halves_of(pad_to(attention_weights.reshape(att_rows, D), att_rows, wide))
    gain_parts = jnp.stack(split_high(norm_gains, 3), 1)
    gain_rows = jnp.pad(gain_parts, ((0, 0), (0, 8 * EXTRA - 3), (0, LANES - own_gain)))
    gain_rows = gain_rows.reshape(2, EXTRA, 8, LANES)
    att_chip = pair_up(jnp.concatenate([att_shard, gain_rows], 1))
    att_line = gather_direct(att_chip, z)

    gu_rows = feedforward_weights.shape[0] // FF
    down_rows = feedforward_weights.shape[0] // D
    mixed = 2 * D // gu_rows
    rest = 2 * D - mixed * gu_rows
    rest_pad = -(-rest // TILE) * TILE
    gu_shard = deep_halves_of(pad_to(feedforward_weights.reshape(gu_rows, FF), GU_PAD, FF))
    down_shard = deep_halves_of(pad_to(feedforward_weights.reshape(down_rows, D), down_rows, wide))
    mixed_down = pad_to(
        feedforward_weights[rest * FF :].reshape(-1, D), down_rows - rest * FF // D, wide
    )
    mixed_shard = jnp.concatenate(
        [
            deep_halves_of(
                pad_to(feedforward_weights[: rest * FF].reshape(rest, FF), rest_pad, FF)
            ),
            deep_halves_of(mixed_down),
        ],
        1,
    )
    ff_shard = jnp.where(device < mixed, gu_shard, jnp.where(device == mixed, mixed_shard, down_shard))
    ff_body = ff_shard.shape[1]
    ff_chip, att_line = lax.optimization_barrier((pair_up(ff_shard), att_line))
    ff_line = gather_line(ff_chip, z)
    ff_line_other = swap_core(ff_line)

    att_x, att_y = gather_near(att_line)
    gu_total = mixed * GU_PAD + rest_pad
    pad_row = jnp.arange(gu_total, dtype=jnp.int32)
    true_row = pad_row // GU_PAD * gu_rows + pad_row % GU_PAD
    real = pad_row % GU_PAD < gu_rows
    is_gate = real & (true_row < D)
    is_up = real & (true_row >= D)
    spread = ((true_row % D)[None, :] == jnp.arange(D, dtype=jnp.int32)[:, None]) & real[None, :]
    spread = spread.astype(BF)
    third = D // 3
    order3 = jnp.arange(D, dtype=jnp.int32)
    perm3 = (order3[:, None] == (order3 % third * 3 + order3 // third)[None, :]).astype(BF)

    att_first, att_second = gather_far(att_x, att_y)
    att_pieces = (
        (0, 0, att_line), (1, 0, att_x), (2, 0, att_y), (3, 0, att_first), (3, 2, att_second)
    )
    att_body = att_rows * wide // (2 * 8 * LANES)
    att_mine = place(att_pieces, b, 0, att_body).reshape(-1, 8, LANES)
    gain_mine = place(att_pieces, b, att_body, att_body + EXTRA)
    att_other = swap_core(att_mine)
    gain_other = swap_core(gain_mine)

    def gain_from(a):
        parts = a[0, :, :, 0, :3, :own_gain].astype(F32)
        return (parts[:, :, 0] + parts[:, :, 1] + parts[:, :, 2]).reshape(D)

    gain_m, gain_o = gain_from(gain_mine), gain_from(gain_other)
    gain_full = jnp.stack([pick(gain_m, gain_o), pick(gain_o, gain_m)])


    offsets = jnp.arange(halves, dtype=jnp.int32)
    query_pos = (span_order[0][:, None] * halves + offsets[None, :]).reshape(rows_here)
    cos_table, sin_table = rope_tables(query_pos)

    inputs = tokens[0].astype(F32)
    hidden = normalize(inputs, gain_full[0]).astype(BF)
    hidden3 = jnp.dot(hidden, perm3, preferred_element_type=F32).astype(BF)
    hidden3 = hidden3.reshape(rows_here, 3, third)
    att_m, att_o = untile(att_mine, wide // 2), untile(att_other, wide // 2)
    cut_k, cut_v, cut_o = D, D + third, D + 2 * third

    def project(a, start, stop):
        return merge(
            jnp.dot(a, att_m[start:stop], preferred_element_type=F32),
            jnp.dot(a, att_o[start:stop], preferred_element_type=F32),
        )

    def thirds(start, stop):
        out = project(hidden3.transpose(1, 0, 2).reshape(3 * rows_here, third), start, stop)
        out = out.reshape(3, rows_here, wide)
        return out[0, :, :third] + out[1, :, third : 2 * third] + out[2, :, 2 * third : 3 * third]

    query_raw = project(hidden, 0, D)[:, :width_q].reshape(rows_here, HEADS, HEAD_DIM)
    key_raw = thirds(cut_k, cut_v).reshape(rows_here, KV_HEADS, HEAD_DIM)
    values = thirds(cut_v, cut_o).astype(BF)
    query_rot, query_pull = jax.vjp(lambda a: rotate(a, cos_table, sin_table), query_raw)
    key_rot, key_pull = jax.vjp(lambda a: rotate(a, cos_table, sin_table), key_raw)
    queries = query_rot.astype(BF).reshape(rows_here, width_q)
    keys = key_rot.astype(BF).reshape(rows_here, width_kv)

    span_rows = jnp.pad(span_order.astype(BF), ((0, 15), (0, 2 * width_kv - 2)))
    key_value = jnp.concatenate([jnp.concatenate([keys, values], 1), span_rows], 0)
    ff_near = gather_near(ff_line)
    waited = []

    def wait_for_near(parts):
        near, parts = lax.optimization_barrier((ff_near, parts))
        waited.append(near)
        return parts

    line_mine = gather_line(key_value, z, wait_for_near)
    ff_near = waited[0]
    line_mine, queries, spread = lax.optimization_barrier((line_mine, queries, spread))
    line_other = swap_core(line_mine)
    ff_far = gather_far(*ff_near)
    spans = jnp.stack([line_mine[:, rows_here, :2], line_other[:, rows_here, :2]]).astype(jnp.int32)
    spans = jnp.concatenate([spans, jnp.broadcast_to(span_order[None], (2, 1, 2))], 1)
    attended, log_total = attend(spans, queries, line_mine, line_other)
    ff_far, attended = lax.optimization_barrier((ff_far, attended))
    ff_mine = (ff_line, *ff_near, *ff_far)
    ff_other = (ff_line_other, *(swap_core(piece) for piece in ff_mine[1:]))
    attended_low = attended.astype(BF)
    middle = inputs + project(attended_low, cut_o, cut_o + D)[:, :D]
    gate_end = -(-D // gu_rows) * GU_PAD
    up_start = D // gu_rows * GU_PAD
    grad_wide = jnp.pad(cotangent[0], ((0, 0), (0, wide - D)))
    kind = (is_gate.astype(jnp.int32) + 2 * is_up.astype(jnp.int32))[None]
    result, spread_two, activ, grad_gate, grad_upward, grad_middle, grad_branch, grad_gain_two = (
        feed_forward(
            jnp.stack([c, b, b ^ 1, b ^ 2, b ^ 3])[None], middle, gain_full[1:2], cotangent[0], kind, spread,
            ff_mine, ff_other,
            gu_total // TILE, gate_end // TILE, up_start // TILE,
        )
    )
    grad_gain_two = grad_gain_two[0]

    def times_transposed(a, w):
        return lax.dot_general(a, w, (((1,), (1,)), ((), ())), preferred_element_type=F32)

    def transposed_times(a, w):
        return lax.dot_general(a, w, (((0,), (0,)), ((), ())), preferred_element_type=F32)

    def terms_of_half(half, rows_in):
        return ff_terms(
            half.reshape(1, 1), kind, rows_in, activ, grad_gate, grad_upward, grad_wide,
            gate_end // TILE, up_start // TILE,
        )

    ff_send, spread_two, grad_branch = lax.optimization_barrier(
        (terms_of_half(1 - c, spread_two), spread_two, grad_branch)
    )
    ff_from = swap_core(ff_send)
    ff_keep = terms_of_half(c, spread_two)
    ff_blocks = scatter_blocks(
        [a.reshape(4, 4, 2, ff_body, LANES) for a in (ff_keep, ff_from)], b
    )
    branch_wide = jnp.pad(grad_branch, ((0, 0), (0, wide - D)))

    def project_back(a, start, stop):
        return times_transposed(half_of(a, 0), att_m[start:stop]) + times_transposed(
            half_of(a, 1), att_o[start:stop]
        )

    grad_attended = project_back(branch_wide, cut_o, cut_o + D).astype(BF)
    ff_far, grad_attended = lax.optimization_barrier((scatter_far(ff_blocks[3]), grad_attended))
    ff_far = swap_x(ff_far[0]), swap_y(ff_far[1])
    grad_query_rot, both_mine, both_other = attend_back(
        spans, queries, line_mine, line_other, attended, log_total, grad_attended
    )
    ff_far, both_other = lax.optimization_barrier((ff_far, both_other))
    both_from = swap_core(both_other)
    ff_near = scatter_near(ff_blocks, *ff_far)
    both_own = scatter_direct(add(both_mine, both_from), z)
    ff_line_sum, both_own = lax.optimization_barrier((add(*ff_blocks[0], *ff_near), both_own))
    ff_own = lax.psum_scatter(
        ff_line_sum, "ctx", scatter_dimension=0, axis_index_groups=LINES, tiled=True
    )[0].astype(F32)
    grad_key_rot, grad_value_f = both_own[:, :width_kv], both_own[:, width_kv:]
    grad_query_raw = query_pull(grad_query_rot.reshape(rows_here, HEADS, HEAD_DIM))[0]
    grad_key_raw = key_pull(grad_key_rot.reshape(rows_here, KV_HEADS, HEAD_DIM))[0]
    grad_query = grad_query_raw.reshape(rows_here, width_q).astype(BF)
    grad_key = grad_key_raw.reshape(rows_here, width_kv).astype(BF)
    grad_value = grad_value_f.astype(BF)

    def spots(a):
        return jnp.concatenate(
            [jnp.pad(a, ((0, 0), (q * third, wide - (q + 1) * third))) for q in range(3)], 0
        )

    query_wide = jnp.pad(grad_query, ((0, 0), (0, wide - D)))
    key_spots, value_spots = spots(grad_key), spots(grad_value)
    hidden_rows = hidden3.transpose(1, 0, 2).reshape(3 * rows_here, third)
    def att_terms(k):
        terms = jnp.concatenate(
            [
                transposed_times(hidden, half_of(query_wide, k)).astype(BF),
                transposed_times(hidden_rows, half_of(key_spots, k)).astype(BF),
                transposed_times(hidden_rows, half_of(value_spots, k)).astype(BF),
                transposed_times(attended_low, half_of(branch_wide, k)).astype(BF),
            ],
            0,
        )
        return tiles(terms).reshape(4, 4, 2, att_body, 8, LANES)

    grad_inputs, grad_gain_one = input_grad(
        tokens[0], gain_full[:1], grad_middle,
        *([half_of(a, k) for k in range(2)] for a in (query_wide, key_spots, value_spots)),
        (att_m, att_o), perm3,
    )
    att_from = swap_core(att_terms(1))
    att_from, grad_inputs, grad_gain_one = lax.optimization_barrier(
        (att_from, grad_inputs, grad_gain_one)
    )
    att_blocks = scatter_blocks((att_terms(0), att_from), b)
    att_far = scatter_far(att_blocks[3])
    att_far = swap_x(att_far[0]), swap_y(att_far[1])
    gain_terms = jnp.stack([grad_gain_one[0], grad_gain_two])
    gain_terms = gain_terms + swap_core(gain_terms)
    gain_terms = gain_terms + swap_x(gain_terms)
    gain_terms = gain_terms + swap_y(gain_terms)
    att_far, gain_terms = lax.optimization_barrier((att_far, gain_terms))
    att_near = scatter_near(att_blocks, *att_far)
    gain_terms = pick(gain_terms[0], gain_terms[1]).reshape(8, own_gain)
    gain_terms = jnp.pad(
        jnp.stack(split_high(gain_terms, 2), 1),
        ((0, 0), (0, 8 * EXTRA - 2), (0, LANES - own_gain)),
    ).reshape(4, 2, EXTRA, 8, LANES)

    def settle(own):
        mine = pick(own[0], own[1])
        other = swap_core(pick(own[1], own[0]))
        return pick(jnp.stack([mine, other]), jnp.stack([other, mine]))

    ff_done = settle(ff_own)
    variant = jnp.where(device < mixed, 0, jnp.where(device == mixed, 1, 2)).astype(jnp.int32)
    ff_flat = flat_call(
        functools.partial(ff_flat_kernel, rest), feedforward_weights.shape[0],
        variant.reshape(1, 1), ff_done,
    )
    ff_flat, att_near = lax.optimization_barrier((ff_flat, att_near))
    att_sum = jnp.concatenate([add(*att_blocks[0], *att_near), gain_terms], 2)
    att_own = scatter_direct(att_sum, z)
    att_done = settle(att_own)
    gain_own = att_done[:, att_body, 0, :own_gain] + att_done[:, att_body, 1, :own_gain]
    att_flat = flat_call(
        att_flat_kernel, attention_weights.shape[0], att_done.reshape(2, -1, LANES)
    )
    return (
        result[None],
        grad_inputs[None],
        att_flat,
        ff_flat,
        gain_own,
    )


def solution(mesh):
    fits = mesh.shape["batch"] == 4 and mesh.shape["ctx"] == 8
    local = local_block if fits else local_any
    placed = (
        P("batch", "ctx", None),
        P(("batch", "ctx")),
        P(("batch", "ctx")),
        P(None, "ctx"),
        P("batch", "ctx"),
        P("batch", "ctx", None),
    )
    return jax.shard_map(
        local,
        mesh=mesh,
        in_specs=placed,
        out_specs=(
            P("batch", "ctx", None),
            P("batch", "ctx", None),
            P(("batch", "ctx")),
            P(("batch", "ctx")),
            P(None, "ctx"),
        ),
        check_vma=False,
    )
```

```python
import functools
import math

import jax
import jax.numpy as jnp
from jax import lax
from jax.experimental import pallas as pl
from jax.experimental.pallas import tpu as pltpu
from jax.sharding import PartitionSpec as P

D = 960
HEADS = 15
KV_HEADS = 5
HEAD_DIM = 64
FF = 2560


ROPE_BASE = 100000.0
EPS = 1e-05
NEG = -1e30


def normalize(values, gain):
    return values * lax.rsqrt(jnp.mean(values * values, -1, keepdims=True) + EPS) * gain


def swiglu(gate, upward):
    return jax.nn.silu(gate) * upward


def rope_tables(positions):
    halves = HEAD_DIM // 2
    inverse_freq = ROPE_BASE ** (-jnp.arange(halves, dtype=jnp.float32) / halves)
    angles = positions.astype(jnp.float32)[:, None] * inverse_freq[None, :]
    return (jnp.cos(angles), jnp.sin(angles))


def rotate(values, cos_table, sin_table):
    halves = HEAD_DIM // 2
    first = values[..., :halves]
    second = values[..., halves:]
    cos_table = cos_table[:, None, :]
    sin_table = sin_table[:, None, :]
    return jnp.concatenate(
        [first * cos_table - second * sin_table, second * cos_table + first * sin_table], -1
    )


def split_flat(flat, shapes):
    pieces = []
    offset = 0
    for rows_in, cols_in in shapes:
        pieces.append(flat[offset : offset + rows_in * cols_in].reshape(rows_in, cols_in))
        offset += rows_in * cols_in
    return pieces


def unpack(att_flat, ff_flat):
    width_q = HEADS * HEAD_DIM
    width_kv = KV_HEADS * HEAD_DIM
    att_parts = split_flat(att_flat, [(D, width_q), (D, width_kv), (D, width_kv), (width_q, D)])
    ff_parts = split_flat(ff_flat, [(D, FF), (D, FF), (FF, D)])
    return (att_parts, ff_parts)


def score_block(queries, key_block, query_pos, key_pos):
    keys_three = key_block.reshape(key_block.shape[0], KV_HEADS, HEAD_DIM)
    scores = jnp.einsum(
        "qhgd,khd->hgqk", queries, keys_three, preferred_element_type=jnp.float32
    ) * HEAD_DIM ** (-0.5)
    visible = key_pos[None, None, None, :] <= query_pos[None, None, :, None]
    return (scores, visible)


def attention_forward(queries, key_all, value_all, query_pos, key_pos, block):
    rows_here = queries.shape[0]
    group = HEADS // KV_HEADS
    count = key_all.shape[0] // block
    key_blocks = key_all.reshape(count, block, key_all.shape[1])
    value_blocks = value_all.reshape(count, block, value_all.shape[1])
    pos_blocks = key_pos.reshape(count, block)

    def online_step(carry, item):
        top, total, accum = carry
        key_block, value_block, pos_block = item
        scores, visible = score_block(queries, key_block, query_pos, pos_block)
        scores = jnp.where(visible, scores, NEG)
        new_top = jnp.maximum(top, jnp.max(scores, -1))
        weights = jnp.where(visible, jnp.exp(scores - new_top[..., None]), 0.0)
        factor = jnp.exp(top - new_top)
        total = total * factor + jnp.sum(weights, -1)
        values_three = value_block.reshape(block, KV_HEADS, HEAD_DIM)
        accum = accum * jnp.transpose(factor, (2, 0, 1))[..., None]
        accum = accum + jnp.einsum(
            "hgqk,khd->qhgd",
            weights.astype(jnp.bfloat16),
            values_three,
            preferred_element_type=jnp.float32,
        )
        return ((new_top, total, accum), None)

    start_top = jnp.full((KV_HEADS, group, rows_here), NEG, jnp.float32)
    start_total = jnp.zeros((KV_HEADS, group, rows_here), jnp.float32)
    start_out = jnp.zeros((rows_here, KV_HEADS, group, HEAD_DIM), jnp.float32)
    (top, total, accum), unused = lax.scan(
        online_step, (start_top, start_total, start_out), (key_blocks, value_blocks, pos_blocks)
    )
    log_total = top + jnp.log(total)
    attended = accum / jnp.transpose(total, (2, 0, 1))[..., None]
    return (attended, log_total)


def attention_backward(
    queries, key_all, value_all, query_pos, key_pos, block, log_total, grad_out, attended
):
    rows_here = queries.shape[0]
    group = HEADS // KV_HEADS
    width_kv = key_all.shape[1]
    count = key_all.shape[0] // block
    items = (
        key_all.reshape(count, block, width_kv),
        value_all.reshape(count, block, width_kv),
        key_pos.reshape(count, block),
    )
    delta = jnp.transpose(jnp.sum(grad_out.astype(jnp.float32) * attended, -1), (1, 2, 0))

    def grad_step(grad_query, item):
        key_block, value_block, pos_block = item
        scores, visible = score_block(queries, key_block, query_pos, pos_block)
        probs = jnp.where(visible, jnp.exp(scores - log_total[..., None]), 0.0)
        values_three = value_block.reshape(block, KV_HEADS, HEAD_DIM)
        grad_probs = jnp.einsum(
            "qhgd,khd->hgqk", grad_out, values_three, preferred_element_type=jnp.float32
        )
        grad_scores = (probs * (grad_probs - delta[..., None])).astype(jnp.bfloat16)
        keys_three = key_block.reshape(block, KV_HEADS, HEAD_DIM)
        grad_query = grad_query + jnp.einsum(
            "hgqk,khd->qhgd", grad_scores, keys_three, preferred_element_type=jnp.float32
        )
        grad_key = jnp.einsum(
            "hgqk,qhgd->khd", grad_scores, queries, preferred_element_type=jnp.float32
        )
        grad_value = jnp.einsum(
            "hgqk,qhgd->khd",
            probs.astype(jnp.bfloat16),
            grad_out,
            preferred_element_type=jnp.float32,
        )
        return (
            grad_query,
            (grad_key.reshape(block, width_kv), grad_value.reshape(block, width_kv)),
        )

    start_query = jnp.zeros((rows_here, KV_HEADS, group, HEAD_DIM), jnp.float32)
    grad_query, (grad_keys, grad_values) = lax.scan(grad_step, start_query, items)
    return (
        grad_query,
        grad_keys.reshape(count * block, width_kv),
        grad_values.reshape(count * block, width_kv),
    )


def local_any(tokens, attention_weights, feedforward_weights, norm_gains, span_order, cotangent):
    ctx_count = lax.axis_size("ctx")
    batch_count = lax.axis_size("batch")
    rows_here = tokens.shape[1]
    halves = rows_here // 2
    length = rows_here * ctx_count
    group = HEADS // KV_HEADS
    width_q = HEADS * HEAD_DIM
    width_kv = KV_HEADS * HEAD_DIM
    block = math.gcd(length, 512)
    scaling = HEAD_DIM ** (-0.5)
    att_full, ff_full = (
        lax.all_gather(attention_weights, ("batch", "ctx"), axis=0, tiled=True),
        lax.all_gather(feedforward_weights, ("batch", "ctx"), axis=0, tiled=True),
    )
    gain_full = lax.all_gather(norm_gains, "ctx", axis=1, tiled=True)
    order_full = lax.all_gather(span_order, "ctx", axis=1, tiled=True)
    offsets = jnp.arange(halves, dtype=jnp.int32)
    key_pos = (order_full[0][:, None] * halves + offsets[None, :]).reshape(length)
    query_pos = (span_order[0][:, None] * halves + offsets[None, :]).reshape(rows_here)
    cos_table, sin_table = rope_tables(query_pos)
    (w_query, w_key, w_value, w_out), (w_gate, w_up, w_down) = unpack(att_full, ff_full)
    inputs = tokens[0].astype(jnp.float32)
    hidden_f, norm_one_pull = jax.vjp(normalize, inputs, gain_full[0])
    hidden = hidden_f.astype(jnp.bfloat16)
    query_raw = jnp.dot(hidden, w_query, preferred_element_type=jnp.float32).reshape(
        rows_here, HEADS, HEAD_DIM
    )
    key_raw = jnp.dot(hidden, w_key, preferred_element_type=jnp.float32).reshape(
        rows_here, KV_HEADS, HEAD_DIM
    )
    values = jnp.dot(hidden, w_value, preferred_element_type=jnp.float32).astype(jnp.bfloat16)
    query_rot, query_pull = jax.vjp(lambda a: rotate(a, cos_table, sin_table), query_raw)
    key_rot, key_pull = jax.vjp(lambda a: rotate(a, cos_table, sin_table), key_raw)
    queries = query_rot.astype(jnp.bfloat16).reshape(rows_here, KV_HEADS, group, HEAD_DIM)
    keys = key_rot.astype(jnp.bfloat16).reshape(rows_here, width_kv)
    key_all, value_all = (
        lax.all_gather(keys, "ctx", axis=0, tiled=True),
        lax.all_gather(values, "ctx", axis=0, tiled=True),
    )
    attended, log_total = attention_forward(queries, key_all, value_all, query_pos, key_pos, block)
    attended_low = attended.reshape(rows_here, width_q).astype(jnp.bfloat16)
    middle = inputs + jnp.dot(attended_low, w_out, preferred_element_type=jnp.float32)
    hidden_two_f, norm_two_pull = jax.vjp(normalize, middle, gain_full[1])
    hidden_two = hidden_two_f.astype(jnp.bfloat16)
    gate = jnp.dot(hidden_two, w_gate, preferred_element_type=jnp.float32)
    upward = jnp.dot(hidden_two, w_up, preferred_element_type=jnp.float32)
    activ_f, swiglu_pull = jax.vjp(swiglu, gate, upward)
    activ = activ_f.astype(jnp.bfloat16)
    result = middle + jnp.dot(activ, w_down, preferred_element_type=jnp.float32)
    grad_result = cotangent[0]
    grad_down = jnp.einsum("tf,td->fd", activ, grad_result, preferred_element_type=jnp.float32)
    grad_activ = jnp.einsum("td,fd->tf", grad_result, w_down, preferred_element_type=jnp.float32)
    grad_gate_f, grad_up_f = swiglu_pull(grad_activ)
    grad_gate = grad_gate_f.astype(jnp.bfloat16)
    grad_upward = grad_up_f.astype(jnp.bfloat16)
    grad_w_gate = jnp.einsum("td,tf->df", hidden_two, grad_gate, preferred_element_type=jnp.float32)
    grad_w_up = jnp.einsum("td,tf->df", hidden_two, grad_upward, preferred_element_type=jnp.float32)
    grad_hidden_two = jnp.einsum("tf,df->td", grad_gate, w_gate, preferred_element_type=jnp.float32)
    grad_hidden_two = grad_hidden_two + jnp.einsum(
        "tf,df->td", grad_upward, w_up, preferred_element_type=jnp.float32
    )
    grad_middle_norm, grad_gain_two = norm_two_pull(grad_hidden_two)
    grad_middle = grad_result.astype(jnp.float32) + grad_middle_norm
    grad_branch = grad_middle.astype(jnp.bfloat16)
    grad_w_out = jnp.einsum(
        "tq,td->qd", attended_low, grad_branch, preferred_element_type=jnp.float32
    )
    grad_attended = jnp.einsum(
        "td,qd->tq", grad_branch, w_out, preferred_element_type=jnp.float32
    ).astype(jnp.bfloat16)
    grad_attended = grad_attended.reshape(rows_here, KV_HEADS, group, HEAD_DIM)
    grad_query_rot, grad_key_all, grad_value_all = attention_backward(
        queries, key_all, value_all, query_pos, key_pos, block, log_total, grad_attended, attended
    )
    grad_key_rot, grad_value_f = (
        lax.psum_scatter(
            grad_key_all.astype(jnp.bfloat16), "ctx", scatter_dimension=0, tiled=True
        ).astype(jnp.float32),
        lax.psum_scatter(
            grad_value_all.astype(jnp.bfloat16), "ctx", scatter_dimension=0, tiled=True
        ).astype(jnp.float32),
    )
    grad_query_raw = query_pull(grad_query_rot.reshape(rows_here, HEADS, HEAD_DIM) * scaling)[0]
    grad_key_raw = key_pull(grad_key_rot.reshape(rows_here, KV_HEADS, HEAD_DIM) * scaling)[0]
    grad_query = grad_query_raw.reshape(rows_here, width_q).astype(jnp.bfloat16)
    grad_key = grad_key_raw.reshape(rows_here, width_kv).astype(jnp.bfloat16)
    grad_value = grad_value_f.astype(jnp.bfloat16)
    grad_w_query = jnp.einsum("td,tq->dq", hidden, grad_query, preferred_element_type=jnp.float32)
    grad_w_key = jnp.einsum("td,tq->dq", hidden, grad_key, preferred_element_type=jnp.float32)
    grad_w_value = jnp.einsum("td,tq->dq", hidden, grad_value, preferred_element_type=jnp.float32)
    grad_hidden = jnp.einsum("tq,dq->td", grad_query, w_query, preferred_element_type=jnp.float32)
    grad_hidden = grad_hidden + jnp.einsum(
        "tq,dq->td", grad_key, w_key, preferred_element_type=jnp.float32
    )
    grad_hidden = grad_hidden + jnp.einsum(
        "tq,dq->td", grad_value, w_value, preferred_element_type=jnp.float32
    )
    grad_inputs_norm, grad_gain_one = norm_one_pull(grad_hidden)
    grad_inputs = grad_middle + grad_inputs_norm
    grad_att_flat = jnp.concatenate(
        [
            grad_w_query.reshape(-1),
            grad_w_key.reshape(-1),
            grad_w_value.reshape(-1),
            grad_w_out.reshape(-1),
        ]
    )
    grad_ff_flat = jnp.concatenate(
        [grad_w_gate.reshape(-1), grad_w_up.reshape(-1), grad_down.reshape(-1)]
    )
    width_own = D // ctx_count
    gain_terms = jnp.stack([grad_gain_one, grad_gain_two]).reshape(2, ctx_count, width_own)
    gain_terms = jnp.transpose(gain_terms, (1, 0, 2)).reshape(ctx_count, 2 * width_own)
    gain_terms = jnp.broadcast_to(
        gain_terms[None], (batch_count, ctx_count, 2 * width_own)
    ).reshape(batch_count * ctx_count, 2 * width_own)
    att_part, ff_part, gain_part = (
        lax.psum_scatter(
            grad_att_flat.astype(jnp.bfloat16), "batch", scatter_dimension=0, tiled=True
        ).astype(jnp.float32),
        lax.psum_scatter(
            grad_ff_flat.astype(jnp.bfloat16), "batch", scatter_dimension=0, tiled=True
        ).astype(jnp.float32),
        lax.psum_scatter(
            gain_terms.astype(jnp.bfloat16), "batch", scatter_dimension=0, tiled=True
        ).astype(jnp.float32),
    )
    grad_att_own, grad_ff_own, gain_own = (
        lax.psum_scatter(
            att_part.astype(jnp.bfloat16), "ctx", scatter_dimension=0, tiled=True
        ).astype(jnp.float32),
        lax.psum_scatter(
            ff_part.astype(jnp.bfloat16), "ctx", scatter_dimension=0, tiled=True
        ).astype(jnp.float32),
        lax.psum_scatter(
            gain_part.astype(jnp.bfloat16), "ctx", scatter_dimension=0, tiled=True
        ).astype(jnp.float32),
    )
    grad_gain_own = gain_own.reshape(2, width_own)
    return (
        result.astype(jnp.bfloat16)[None],
        grad_inputs[None],
        grad_att_own,
        grad_ff_own,
        grad_gain_own,
    )


CHUNK = 4


def sort_rows(spans_ref, own_ref, other_ref, sorted_ref, span):
    for m, ref in enumerate((own_ref, other_ref)):
        for z in range(4):
            for j in range(2):
                start = pl.multiple_of(spans_ref[m, z, j] * span, span)
                sorted_ref[pl.ds(start, span), :] = ref[z, j * span : (j + 1) * span, :]


def group_rows(ref, part, span, head):
    group = HEADS // KV_HEADS
    rows = ref[part * span : (part + 1) * span, :]
    columns = [
        rows[:, (head * group + j) * HEAD_DIM : (head * group + j + 1) * HEAD_DIM]
        for j in range(group)
    ]
    return jnp.concatenate(columns, 0)


def seen(position, step, span, rows, cols):
    row = lax.broadcasted_iota(jnp.int32, (rows, cols), 0) % span
    col = lax.broadcasted_iota(jnp.int32, (rows, cols), 1)
    return col + step * cols <= row + position * span


def attend_kernel(
    spans_ref, q_ref, own_ref, other_ref, out_ref, lse_ref, sorted_ref, q_scr, top_ref, sum_ref, acc_ref
):
    group = HEADS // KV_HEADS
    span = q_ref.shape[0] // 2
    width_kv = KV_HEADS * HEAD_DIM
    rows, cols = group * span, CHUNK * span
    sort_rows(spans_ref, own_ref, other_ref, sorted_ref, span)
    for part in range(2):
        position = spans_ref[0, 4, part]
        for g in range(KV_HEADS):
            q_scr[g] = group_rows(q_ref, part, span, g) * jnp.bfloat16(HEAD_DIM**-0.5)
        top_ref[...] = jnp.full(top_ref.shape, NEG, jnp.float32)
        sum_ref[...] = jnp.zeros(sum_ref.shape, jnp.float32)
        acc_ref[...] = jnp.zeros(acc_ref.shape, jnp.float32)

        def step(i, unused):
            visible = seen(position, i, span, rows, cols)
            base = pl.multiple_of(i * cols, cols)
            for g in range(KV_HEADS):
                k = sorted_ref[pl.ds(base, cols), g * HEAD_DIM : (g + 1) * HEAD_DIM]
                v = sorted_ref[
                    pl.ds(base, cols), width_kv + g * HEAD_DIM : width_kv + (g + 1) * HEAD_DIM
                ]
                s = lax.dot_general(
                    q_scr[g], k, (((1,), (1,)), ((), ())), preferred_element_type=jnp.float32
                )
                s = jnp.where(visible, s, NEG)
                old = top_ref[g]
                top = jnp.maximum(old, jnp.max(s, 1, keepdims=True))
                weights = jnp.where(visible, jnp.exp(s - top), 0.0)
                factor = jnp.exp(old - top)
                top_ref[g] = top
                sum_ref[g] = sum_ref[g] * factor + jnp.sum(weights, 1, keepdims=True)
                acc_ref[g] = acc_ref[g] * factor + jnp.dot(
                    weights.astype(jnp.bfloat16), v, preferred_element_type=jnp.float32
                )
            return 0

        lax.fori_loop(0, (position + CHUNK) // CHUNK, step, 0)
        for g in range(KV_HEADS):
            out = acc_ref[g] / sum_ref[g]
            lse_ref[part * KV_HEADS + g] = top_ref[g] + jnp.log(sum_ref[g])
            for j in range(group):
                h = g * group + j
                out_ref[part * span : (part + 1) * span, h * HEAD_DIM : (h + 1) * HEAD_DIM] = out[
                    j * span : (j + 1) * span
                ]


def attend(spans, queries, own, other):
    rows, width = queries.shape
    group = HEADS // KV_HEADS
    stacked = group * rows // 2
    vmem = pl.BlockSpec(memory_space=pltpu.VMEM)
    return pl.pallas_call(
        attend_kernel,
        out_shape=(
            jax.ShapeDtypeStruct((rows, width), jnp.float32),
            jax.ShapeDtypeStruct((2 * KV_HEADS, stacked, 1), jnp.float32),
        ),
        in_specs=[pl.BlockSpec(memory_space=pltpu.SMEM), vmem, vmem, vmem],
        out_specs=(vmem, vmem),
        scratch_shapes=[
            pltpu.VMEM((8 * rows, own.shape[2]), jnp.bfloat16),
            pltpu.VMEM((KV_HEADS, stacked, HEAD_DIM), jnp.bfloat16),
            pltpu.VMEM((KV_HEADS, stacked, 1), jnp.float32),
            pltpu.VMEM((KV_HEADS, stacked, 1), jnp.float32),
            pltpu.VMEM((KV_HEADS, stacked, HEAD_DIM), jnp.float32),
        ],
        compiler_params=pltpu.CompilerParams(vmem_limit_bytes=24 * 2**20),
        cost_estimate=pl.CostEstimate(flops=10**6, bytes_accessed=10**5, transcendentals=0),
        name="attend",
    )(spans, queries, own, other)


def attend_back_kernel(
    spans_ref, q_ref, own_ref, other_ref, out_ref, lse_ref, grad_ref,
    dq_ref, own_grad_ref, other_grad_ref,
    sorted_ref, q_scr, grad_scr, delta_ref, dq_scr, dk_scr, dv_scr,
):
    group = HEADS // KV_HEADS
    span = q_ref.shape[0] // 2
    width_kv = KV_HEADS * HEAD_DIM
    rows, cols = group * span, CHUNK * span
    sort_rows(spans_ref, own_ref, other_ref, sorted_ref, span)
    dk_scr[...] = jnp.zeros(dk_scr.shape, jnp.float32)
    dv_scr[...] = jnp.zeros(dv_scr.shape, jnp.float32)
    for part in range(2):
        position = spans_ref[0, 4, part]
        for g in range(KV_HEADS):
            q_scr[g] = group_rows(q_ref, part, span, g) * jnp.bfloat16(HEAD_DIM**-0.5)
            grad = group_rows(grad_ref, part, span, g)
            grad_scr[g] = grad
            delta_ref[g] = jnp.sum(
                grad.astype(jnp.float32) * group_rows(out_ref, part, span, g), 1, keepdims=True
            )
        dq_scr[...] = jnp.zeros(dq_scr.shape, jnp.float32)

        def step(i, unused):
            visible = seen(position, i, span, rows, cols)
            base = pl.multiple_of(i * cols, cols)
            for g in range(KV_HEADS):
                k = sorted_ref[pl.ds(base, cols), g * HEAD_DIM : (g + 1) * HEAD_DIM]
                v = sorted_ref[
                    pl.ds(base, cols), width_kv + g * HEAD_DIM : width_kv + (g + 1) * HEAD_DIM
                ]
                q, grad = q_scr[g], grad_scr[g]
                s = lax.dot_general(
                    q, k, (((1,), (1,)), ((), ())), preferred_element_type=jnp.float32
                )
                probs = jnp.where(visible, jnp.exp(s - lse_ref[part * KV_HEADS + g]), 0.0)
                grad_probs = lax.dot_general(
                    grad, v, (((1,), (1,)), ((), ())), preferred_element_type=jnp.float32
                )
                grad_s = (probs * (grad_probs - delta_ref[g])).astype(jnp.bfloat16)
                dq_scr[g] += jnp.dot(grad_s, k, preferred_element_type=jnp.float32)
                dk_scr[g, pl.ds(base, cols), :] += lax.dot_general(
                    grad_s, q, (((0,), (0,)), ((), ())), preferred_element_type=jnp.float32
                )
                dv_scr[g, pl.ds(base, cols), :] += lax.dot_general(
                    probs.astype(jnp.bfloat16), grad, (((0,), (0,)), ((), ())),
                    preferred_element_type=jnp.float32,
                )
            return 0

        lax.fori_loop(0, (position + CHUNK) // CHUNK, step, 0)
        for g in range(KV_HEADS):
            dq = dq_scr[g] * HEAD_DIM**-0.5
            for j in range(group):
                h = g * group + j
                dq_ref[part * span : (part + 1) * span, h * HEAD_DIM : (h + 1) * HEAD_DIM] = dq[
                    j * span : (j + 1) * span
                ]
    for m, ref in enumerate((own_grad_ref, other_grad_ref)):
        for z in range(4):
            for j in range(2):
                start = pl.multiple_of(spans_ref[m, z, j] * span, span)
                parts = [scr[g, pl.ds(start, span), :] for scr in (dk_scr, dv_scr) for g in range(KV_HEADS)]
                ref[z, j * span : (j + 1) * span, :] = jnp.concatenate(parts, 1).astype(jnp.bfloat16)


def attend_back(spans, queries, own, other, out, lse, grad):
    rows, width = queries.shape
    group = HEADS // KV_HEADS
    stacked = group * rows // 2
    wide = own.shape[2]
    vmem = pl.BlockSpec(memory_space=pltpu.VMEM)
    return pl.pallas_call(
        attend_back_kernel,
        out_shape=(
            jax.ShapeDtypeStruct((rows, width), jnp.float32),
            jax.ShapeDtypeStruct((4, rows, wide), jnp.bfloat16),
            jax.ShapeDtypeStruct((4, rows, wide), jnp.bfloat16),
        ),
        in_specs=[pl.BlockSpec(memory_space=pltpu.SMEM)] + [vmem] * 6,
        out_specs=(vmem, vmem, vmem),
        scratch_shapes=[
            pltpu.VMEM((8 * rows, wide), jnp.bfloat16),
            pltpu.VMEM((KV_HEADS, stacked, HEAD_DIM), jnp.bfloat16),
            pltpu.VMEM((KV_HEADS, stacked, HEAD_DIM), jnp.bfloat16),
            pltpu.VMEM((KV_HEADS, stacked, 1), jnp.float32),
            pltpu.VMEM((KV_HEADS, stacked, HEAD_DIM), jnp.float32),
            pltpu.VMEM((KV_HEADS, 8 * rows, HEAD_DIM), jnp.float32),
            pltpu.VMEM((KV_HEADS, 8 * rows, HEAD_DIM), jnp.float32),
        ],
        compiler_params=pltpu.CompilerParams(vmem_limit_bytes=32 * 2**20),
        cost_estimate=pl.CostEstimate(flops=10**6, bytes_accessed=10**5, transcendentals=0),
        name="attend_back",
    )(spans, queries, own, other, out, lse, grad)


TILE = 16
GU_TILES = 10
DOWN_TILES = 4
STEP = 256


def contract_last(a, w):
    return lax.dot_general(a, w, (((1,), (1,)), ((), ())), preferred_element_type=jnp.float32)


def contract_first(a, w):
    return lax.dot_general(a, w, (((0,), (0,)), ((), ())), preferred_element_type=jnp.float32)


def ff_kernel(gate_rt, up_rt, place_ref, mid_ref, gain_ref, grad_ref, target_ref, spread_ref, *refs):
    pieces, refs = refs[:10], refs[10:]
    out_ref, spread_out, act_ref, dgate_ref, dup_ref, dmid_ref, branch_ref, dgain_ref = refs[:8]
    w_scr, total_scr, back_scr, gwide_scr, sems = refs[8:]
    core = place_ref[0, 0]
    rows, width = mid_ref.shape
    half_out = DOWN_TILES * 128
    gu_rt = target_ref.shape[1] // TILE
    part = w_scr.shape[1] // 8
    copies = []
    for k in range(2):
        half = core if k == 0 else 1 - core
        spots = [(1, 0, 2), (2, 0, 2), (3, 0, 2), (4, 0, 1), (4, 1, 1)]
        for i, (n, j, parts) in enumerate(spots):
            start = (place_ref[0, n] * 2 + j) * part
            source = pieces[5 * k + i]
            target = w_scr.at[half, pl.ds(start, parts * part)]
            copies.append(pltpu.make_async_copy(source, target, sems.at[5 * k + i]))
    for copy in copies:
        copy.start()
    mid = mid_ref[...]
    scale = lax.rsqrt(jnp.mean(mid * mid, -1, keepdims=True) + EPS)
    hidden = (mid * scale * gain_ref[...]).astype(jnp.bfloat16)
    grad = grad_ref[...]
    gwide_scr[...] = jnp.zeros(gwide_scr.shape, gwide_scr.dtype)
    gwide_scr[:, :width] = grad
    total_scr[...] = jnp.zeros(total_scr.shape, jnp.float32)
    back_scr[...] = jnp.zeros(back_scr.shape, jnp.float32)
    spread_out[...] = jnp.dot(hidden, spread_ref[...], preferred_element_type=jnp.float32).astype(
        jnp.bfloat16
    )
    for copy in copies:
        copy.wait()
    kind = target_ref[...]
    gate_cols, up_first = gate_rt * TILE, up_rt * TILE
    for_gate = jnp.where(kind[:, :gate_cols] == 1, spread_out[:, :gate_cols].astype(jnp.float32), 0.0)
    for_gate = for_gate.astype(jnp.bfloat16)
    for_up = jnp.where(kind[:, up_first:] == 2, spread_out[:, up_first:].astype(jnp.float32), 0.0)
    for_up = for_up.astype(jnp.bfloat16)

    def gu_block(half, column, first, last):
        parts = [
            jnp.concatenate(
                [w_scr[half, r * GU_TILES + column + j] for r in range(first, last)], 0
            )
            for j in range(STEP // 128)
        ]
        return jnp.concatenate(parts, 1)

    def down_block(k, n):
        base = gu_rt * GU_TILES + n * (STEP // TILE * DOWN_TILES)
        parts = [
            jnp.concatenate([w_scr[k, base + r * DOWN_TILES + j] for r in range(STEP // TILE)], 0)
            for j in range(DOWN_TILES)
        ]
        return jnp.concatenate(parts, 1)

    def step(n, unused):
        half = n // (GU_TILES * 128 // STEP)
        column = n % (GU_TILES * 128 // STEP) * (STEP // 128)
        here = pl.ds(pl.multiple_of(n * STEP, STEP), STEP)
        w_gate = gu_block(half, column, 0, gate_rt)
        w_up = gu_block(half, column, up_rt, gu_rt)
        gate = jnp.dot(for_gate, w_gate, preferred_element_type=jnp.float32)
        up = jnp.dot(for_up, w_up, preferred_element_type=jnp.float32)
        sig = 1.0 / (1.0 + jnp.exp(-gate))
        silu = gate * sig
        slope = up * (sig + silu * (1.0 - sig))
        act = (silu * up).astype(jnp.bfloat16)
        act_ref[:, here] = act
        d_act = jnp.zeros((rows, STEP), jnp.float32)
        for k in range(2):
            w_down = down_block(k, n)
            cols = slice(k * half_out, (k + 1) * half_out)
            total_scr[:, cols] += jnp.dot(act, w_down, preferred_element_type=jnp.float32)
            d_act = d_act + contract_last(gwide_scr[:, cols], w_down)
        d_gate = (d_act * slope).astype(jnp.bfloat16)
        d_up = (d_act * silu).astype(jnp.bfloat16)
        dgate_ref[:, here] = d_gate
        dup_ref[:, here] = d_up
        back_gate = contract_last(d_gate, w_gate)
        back_up = contract_last(d_up, w_up)
        back_scr[:, :gate_cols] += jnp.where(kind[:, :gate_cols] == 1, back_gate, 0.0)
        back_scr[:, up_first:] += jnp.where(kind[:, up_first:] == 2, back_up, 0.0)
        return 0

    lax.fori_loop(0, 2 * GU_TILES * 128 // STEP, step, 0)
    out_ref[...] = (mid + total_scr[:, :width]).astype(jnp.bfloat16)
    back = back_scr[...]
    high = back.astype(jnp.bfloat16)
    low = (back - high.astype(jnp.float32)).astype(jnp.bfloat16)
    d_hidden = contract_last(high, spread_ref[...]) + contract_last(low, spread_ref[...])
    normed = mid * scale
    dgain_ref[...] = jnp.sum(d_hidden * normed, 0, keepdims=True)
    e = d_hidden * gain_ref[...]
    d_mid = grad.astype(jnp.float32) + scale * (e - normed * jnp.mean(e * normed, -1, keepdims=True))
    dmid_ref[...] = d_mid
    branch_ref[...] = d_mid.astype(jnp.bfloat16)


def feed_forward(core, middle, gain, grad, kind, spread, mine, other, gu_rt, gate_rt, up_rt):
    rows, width = middle.shape
    count = gu_rt * GU_TILES + FF // TILE * DOWN_TILES
    pieces = [a.reshape(-1, TILE, 128) for a in (*mine, *other)]
    padded = gu_rt * TILE
    vmem = pl.BlockSpec(memory_space=pltpu.VMEM)
    hbm = pl.BlockSpec(memory_space=pl.ANY)
    bf, f32 = jnp.bfloat16, jnp.float32
    shape = jax.ShapeDtypeStruct
    return pl.pallas_call(
        functools.partial(ff_kernel, gate_rt, up_rt),
        out_shape=(
            shape((rows, width), bf),
            shape((rows, padded), bf),
            shape((rows, FF), bf),
            shape((rows, FF), bf),
            shape((rows, FF), bf),
            shape((rows, width), f32),
            shape((rows, width), bf),
            shape((1, width), f32),
        ),
        in_specs=[pl.BlockSpec(memory_space=pltpu.SMEM)] + [vmem] * 5 + [hbm] * 10,
        out_specs=[vmem] * 8,
        scratch_shapes=[
            pltpu.VMEM((2, count, TILE, 128), bf),
            pltpu.VMEM((rows, 2 * DOWN_TILES * 128), f32),
            pltpu.VMEM((rows, padded), f32),
            pltpu.VMEM((rows, 2 * DOWN_TILES * 128), bf),
            pltpu.SemaphoreType.DMA((10,)),
        ],
        compiler_params=pltpu.CompilerParams(vmem_limit_bytes=40 * 2**20),
        cost_estimate=pl.CostEstimate(flops=10**6, bytes_accessed=10**5, transcendentals=0),
        name="feed_forward",
    )(
        core, middle, gain, grad, kind, spread, *pieces,
    )


def ff_terms_kernel(
    gate_rt, up_rt, half_ref, kind_ref, spread_ref, act_ref, dgate_ref, dup_ref, gwide_ref, out_ref
):
    half = half_ref[0, 0]
    gu_cols = GU_TILES * 128
    gu_here = pl.ds(pl.multiple_of(half * gu_cols, gu_cols), gu_cols)
    padded = spread_ref.shape[1]
    block = 256
    gu_total = padded // TILE * GU_TILES

    def put(terms, base):
        tiles_wide = terms.shape[1] // 128
        for r in range(terms.shape[0] // TILE):
            for ct in range(tiles_wide):
                tile = terms[r * TILE : (r + 1) * TILE, ct * 128 : (ct + 1) * 128]
                at = base + r * tiles_wide + ct
                out_ref[at] = tile.astype(jnp.bfloat16)

    def part(j, number, d_ref):
        here = pl.ds(pl.multiple_of(j * block, block), block)
        rows_in = jnp.where(kind_ref[:, here] == number, spread_ref[:, here].astype(jnp.float32), 0.0)
        return contract_first(rows_in.astype(jnp.bfloat16), d_ref[:, gu_here])

    def base_of(j):
        return j * (block // TILE * GU_TILES)

    mixed = (gate_rt * TILE - 1) // block

    def gate_step(j, unused):
        put(part(j, 1, dgate_ref), base_of(j))
        return 0

    def up_step(j, unused):
        put(part(j, 2, dup_ref), base_of(j))
        return 0

    lax.fori_loop(0, up_rt * TILE // block, gate_step, 0)
    for j in range(up_rt * TILE // block, mixed + 1):
        put(part(j, 1, dgate_ref) + part(j, 2, dup_ref), base_of(j))
    lax.fori_loop(mixed + 1, padded // block, up_step, 0)
    down_cols = DOWN_TILES * 128
    down_here = pl.ds(pl.multiple_of(half * down_cols, down_cols), down_cols)

    def down_step(j, unused):
        here = pl.ds(pl.multiple_of(j * STEP, STEP), STEP)
        terms = contract_first(act_ref[:, here], gwide_ref[:, down_here])
        put(terms, gu_total + j * (STEP // TILE * DOWN_TILES))
        return 0

    lax.fori_loop(0, FF // STEP, down_step, 0)


def ff_terms(half, kind, spread, act, d_gate, d_up, grad_wide, gate_rt, up_rt):
    vmem = pl.BlockSpec(memory_space=pltpu.VMEM)
    count = spread.shape[1] // TILE * GU_TILES + FF // TILE * DOWN_TILES
    operands = [kind, spread, act, d_gate, d_up, grad_wide]
    return pl.pallas_call(
        functools.partial(ff_terms_kernel, gate_rt, up_rt),
        out_shape=jax.ShapeDtypeStruct((count, TILE, 128), jnp.bfloat16),
        in_specs=[pl.BlockSpec(memory_space=pltpu.SMEM)] + [vmem] * len(operands),
        out_specs=vmem,
        compiler_params=pltpu.CompilerParams(vmem_limit_bytes=32 * 2**20),
        cost_estimate=pl.CostEstimate(flops=10**6, bytes_accessed=10**5, transcendentals=0),
        name="ff_terms",
    )(half, *operands)


def flat_wide(in_ref, out_ref, rows):
    for half in range(2):
        for rt in range(-(-rows // TILE)):
            count = min(TILE, rows - rt * TILE)
            for ct in range(GU_TILES):
                start = (rt * GU_TILES + ct) * TILE
                to = rt * TILE * 2 * GU_TILES + half * GU_TILES + ct
                out_ref[pl.ds(to, count, stride=2 * GU_TILES), :] = in_ref[
                    half, start : start + count, :
                ]


def flat_narrow(in_ref, out_ref, rows, in_start, out_start, tile):
    pairs = tile // 2
    left = lax.broadcasted_iota(jnp.int32, (pairs, 128), 1) < 64
    for rt in range(rows // tile):
        even, odd = [], []
        for ct in range(2 * DOWN_TILES):
            half, column = divmod(ct, DOWN_TILES)
            start = in_start + (rt * DOWN_TILES + column) * tile
            even.append(in_ref[half, pl.ds(start, pairs, stride=2), :])
            odd.append(pltpu.roll(in_ref[half, pl.ds(start + 1, pairs, stride=2), :], 64, 1))
        lines = even[:7] + [jnp.where(left, even[7], odd[0])]
        lines += [jnp.where(left, odd[j - 1], odd[j]) for j in range(1, 8)]
        for i, line in enumerate(lines):
            out_ref[pl.ds(out_start + 15 * pairs * rt + i, pairs, stride=15), :] = line


def ff_flat_kernel(rest, variant_ref, in_ref, out_ref):
    variant = variant_ref[0, 0]
    total = out_ref.shape[0]

    @pl.when(variant == 0)
    def gate_or_up():
        flat_wide(in_ref, out_ref, total // (2 * GU_TILES))

    @pl.when(variant == 1)
    def mixed():
        flat_wide(in_ref, out_ref, rest)
        done = rest * 2 * GU_TILES
        first = -(-rest // TILE) * TILE * GU_TILES
        flat_narrow(in_ref, out_ref, (total - done) * 2 // 15, first, done, TILE)

    @pl.when(variant == 2)
    def down():
        flat_narrow(in_ref, out_ref, total * 2 // 15, 0, 0, TILE)


def att_flat_kernel(in_ref, out_ref):
    flat_narrow(in_ref, out_ref, out_ref.shape[0] * 2 // 15, 0, 0, 8)


def flat_call(kernel, size, *operands):
    vmem = pl.BlockSpec(memory_space=pltpu.VMEM)
    smem = [pl.BlockSpec(memory_space=pltpu.SMEM)] * (len(operands) - 1)
    out = pl.pallas_call(
        kernel,
        out_shape=jax.ShapeDtypeStruct((size // 128, 128), jnp.float32),
        in_specs=smem + [vmem],
        out_specs=vmem,
        compiler_params=pltpu.CompilerParams(vmem_limit_bytes=16 * 2**20),
        cost_estimate=pl.CostEstimate(flops=10**6, bytes_accessed=10**5, transcendentals=0),
        name="flatten",
    )(*operands)
    return out.reshape(size)


def input_grad_kernel(
    x_ref, gain_ref, mid_ref, q_own, q_other, k_own, k_other, v_own, v_other, w_own, w_other, perm_ref,
    out_ref, dgain_ref,
):
    rows, width = x_ref.shape
    third = width // 3
    x = x_ref[...].astype(jnp.float32)
    scale = lax.rsqrt(jnp.mean(x * x, -1, keepdims=True) + EPS)
    normed = x * scale
    cut_v = width + third

    def back(own, other, start, stop):
        return contract_last(own[...], w_own[start:stop, :]) + contract_last(
            other[...], w_other[start:stop, :]
        )

    three = back(k_own, k_other, width, cut_v) + back(v_own, v_other, cut_v, cut_v + third)
    three = jnp.concatenate([three[q * rows : (q + 1) * rows] for q in range(3)], 1)
    high = three.astype(jnp.bfloat16)
    low = (three - high.astype(jnp.float32)).astype(jnp.bfloat16)
    d_hidden = back(q_own, q_other, 0, width)
    d_hidden = d_hidden + contract_last(high, perm_ref[...]) + contract_last(low, perm_ref[...])
    dgain_ref[...] = jnp.sum(d_hidden * normed, 0, keepdims=True)
    e = d_hidden * gain_ref[...]
    out_ref[...] = mid_ref[...] + scale * (e - normed * jnp.mean(e * normed, -1, keepdims=True))


def input_grad(x, gain, d_mid, q_halves, k_halves, v_halves, weights, perm):
    rows, width = x.shape
    vmem = pl.BlockSpec(memory_space=pltpu.VMEM)
    return pl.pallas_call(
        input_grad_kernel,
        out_shape=(
            jax.ShapeDtypeStruct((rows, width), jnp.float32),
            jax.ShapeDtypeStruct((1, width), jnp.float32),
        ),
        in_specs=[vmem] * 12,
        out_specs=(vmem, vmem),
        compiler_params=pltpu.CompilerParams(vmem_limit_bytes=28 * 2**20),
        cost_estimate=pl.CostEstimate(flops=10**6, bytes_accessed=10**5, transcendentals=0),
        name="input_grad",
    )(x, gain, d_mid, *q_halves, *k_halves, *v_halves, *weights, perm)


BF = jnp.bfloat16
F32 = jnp.float32
LANES = 128
GU_PAD = 96
X_PAIRS = [(j, j ^ 1) for j in range(4)]
Y_PAIRS = [(j, j ^ 2) for j in range(4)]
CORE_PAIRS = [(j, j ^ 1) for j in range(8)]
LINES = [[0, 2, 4, 6], [1, 3, 5, 7]]
EXTRA = 2


def up_pairs(first, last):
    return [(2 * z + c, 2 * z + 2 + c) for z in range(first, last) for c in range(2)]


def down_pairs(first, last):
    return [(2 * z + 2 + c, 2 * z + c) for z in range(first, last) for c in range(2)]


def swap_x(a):
    return lax.ppermute(a, "batch", X_PAIRS)


def swap_y(a):
    return lax.ppermute(a, "batch", Y_PAIRS)


def swap_core(a):
    return lax.ppermute(a, "ctx", CORE_PAIRS)


def tiles(a):
    rows, cols = a.shape
    a = a.reshape(rows // 8, 8, cols // LANES, LANES)
    return a.transpose(0, 2, 1, 3).reshape(rows * cols // (8 * LANES), 8, LANES)


def untile(a, cols):
    rows = a.shape[0] * 8 * LANES // cols
    a = a.reshape(rows // 8, cols // LANES, 8, LANES)
    return a.transpose(0, 2, 1, 3).reshape(rows, cols)


def pad_to(a, rows, cols):
    return jnp.pad(a, ((0, rows - a.shape[0]), (0, cols - a.shape[1])))


def halves_of(a):
    half = a.shape[1] // 2
    return jnp.stack([tiles(a[:, :half]), tiles(a[:, half:])])


def deep_halves_of(a):
    rows, cols = a.shape
    a = a.reshape(rows // TILE, TILE, 2, cols // (2 * LANES), LANES)
    return a.transpose(2, 0, 3, 1, 4).reshape(2, rows * cols // (2 * LANES), LANES)


def gather_line(a, z, before_last=lambda parts: parts):
    u1 = lax.ppermute(a, "ctx", up_pairs(0, 3))
    d1 = lax.ppermute(a, "ctx", down_pairs(0, 3))
    u2 = lax.ppermute(u1, "ctx", up_pairs(1, 3))
    d2 = lax.ppermute(d1, "ctx", down_pairs(0, 2))
    u2, d2 = before_last((u2, d2))
    u3 = lax.ppermute(u2, "ctx", up_pairs(2, 3))
    d3 = lax.ppermute(d2, "ctx", down_pairs(0, 1))
    seven = jnp.stack([u3, u2, u1, a, d1, d2, d3])
    return lax.dynamic_slice_in_dim(seven, 3 - z, 4, 0)


def line_pairs(hops):
    return [(2 * z + c, 2 * (z + hops) + c) for z in range(4) for c in range(2) if 0 <= z + hops < 4]


def gather_direct(a, z):
    got = {k: lax.ppermute(a, "ctx", line_pairs(k)) for k in (1, -1, 2, -2, 3, -3)}
    seven = jnp.stack([got[3], got[2], got[1], a, got[-1], got[-2], got[-3]])
    return lax.dynamic_slice_in_dim(seven, 3 - z, 4, 0)


def send_line(t, z, hops):
    out = []
    for k in hops:
        block = lax.dynamic_index_in_dim(t, jnp.clip(z + k, 0, 3), 0, keepdims=False)
        out.append(lax.ppermute(block, "ctx", line_pairs(k)))
    return out


def sum_line(t, z, got):
    total = lax.dynamic_index_in_dim(t, z, 0, keepdims=False).astype(F32)
    for k, block in got:
        total = total + jnp.where((z - k >= 0) & (z - k < 4), block.astype(F32), 0.0)
    return total


def scatter_direct(t, z):
    hops = (3, -3, 2, -2, 1, -1)
    return sum_line(t, z, zip(hops, send_line(t, z, hops)))


def gather_near(a):
    return swap_x(a), swap_y(a)


def gather_far(from_x, from_y):
    return swap_y(from_x[:2]), swap_x(from_y[2:])


def place(pieces, b, start, stop):
    shape = pieces[0][2].shape
    whole = jnp.zeros((4, 4, shape[1], stop - start) + shape[3:], BF)
    for step, row, piece in pieces:
        whole = lax.dynamic_update_slice(
            whole, piece[None, :, :, start:stop], (b ^ step, row) + (0,) * (len(shape) - 1)
        )
    return whole


def add(*terms):
    total = terms[0].astype(F32)
    for term in terms[1:]:
        total = total + term.astype(F32)
    return total.astype(BF)


def scatter_blocks(arrays, b):
    return [
        [lax.dynamic_index_in_dim(a, b ^ k, 0, keepdims=False) for a in arrays] for k in range(4)
    ]


def scatter_far(terms):
    return add(*(t[:2] for t in terms)), add(*(t[2:] for t in terms))


def scatter_near(blocks, far_x, far_y):
    xs, ys = blocks[1], blocks[2]
    x_parts = add(*(t[:2] for t in xs)), add(*(t[2:] for t in xs), far_y)
    y_parts = add(*(t[:2] for t in ys), far_x), add(*(t[2:] for t in ys))
    return swap_x(jnp.concatenate(x_parts, 0)), swap_y(jnp.concatenate(y_parts, 0))


def split_high(a, parts):
    out = []
    for unused in range(parts):
        high = lax.reduce_precision(a, 8, 7)
        out.append(high.astype(BF))
        a = a - high
    return out


def local_block(tokens, attention_weights, feedforward_weights, norm_gains, span_order, cotangent):
    rows_here = tokens.shape[1]
    halves = rows_here // 2
    width_q = HEADS * HEAD_DIM
    width_kv = KV_HEADS * HEAD_DIM
    wide = 2 * 512
    b = lax.axis_index("batch")
    place_ctx = lax.axis_index("ctx")
    z = place_ctx // 2
    c = place_ctx % 2
    device = b * 8 + place_ctx
    own_gain = D // 8

    def pick(first, second):
        return jnp.where(c == 0, first, second)

    def merge(mine, other):
        return pick(
            jnp.concatenate([mine, other], -1), jnp.concatenate([other, mine], -1)
        )

    def half_of(a, k):
        half = a.shape[-1] // 2
        return jnp.where((c ^ k) == 0, a[..., :half], a[..., half:])

    def pair_up(shard):
        mine = pick(shard[0], shard[1])
        other = swap_core(pick(shard[1], shard[0]))
        return pick(jnp.stack([mine, other]), jnp.stack([other, mine]))

    att_rows = attention_weights.shape[0] // D
    att_shard = halves_of(pad_to(attention_weights.reshape(att_rows, D), att_rows, wide))
    gain_parts = jnp.stack(split_high(norm_gains, 3), 1)
    gain_rows = jnp.pad(gain_parts, ((0, 0), (0, 8 * EXTRA - 3), (0, LANES - own_gain)))
    gain_rows = gain_rows.reshape(2, EXTRA, 8, LANES)
    att_chip = pair_up(jnp.concatenate([att_shard, gain_rows], 1))
    att_line = gather_direct(att_chip, z)

    gu_rows = feedforward_weights.shape[0] // FF
    down_rows = feedforward_weights.shape[0] // D
    mixed = 2 * D // gu_rows
    rest = 2 * D - mixed * gu_rows
    rest_pad = -(-rest // TILE) * TILE
    gu_shard = deep_halves_of(pad_to(feedforward_weights.reshape(gu_rows, FF), GU_PAD, FF))
    down_shard = deep_halves_of(pad_to(feedforward_weights.reshape(down_rows, D), down_rows, wide))
    mixed_down = pad_to(
        feedforward_weights[rest * FF :].reshape(-1, D), down_rows - rest * FF // D, wide
    )
    mixed_shard = jnp.concatenate(
        [
            deep_halves_of(
                pad_to(feedforward_weights[: rest * FF].reshape(rest, FF), rest_pad, FF)
            ),
            deep_halves_of(mixed_down),
        ],
        1,
    )
    ff_shard = jnp.where(device < mixed, gu_shard, jnp.where(device == mixed, mixed_shard, down_shard))
    ff_body = ff_shard.shape[1]
    ff_line = lax.all_gather(pair_up(ff_shard), "ctx", axis_index_groups=LINES)
    ff_line_other = swap_core(ff_line)

    att_x, att_y = gather_near(att_line)
    gu_total = mixed * GU_PAD + rest_pad
    pad_row = jnp.arange(gu_total, dtype=jnp.int32)
    true_row = pad_row // GU_PAD * gu_rows + pad_row % GU_PAD
    real = pad_row % GU_PAD < gu_rows
    is_gate = real & (true_row < D)
    is_up = real & (true_row >= D)
    spread = ((true_row % D)[None, :] == jnp.arange(D, dtype=jnp.int32)[:, None]) & real[None, :]
    spread = spread.astype(BF)
    third = D // 3
    order3 = jnp.arange(D, dtype=jnp.int32)
    perm3 = (order3[:, None] == (order3 % third * 3 + order3 // third)[None, :]).astype(BF)

    att_first, att_second = gather_far(att_x, att_y)
    att_pieces = (
        (0, 0, att_line), (1, 0, att_x), (2, 0, att_y), (3, 0, att_first), (3, 2, att_second)
    )
    att_body = att_rows * wide // (2 * 8 * LANES)
    att_mine = place(att_pieces, b, 0, att_body).reshape(-1, 8, LANES)
    gain_mine = place(att_pieces, b, att_body, att_body + EXTRA)
    att_other = swap_core(att_mine)
    gain_other = swap_core(gain_mine)

    def gain_from(a):
        parts = a[0, :, :, 0, :3, :own_gain].astype(F32)
        return (parts[:, :, 0] + parts[:, :, 1] + parts[:, :, 2]).reshape(D)

    gain_m, gain_o = gain_from(gain_mine), gain_from(gain_other)
    gain_full = jnp.stack([pick(gain_m, gain_o), pick(gain_o, gain_m)])


    offsets = jnp.arange(halves, dtype=jnp.int32)
    query_pos = (span_order[0][:, None] * halves + offsets[None, :]).reshape(rows_here)
    cos_table, sin_table = rope_tables(query_pos)

    inputs = tokens[0].astype(F32)
    hidden = normalize(inputs, gain_full[0]).astype(BF)
    hidden3 = jnp.dot(hidden, perm3, preferred_element_type=F32).astype(BF)
    hidden3 = hidden3.reshape(rows_here, 3, third)
    att_m, att_o = untile(att_mine, wide // 2), untile(att_other, wide // 2)
    cut_k, cut_v, cut_o = D, D + third, D + 2 * third

    def project(a, start, stop):
        return merge(
            jnp.dot(a, att_m[start:stop], preferred_element_type=F32),
            jnp.dot(a, att_o[start:stop], preferred_element_type=F32),
        )

    def thirds(start, stop):
        out = project(hidden3.transpose(1, 0, 2).reshape(3 * rows_here, third), start, stop)
        out = out.reshape(3, rows_here, wide)
        return out[0, :, :third] + out[1, :, third : 2 * third] + out[2, :, 2 * third : 3 * third]

    query_raw = project(hidden, 0, D)[:, :width_q].reshape(rows_here, HEADS, HEAD_DIM)
    key_raw = thirds(cut_k, cut_v).reshape(rows_here, KV_HEADS, HEAD_DIM)
    values = thirds(cut_v, cut_o).astype(BF)
    query_rot, query_pull = jax.vjp(lambda a: rotate(a, cos_table, sin_table), query_raw)
    key_rot, key_pull = jax.vjp(lambda a: rotate(a, cos_table, sin_table), key_raw)
    queries = query_rot.astype(BF).reshape(rows_here, width_q)
    keys = key_rot.astype(BF).reshape(rows_here, width_kv)

    span_rows = jnp.pad(span_order.astype(BF), ((0, 15), (0, 2 * width_kv - 2)))
    key_value = jnp.concatenate([jnp.concatenate([keys, values], 1), span_rows], 0)
    ff_near = gather_near(ff_line)
    line_mine = gather_line(key_value, z)
    ff_near, line_mine, queries, spread = lax.optimization_barrier(
        (ff_near, line_mine, queries, spread)
    )
    line_other = swap_core(line_mine)
    ff_far = gather_far(*ff_near)
    spans = jnp.stack([line_mine[:, rows_here, :2], line_other[:, rows_here, :2]]).astype(jnp.int32)
    spans = jnp.concatenate([spans, jnp.broadcast_to(span_order[None], (2, 1, 2))], 1)
    attended, log_total = attend(spans, queries, line_mine, line_other)
    ff_far, attended = lax.optimization_barrier((ff_far, attended))
    ff_mine = (ff_line, *ff_near, *ff_far)
    ff_other = (ff_line_other, *(swap_core(piece) for piece in ff_mine[1:]))
    attended_low = attended.astype(BF)
    middle = inputs + project(attended_low, cut_o, cut_o + D)[:, :D]
    gate_end = -(-D // gu_rows) * GU_PAD
    up_start = D // gu_rows * GU_PAD
    grad_wide = jnp.pad(cotangent[0], ((0, 0), (0, wide - D)))
    kind = (is_gate.astype(jnp.int32) + 2 * is_up.astype(jnp.int32))[None]
    result, spread_two, activ, grad_gate, grad_upward, grad_middle, grad_branch, grad_gain_two = (
        feed_forward(
            jnp.stack([c, b, b ^ 1, b ^ 2, b ^ 3])[None], middle, gain_full[1:2], cotangent[0], kind, spread,
            ff_mine, ff_other,
            gu_total // TILE, gate_end // TILE, up_start // TILE,
        )
    )
    grad_gain_two = grad_gain_two[0]

    def times_transposed(a, w):
        return lax.dot_general(a, w, (((1,), (1,)), ((), ())), preferred_element_type=F32)

    def transposed_times(a, w):
        return lax.dot_general(a, w, (((0,), (0,)), ((), ())), preferred_element_type=F32)

    def terms_of_half(half, rows_in):
        return ff_terms(
            half.reshape(1, 1), kind, rows_in, activ, grad_gate, grad_upward, grad_wide,
            gate_end // TILE, up_start // TILE,
        )

    ff_send, spread_two, grad_branch = lax.optimization_barrier(
        (terms_of_half(1 - c, spread_two), spread_two, grad_branch)
    )
    ff_from = swap_core(ff_send)
    ff_keep = terms_of_half(c, spread_two)
    ff_blocks = scatter_blocks(
        [a.reshape(4, 4, 2, ff_body, LANES) for a in (ff_keep, ff_from)], b
    )
    branch_wide = jnp.pad(grad_branch, ((0, 0), (0, wide - D)))

    def project_back(a, start, stop):
        return times_transposed(half_of(a, 0), att_m[start:stop]) + times_transposed(
            half_of(a, 1), att_o[start:stop]
        )

    grad_attended = project_back(branch_wide, cut_o, cut_o + D).astype(BF)
    ff_far, grad_attended = lax.optimization_barrier((scatter_far(ff_blocks[3]), grad_attended))
    ff_far = swap_x(ff_far[0]), swap_y(ff_far[1])
    grad_query_rot, both_mine, both_other = attend_back(
        spans, queries, line_mine, line_other, attended, log_total, grad_attended
    )
    ff_far, both_other = lax.optimization_barrier((ff_far, both_other))
    both_from = swap_core(both_other)
    ff_near = scatter_near(ff_blocks, *ff_far)
    both_own = scatter_direct(add(both_mine, both_from), z)
    ff_line_sum, both_own = lax.optimization_barrier((add(*ff_blocks[0], *ff_near), both_own))
    ff_own = lax.psum_scatter(
        ff_line_sum, "ctx", scatter_dimension=0, axis_index_groups=LINES, tiled=True
    )[0].astype(F32)
    grad_key_rot, grad_value_f = both_own[:, :width_kv], both_own[:, width_kv:]
    grad_query_raw = query_pull(grad_query_rot.reshape(rows_here, HEADS, HEAD_DIM))[0]
    grad_key_raw = key_pull(grad_key_rot.reshape(rows_here, KV_HEADS, HEAD_DIM))[0]
    grad_query = grad_query_raw.reshape(rows_here, width_q).astype(BF)
    grad_key = grad_key_raw.reshape(rows_here, width_kv).astype(BF)
    grad_value = grad_value_f.astype(BF)

    def spots(a):
        return jnp.concatenate(
            [jnp.pad(a, ((0, 0), (q * third, wide - (q + 1) * third))) for q in range(3)], 0
        )

    query_wide = jnp.pad(grad_query, ((0, 0), (0, wide - D)))
    key_spots, value_spots = spots(grad_key), spots(grad_value)
    hidden_rows = hidden3.transpose(1, 0, 2).reshape(3 * rows_here, third)
    def att_terms(k):
        terms = jnp.concatenate(
            [
                transposed_times(hidden, half_of(query_wide, k)).astype(BF),
                transposed_times(hidden_rows, half_of(key_spots, k)).astype(BF),
                transposed_times(hidden_rows, half_of(value_spots, k)).astype(BF),
                transposed_times(attended_low, half_of(branch_wide, k)).astype(BF),
            ],
            0,
        )
        return tiles(terms).reshape(4, 4, 2, att_body, 8, LANES)

    grad_inputs, grad_gain_one = input_grad(
        tokens[0], gain_full[:1], grad_middle,
        *([half_of(a, k) for k in range(2)] for a in (query_wide, key_spots, value_spots)),
        (att_m, att_o), perm3,
    )
    att_from = swap_core(att_terms(1))
    att_from, grad_inputs, grad_gain_one = lax.optimization_barrier(
        (att_from, grad_inputs, grad_gain_one)
    )
    att_blocks = scatter_blocks((att_terms(0), att_from), b)
    att_far = scatter_far(att_blocks[3])
    att_far = swap_x(att_far[0]), swap_y(att_far[1])
    gain_terms = jnp.stack([grad_gain_one[0], grad_gain_two])
    gain_terms = gain_terms + swap_core(gain_terms)
    gain_terms = gain_terms + swap_x(gain_terms)
    gain_terms = gain_terms + swap_y(gain_terms)
    att_far, gain_terms = lax.optimization_barrier((att_far, gain_terms))
    att_near = scatter_near(att_blocks, *att_far)
    gain_terms = pick(gain_terms[0], gain_terms[1]).reshape(8, own_gain)
    gain_terms = jnp.pad(
        jnp.stack(split_high(gain_terms, 2), 1),
        ((0, 0), (0, 8 * EXTRA - 2), (0, LANES - own_gain)),
    ).reshape(4, 2, EXTRA, 8, LANES)

    def settle(own):
        mine = pick(own[0], own[1])
        other = swap_core(pick(own[1], own[0]))
        return pick(jnp.stack([mine, other]), jnp.stack([other, mine]))

    ff_done = settle(ff_own)
    variant = jnp.where(device < mixed, 0, jnp.where(device == mixed, 1, 2)).astype(jnp.int32)
    ff_flat = flat_call(
        functools.partial(ff_flat_kernel, rest), feedforward_weights.shape[0],
        variant.reshape(1, 1), ff_done,
    )
    ff_flat, att_near = lax.optimization_barrier((ff_flat, att_near))
    att_sum = jnp.concatenate([add(*att_blocks[0], *att_near), gain_terms], 2)
    att_own = scatter_direct(att_sum, z)
    att_done = settle(att_own)
    gain_own = att_done[:, att_body, 0, :own_gain] + att_done[:, att_body, 1, :own_gain]
    att_flat = flat_call(
        att_flat_kernel, attention_weights.shape[0], att_done.reshape(2, -1, LANES)
    )
    return (
        result[None],
        grad_inputs[None],
        att_flat,
        ff_flat,
        gain_own,
    )


def solution(mesh):
    fits = mesh.shape["batch"] == 4 and mesh.shape["ctx"] == 8
    local = local_block if fits else local_any
    placed = (
        P("batch", "ctx", None),
        P(("batch", "ctx")),
        P(("batch", "ctx")),
        P(None, "ctx"),
        P("batch", "ctx"),
        P("batch", "ctx", None),
    )
    return jax.shard_map(
        local,
        mesh=mesh,
        in_specs=placed,
        out_specs=(
            P("batch", "ctx", None),
            P("batch", "ctx", None),
            P(("batch", "ctx")),
            P(("batch", "ctx")),
            P(None, "ctx"),
        ),
        check_vma=False,
    )
```
